32 devices in a mesh: frow: 2 (over x), fcol: 2 (over core), chan: 8 (over z, y).
Axes of the slice: x: 2, y: 2, z: 4, core: 2. Of those that a mesh axis runs over, the one named last changes fastest.
Arguments:
- dirty_image: float32 [32, 64, 512], P('chan', 'frow', 'fcol'), may hold values from -12 to 12
- density: float32 [32, 64, 512], P('chan', 'frow', 'fcol'), may hold values from 0.25 to 4
Outputs:
- image_estimate: float32 [32, 64, 512], P('chan', 'frow', 'fcol')
The draws below stay inside these ranges and needn't reach their ends.
All inputs are finite; a program needn't handle non-finite values.
Results may differ from the reference program's by a relative error of at most 0.0003.
Values sent between devices are 32-bit elements; how exact they have to be, the bound alone decides.
No kernel may reach another device: no remote copies, remote signals or barrier semaphores. Data moves between devices by JAX's collectives and lax.ppermute only.
A program may use at most 64 MiB of HBM per device.

```python
import math
import jax
import jax.numpy as jnp
import numpy as np
from jax import lax

TILE_ROWS = 32
TILE_COLS = 256
NDB = 4
LEVELS = 1
ITERS = 1
CHANNELS = 32
GROUP = 8
NROWS = 64
NCOLS = 512
N_FROW = 2
N_FCOL = 2


def draw_dirty_image(key, part):
    key = jax.random.fold_in(key, 11)
    first_key, latter_seed = jax.random.split(key, 2)
    full_shape = (CHANNELS, NROWS, NCOLS)
    position = jnp.arange(CHANNELS, dtype=jnp.float32) / max(CHANNELS - 1, 1)
    common = jax.random.normal(first_key, (1, NROWS, NCOLS), jnp.float32)
    noise = 0.8 * jax.random.normal(latter_seed, full_shape, jnp.float32)
    tilt = 1.0 + 2.0 * position
    return jnp.clip(tilt[:, None, None] * (common + noise), -12.0, 12.0)


def levels(own_key, shape, cuts, low, top_value):
    level, own = 1.0, jax.random.fold_in(own_key, 6)
    for dim, parts in cuts:
        heights = jnp.exp(jax.random.uniform(jax.random.fold_in(own, dim), (parts,), jnp.float32, low / len(cuts), top_value / len(cuts)))
        level = level * jnp.repeat(heights, shape[dim] // parts).reshape([-1 if axis == dim else 1 for axis in range(len(shape))])
    return level


def setup_inputs(seed: int = 0) -> dict:
    keys = jax.random.split(jax.random.key(seed), 3)
    dirty_image = draw_dirty_image(jax.random.fold_in(keys[2], 71), 0)
    density = jnp.clip(jnp.exp(math.log(4.0) - 2.7725887 * jax.random.uniform(keys[1], (CHANNELS, NROWS, NCOLS), jnp.float32) ** levels(keys[1], (CHANNELS, NROWS, NCOLS), ((0, 8), (1, 2), (2, 2)), -0.2, 0.2)), 0.25, 4.0)
    return dict(dirty_image=dirty_image, density=density)


DAUBECHIES = ((0.7071067811865476, 0.7071067811865476), (0.48296291314469025, 0.836516303737469, 0.22414386804185735, -0.12940952255092145), (0.3326705529509569, 0.8068915093133388, 0.4598775021193313, -0.13501102001039084, -0.08544127388224149, 0.035226291882100656), (0.23037781330885523, 0.7148465705525415, 0.6308807679295904, -0.02798376941698385, -0.18703481171888114, 0.030841381835986965, 0.032883011666982945, -0.010597401784997278))
rim_analysis = 3
rim_synthesis = 2
jacobi_sweeps = 6
STEP_PRIMAL = 0.2
STEP_NUCLEAR = 1.0
STEP_SPARSE = 0.5
NUCLEAR_SCALE = 1.0
SPARSE_SCALE = 0.5
BEST_ACCURACY = lax.Precision.HIGHEST

def analyse_axis(extended, filter_taps, axis_index, margin, out_total):
    tap_count = len(filter_taps)
    offset = tap_count // 2 - 1
    half_total = out_total // 2
    low_band = None
    high_band = None
    for tap_index in range(tap_count):
        start_at = margin + tap_index - offset
        sliced = lax.slice_in_dim(extended, start_at, start_at + 2 * half_total - 1, 2, axis_index)
        low_part = filter_taps[tap_index] * sliced
        high_part = (-1.0) ** tap_index * filter_taps[tap_count - 1 - tap_index] * sliced
        if low_band is None:
            low_band, high_band = (low_part, high_part)
        else:
            low_band, high_band = (low_band + low_part, high_band + high_part)
    return (low_band, high_band)

def decompose_across_width(extended, filter_taps, margin, col_count):
    return jnp.stack(analyse_axis(extended, filter_taps, extended.ndim - 1, margin, col_count), 0)

def analyse_rows(halves, filter_taps, margin, row_count):
    band_ll, band_lh = analyse_axis(halves[0], filter_taps, halves.ndim - 3, margin, row_count)
    band_hl, band_hh = analyse_axis(halves[1], filter_taps, halves.ndim - 3, margin, row_count)
    return jnp.stack([band_ll, band_lh, band_hl, band_hh], 0)

def upsample(values, axis_index):
    spaced = jnp.stack([values, jnp.zeros_like(values)], axis_index + 1)
    new_shape = list(values.shape)
    new_shape[axis_index] = 2 * new_shape[axis_index]
    return spaced.reshape(new_shape)

def synthesise_axis(low_band, high_band, filter_taps, axis_index, margin, out_total):
    tap_count = len(filter_taps)
    offset = tap_count // 2 - 1
    low_up = upsample(low_band, axis_index)
    high_up = upsample(high_band, axis_index)
    result = None
    for tap_index in range(tap_count):
        start_at = offset - tap_index + 2 * margin
        low_slice = lax.slice_in_dim(low_up, start_at, start_at + 2 * out_total, 1, axis_index)
        high_slice = lax.slice_in_dim(high_up, start_at, start_at + 2 * out_total, 1, axis_index)
        contribution = filter_taps[tap_index] * low_slice + (-1.0) ** tap_index * filter_taps[tap_count - 1 - tap_index] * high_slice
        result = contribution if result is None else result + contribution
    return result

def synthesise_plane(band_stack, filter_taps, margin, row_count, col_count):
    col_low = synthesise_axis(band_stack[0], band_stack[1], filter_taps, band_stack.ndim - 3, margin, row_count)
    col_high = synthesise_axis(band_stack[2], band_stack[3], filter_taps, band_stack.ndim - 3, margin, row_count)
    return synthesise_axis(col_low, col_high, filter_taps, band_stack.ndim - 2, margin, col_count)

def pairing_rounds(matrix_order):
    players = list(range(matrix_order))
    rounds_list = []
    for round_index in range(matrix_order - 1):
        left_side = []
        right_side = []
        for slot_index in range(matrix_order // 2):
            first_id = players[slot_index]
            second_id = players[matrix_order - 1 - slot_index]
            left_side.append(min(first_id, second_id))
            right_side.append(max(first_id, second_id))
        rounds_list.append((np.array(left_side), np.array(right_side)))
        players = [players[0]] + [players[-1]] + players[1:-1]
    return rounds_list

def jacobi_mix(gram_matrix, threshold):
    matrix_order = gram_matrix.shape[-1]
    plan = pairing_rounds(matrix_order)
    identity = jnp.broadcast_to(jnp.eye(matrix_order, dtype=gram_matrix.dtype), gram_matrix.shape)

    def jacobi_sweep(step_index, state_pair):
        tableau_array, vectors = state_pair
        for upper_ids, lower_ids in plan:
            diag_upper = tableau_array[..., upper_ids, upper_ids]
            diag_lower = tableau_array[..., lower_ids, lower_ids]
            coupling = tableau_array[..., upper_ids, lower_ids]
            spread = diag_lower - diag_upper
            denominator = jnp.abs(spread) + jnp.sqrt(spread * spread + 4.0 * coupling * coupling)
            positive = denominator > 0
            tangent = jnp.where(positive, jnp.where(spread >= 0, 2.0, -2.0) * coupling / jnp.where(positive, denominator, 1.0), 0.0)
            rotation_cosine = 1.0 / jnp.sqrt(1.0 + tangent * tangent)
            sine_part = tangent * rotation_cosine
            rotation = jnp.zeros_like(tableau_array)
            rotation = rotation.at[..., upper_ids, upper_ids].set(rotation_cosine)
            rotation = rotation.at[..., lower_ids, lower_ids].set(rotation_cosine)
            rotation = rotation.at[..., upper_ids, lower_ids].set(sine_part)
            rotation = rotation.at[..., lower_ids, upper_ids].set(-sine_part)
            tableau_array = jnp.matmul(jnp.matmul(jnp.swapaxes(rotation, -1, -2), tableau_array, precision=BEST_ACCURACY), rotation, precision=BEST_ACCURACY)
            vectors = jnp.matmul(vectors, rotation, precision=BEST_ACCURACY)
        return (tableau_array, vectors)
    tableau_array, vectors = lax.fori_loop(0, jacobi_sweeps, jacobi_sweep, (gram_matrix, identity))
    values = jnp.diagonal(tableau_array, axis1=-2, axis2=-1)
    magnitude = jnp.sqrt(jnp.maximum(values, 0.0))
    weights = threshold / jnp.maximum(magnitude, threshold)
    return jnp.matmul(vectors * weights[..., None, :], jnp.swapaxes(vectors, -1, -2), precision=BEST_ACCURACY)

def pad_plane(values, width):
    widths = [(0, 0)] * (values.ndim - 2) + [(width, width), (width, width)]
    return jnp.pad(values, widths)

def analyse_global(image):
    details = []
    current = image
    for level_index in range(LEVELS):
        row_count = image.shape[1] // 2 ** level_index
        col_count = image.shape[2] // 2 ** level_index
        families = []
        for family in range(NDB):
            source = current if level_index == 0 else current[family]
            halves = decompose_across_width(pad_plane(source, rim_analysis), DAUBECHIES[family], rim_analysis, col_count)
            families.append(analyse_rows(halves, DAUBECHIES[family], rim_analysis, row_count))
        stacked = jnp.stack(families, 0)
        details.append(stacked[:, 1:])
        current = stacked[:, 0]
    return (details, current)

def synthesise_global(details, approx):
    recon = approx
    for level_index in reversed(range(LEVELS)):
        band_stack = jnp.concatenate([recon[:, None], details[level_index]], 1)
        row_count = band_stack.shape[3]
        col_count = band_stack.shape[4]
        families = []
        for family in range(NDB):
            families.append(synthesise_plane(pad_plane(band_stack[family], rim_synthesis), DAUBECHIES[family], rim_synthesis, row_count, col_count))
        recon = jnp.stack(families, 0)
    total = recon[0]
    for family in range(1, NDB):
        total = total + recon[family]
    return total

def nuclear_part(shifted):
    group_count = CHANNELS // GROUP
    blocks = shifted.reshape(group_count, GROUP, N_FROW, TILE_ROWS, N_FCOL, TILE_COLS)
    grams = jnp.einsum('gcarbw,gdarbw->gabcd', blocks, blocks, precision=BEST_ACCURACY)
    rotation_matrix = jacobi_mix(grams, NUCLEAR_SCALE * float(np.sqrt(TILE_ROWS * TILE_COLS)))
    rotated_matrix = jnp.einsum('gabcd,gdarbw->gcarbw', rotation_matrix, blocks, precision=BEST_ACCURACY)
    return rotated_matrix.reshape(shifted.shape)

def reference(dirty_image, density):
    sparse_limit = SPARSE_SCALE * float(np.sqrt(CHANNELS))
    estimate = jnp.maximum(dirty_image, 0.0)
    extrapolated = estimate
    nuclear_dual = jnp.zeros_like(estimate)
    dual_dirac = jnp.zeros_like(estimate)
    dual_details = None
    dual_approx = None
    for iteration in range(ITERS):
        coeff_details, coeff_approx = analyse_global(extrapolated)
        if dual_approx is None:
            dual_details = [jnp.zeros_like(item) for item in coeff_details]
            dual_approx = jnp.zeros_like(coeff_approx)
        upd_dirac = dual_dirac + STEP_SPARSE * extrapolated
        upd_details = [dual_details[idx] + STEP_SPARSE * coeff_details[idx] for idx in range(LEVELS)]
        upd_approx = dual_approx + STEP_SPARSE * coeff_approx
        norm_dirac = lax.optimization_barrier(jnp.sum(upd_dirac * upd_dirac, 0))
        norm_details = [lax.optimization_barrier(jnp.sum(item * item, 2)) for item in upd_details]
        norm_approx = lax.optimization_barrier(jnp.sum(upd_approx * upd_approx, 1))
        dual_dirac = upd_dirac * (sparse_limit / jnp.maximum(jnp.sqrt(norm_dirac), sparse_limit))[None]
        dual_details = [upd_details[idx] * (sparse_limit / jnp.maximum(jnp.sqrt(norm_details[idx]), sparse_limit))[:, :, None] for idx in range(LEVELS)]
        dual_approx = upd_approx * (sparse_limit / jnp.maximum(jnp.sqrt(norm_approx), sparse_limit))[:, None]
        nuclear_dual = nuclear_part(nuclear_dual + STEP_NUCLEAR * extrapolated)
        synthesis = dual_dirac + synthesise_global(dual_details, dual_approx)
        renewed = jnp.maximum(estimate - STEP_PRIMAL * (density * estimate - dirty_image + nuclear_dual + synthesis), 0.0)
        extrapolated = 2.0 * renewed - estimate
        estimate = renewed
    return estimate
```

```python
import math

import jax
import jax.numpy as jnp
import numpy as np
from jax import lax
from jax.experimental import pallas as pl
from jax.experimental.pallas import tpu as pltpu
from jax.sharding import PartitionSpec as P

DAUBECHIES = (
    (0.7071067811865476, 0.7071067811865476),
    (0.48296291314469025, 0.836516303737469, 0.22414386804185735, -0.12940952255092145),
    (
        0.3326705529509569,
        0.8068915093133388,
        0.4598775021193313,
        -0.13501102001039084,
        -0.08544127388224149,
        0.035226291882100656,
    ),
    (
        0.23037781330885523,
        0.7148465705525415,
        0.6308807679295904,
        -0.02798376941698385,
        -0.18703481171888114,
        0.030841381835986965,
        0.032883011666982945,
        -0.010597401784997278,
    ),
)
NDB = len(DAUBECHIES)
JACOBI_SWEEPS = 6
STEP_PRIMAL = 0.2
STEP_SPARSE = 0.5
SPARSE_SCALE = 0.5
LANES = 128
HALO = 8
MIB = 1 << 20
F32 = jnp.float32
BF16 = jnp.bfloat16


def band_taps(family):
    low = DAUBECHIES[family]
    high = [(-1.0) ** k * low[len(low) - 1 - k] for k in range(len(low))]
    return low, high


def phase_taps(family):
    low, high = band_taps(family)
    offset = len(low) // 2 - 1
    table = {}
    for k in range(len(low)):
        s, odd = divmod(k - offset, 2)
        entry = table.setdefault(s, [0.0, 0.0, 0.0, 0.0])
        entry[odd] = low[k]
        entry[2 + odd] = high[k]
    return table


def column_weight(family, band, coefs, pixels):
    taps = band_taps(family)[band]
    k = pixels[:, None] - 2 * coefs[None, :] + len(taps) // 2 - 1
    inside = (k >= 0) & (k < len(taps))
    return np.where(inside, np.asarray(taps)[np.clip(k, 0, len(taps) - 1)], 0.0)


def column_tables(cols, facets):
    half = cols // 2
    pixels = np.arange(cols)
    pairs = [(f, b) for b in range(2) for f in range(NDB)]
    main = np.concatenate([column_weight(f, b, np.arange(half), pixels) for f, b in pairs], 1)
    left, right = pixels[:LANES] - LANES, pixels[:LANES] + cols
    variants = []
    for has_left, has_right in ((False, True), (True, False)) if facets == 2 else ((False, True), (True, True), (True, False)):
        coefs = np.array([-2, -1, half, half + 1])
        real = np.array([has_left, has_left, has_right, has_right])
        around = ([left] if has_left else []) + ([right] if has_right else []) if facets == 2 else [left, right]
        around = np.concatenate(around)

        def strip(rows):
            parts = [column_weight(f, b, coefs, rows) * real for f, b in pairs]
            return np.pad(np.concatenate(parts, 1), ((0, 0), (0, LANES - 4 * len(parts))))

        halo_main = np.concatenate([column_weight(f, b, np.arange(half), around) for f, b in pairs], 1)
        variants.append((strip(pixels), np.concatenate([halo_main, strip(around)], 1)))
    return main, np.stack([v[0] for v in variants]), np.stack([v[1] for v in variants])


def split(table):
    table = jnp.asarray(table, F32)
    top = table.astype(BF16)
    return top, (table - top.astype(F32)).astype(BF16)


def halves(values):
    top = values.astype(BF16)
    return top, (values - top.astype(F32)).astype(BF16)


def dot3(left, right_top, right_low):
    top, low = left
    total = jnp.dot(top, right_low, preferred_element_type=F32) + jnp.dot(low, right_top, preferred_element_type=F32)
    return total + jnp.dot(top, right_top, preferred_element_type=F32)


def side_by_side(ref, tiles):
    return jnp.concatenate([ref[t] for t in tiles], 1)


def swap_halves(values):
    return pltpu.roll(values, 4, 0)


def sublane_taps(first, second):
    rows = lax.broadcasted_iota(jnp.int32, (8, LANES), 0)
    return jnp.where(rows < 4, F32(first), F32(second))


def strip_taps(pick_first, pick_second, s):
    family = lax.broadcasted_iota(jnp.int32, (8, LANES), 1) // 4 % 4
    total = jnp.zeros((8, LANES), F32)
    for f in range(NDB):
        entry = phase_taps(f).get(s)
        if entry is not None:
            total = jnp.where(family == f, sublane_taps(entry[pick_first], entry[pick_second]), total)
    return total


def row_taps(tile, tiles, cross, scale):
    if tile == tiles - 1:
        shifts = range(-2, 3)
        return {s: (strip_taps(0, 3, s) * scale, strip_taps(*cross, s) * scale) for s in shifts}
    table = phase_taps(tile % NDB)
    return {s: (sublane_taps(e[0] * scale, e[3] * scale), sublane_taps(e[cross[0]] * scale, e[cross[1]] * scale)) for s, e in table.items()}


def pack4(squares):
    rows = lax.broadcasted_iota(jnp.int32, (8, LANES), 0)

    def merge(a, b, step):
        keep = rows % (2 * step) < step
        if b is None:
            return a + pltpu.roll(a, 8 - step, 0)
        return jnp.where(keep, a, pltpu.roll(b, step, 0)) + jnp.where(keep, pltpu.roll(a, 8 - step, 0), b)

    items = list(squares) + [None] * (4 - len(squares))
    first = merge(items[0], items[1], 1)
    second = None if items[2] is None else merge(items[2], items[3], 1)
    return merge(first, second, 2)


def analysis_kernel(sides, dirty, above, beside, corner, main_t, main_l, strip_t, strip_l, halo_t, halo_l, u_ref, n_ref, ext, coef):
    channels, rows, cols = dirty.shape
    window = rows + HALO + 4
    x, y = lax.axis_index("frow"), lax.axis_index("chan") % 2
    place, facets = lax.axis_index("fcol"), lax.axis_size("fcol")
    var = place if facets == 2 else jnp.where(place == 0, 0, jnp.where(place == facets - 1, 2, 1))
    tiles = 2 * NDB + 1

    edge = jnp.zeros((ext.shape[0], 4 * channels, LANES), F32)
    ext[:, pl.ds(pl.multiple_of(x * (window - 4) * channels, 16), 4 * channels), :] = edge
    for start, count, mid, wing in ((4 + 4 * x, rows, dirty, beside), ((1 - x) * (window - HALO), HALO, above, corner)):
        for c in range(channels):
            at = pl.ds(start * channels + c, count, stride=channels)
            for t in range(cols // LANES):
                ext[t, at, :] = jnp.maximum(mid[c, :, t * LANES : (t + 1) * LANES], 0.0)
            for t in range(sides):
                ext[cols // LANES + t, at, :] = jnp.maximum(wing[c, :, t * LANES : (t + 1) * LANES], 0.0)

    inner = halves(side_by_side(ext, range(cols // LANES)))
    outer = halves(side_by_side(ext, range(cols // LANES, cols // LANES + sides)))
    coef[:, : cols * NDB] = dot3(inner, main_t[...], main_l[...]) + dot3(outer, halo_t[var, :, : cols * NDB], halo_l[var, :, : cols * NDB])
    coef[:, cols * NDB :] = dot3(inner, strip_t[var], strip_l[var]) + dot3(outer, halo_t[var, :, cols * NDB :], halo_l[var, :, cols * NDB :])

    outs = rows // 2 + 2
    squares = {}
    for tile in range(tiles):
        lanes = slice(tile * LANES, (tile + 1) * LANES)
        taps = row_taps(tile, tiles, (2, 1), STEP_SPARSE)
        pairs = [coef[8 * i : 8 * i + 8, lanes] for i in range(window // 2)]
        for j in range(outs):
            direct = crossed = None
            for s, (d, e) in taps.items():
                source = pairs[j + 2 + s]
                direct = d * source if direct is None else direct + d * source
                crossed = e * source if crossed is None else crossed + e * source
            value = direct + swap_halves(crossed)
            u_ref[8 * j : 8 * j + 8, lanes] = value
            squares[tile, j] = value * value
        if tile % NDB == NDB - 1:
            side = (tile // NDB) ^ y
            flat = [squares.pop((t, j)) for t in range(tile - NDB + 1, tile + 1) for j in range(outs)]
            for g in range(len(flat) // 4):
                n_ref[side, 8 * g : 8 * g + 8, :] = pack4(flat[4 * g : 4 * g + 4])
    base = outs * NDB * 2
    for half in range(2):
        at = base
        flat = [squares.pop((tiles - 1, j)) for j in range(half * outs // 2, (half + 1) * outs // 2)]
        for g in range(0, len(flat), 4):
            n_ref[half ^ y, at : at + 8, :] = pack4(flat[g : g + 4])
            at += 8
        for r in range(half * rows // 2, (half + 1) * rows // 2, 8):
            for t in range(cols // LANES):
                total = None
                for c in range(channels):
                    value = STEP_SPARSE * jnp.maximum(dirty[c, r : r + 8, t * LANES : (t + 1) * LANES], 0.0)
                    total = value * value if total is None else total + value * value
                n_ref[half ^ y, at : at + 8, :] = total
                at += 8


def pairing_rounds(order):
    players = list(range(order))
    rounds = []
    for _ in range(order - 1):
        rounds.append([(min(a, b), max(a, b)) for a, b in zip(players[: order // 2], players[: order // 2 - 1 : -1])])
        players = [players[0]] + [players[-1]] + players[1:-1]
    return rounds


def down(values):
    for step in (4, 2, 1):
        values = values + pltpu.roll(values, step, 0)
    return values


def nuclear_kernel(limit, own, other, out, group, mix):
    channels, rows, cols = own.shape
    order = 2 * channels
    y = lax.axis_index("chan") % 2
    for c in range(channels):
        group[y * channels + c] = jnp.maximum(own[c], 0.0)
        group[(1 - y) * channels + c] = jnp.maximum(other[c], 0.0)
    blocks = [(slice(r, r + 8), slice(t, t + LANES)) for r in range(0, rows, 8) for t in range(0, cols, LANES)]
    partial = {}
    for at in blocks:
        held = [group[(c, *at)] for c in range(order)]
        for i in range(order):
            for j in range(i + 1):
                term = held[i] * held[j]
                partial[i, j] = partial[i, j] + term if (i, j) in partial else term
    row_sum = {key: jnp.sum(value, axis=0, keepdims=True) for key, value in partial.items()}
    sub = lax.broadcasted_iota(jnp.int32, (order, LANES), 0)
    turned, vectors, diag = [], [], []
    for j in range(order):
        stacked = jnp.concatenate([row_sum[max(i, j), min(i, j)] for i in range(order)], 0)
        column = jnp.broadcast_to(jnp.sum(stacked, axis=1, keepdims=True), (order, LANES))
        turned.append(column)
        unit = jnp.where(sub == j, F32(1.0), F32(0.0))
        vectors.append(unit)
        diag.append(down(column * unit))

    rounds = pairing_rounds(order)

    def sweep(_, state):
        turned, vectors, diag = (list(part) for part in state)
        for pairs in rounds:
            for p, q in pairs:
                coupling = down(vectors[p] * turned[q])
                spread = diag[q] - diag[p]
                square = spread * spread + 4.0 * coupling * coupling
                positive = square > 0.0
                inverse = jnp.where(positive, lax.rsqrt(jnp.where(positive, square, 1.0)), 0.0)
                cosine2 = jnp.where(positive, 0.5 + 0.5 * jnp.abs(spread) * inverse, 1.0)
                other = lax.rsqrt(cosine2)
                c = cosine2 * other
                s = jnp.where(spread >= 0.0, coupling, -coupling) * inverse * other
                shift = s * other * coupling
                diag[p], diag[q] = diag[p] - shift, diag[q] + shift
                turned[p], turned[q] = c * turned[p] - s * turned[q], s * turned[p] + c * turned[q]
                vectors[p], vectors[q] = c * vectors[p] - s * vectors[q], s * vectors[p] + c * vectors[q]
        return tuple(turned), tuple(vectors), tuple(diag)

    turned, vectors, _ = lax.fori_loop(0, JACOBI_SWEEPS, sweep, (tuple(turned), tuple(vectors), tuple(diag)))
    weighted = []
    for j in range(order):
        value = down(vectors[j] * turned[j])
        weighted.append(vectors[j] * (limit / jnp.maximum(jnp.sqrt(jnp.maximum(value, 0.0)), limit)))
    for k in range(order):
        total = None
        for j in range(order):
            term = weighted[j] * jnp.broadcast_to(vectors[j][k : k + 1, :], (order, LANES))
            total = term if total is None else total + term
        mix[k] = total
    for i in range(channels):
        row = [jnp.broadcast_to(mix[k, pl.ds(y * channels + i, 1), :], (order, LANES)) for k in range(order)]
        for at in blocks:
            total = None
            for k in range(order):
                term = row[k] * group[(k, *at)]
                total = term if total is None else total + term
            out[(i, *at)] = total


def synthesis_kernel(limit, dirty, density, nuclear, u_ref, n_ref, main_t, main_l, strip_t, strip_l, out, scale, spread, image):
    channels, rows, cols = dirty.shape
    x, y = lax.axis_index("frow"), lax.axis_index("chan") % 2
    place, facets = lax.axis_index("fcol"), lax.axis_size("fcol")
    var = place if facets == 2 else jnp.where(place == 0, 0, jnp.where(place == facets - 1, 2, 1))
    tiles = 2 * NDB + 1
    outs = rows // 2 + 2
    for half in range(2):
        scale[half] = limit * lax.rsqrt(jnp.maximum(n_ref[half ^ y], limit * limit))
    sub = lax.broadcasted_iota(jnp.int32, (8, LANES), 0)

    def widen(half, at, item):
        first = jnp.broadcast_to(scale[half, at + item : at + item + 1, :], (8, LANES))
        second = jnp.broadcast_to(scale[half, at + 4 + item : at + 5 + item, :], (8, LANES))
        return jnp.where(sub < 4, first, second)

    base = outs * NDB * 2
    strips = (outs // 2 + 3) // 4
    for tile in range(tiles):
        lanes = slice(tile * LANES, (tile + 1) * LANES)
        taps = row_taps(tile, tiles, (1, 2), 1.0)
        dual = []
        for j in range(outs):
            if tile == tiles - 1:
                half, item = divmod(j, outs // 2)
                factor = widen(half, base + 8 * (item // 4), item % 4)
            else:
                half, item = tile // NDB, (tile % NDB) * outs + j
                factor = widen(half, 8 * (item // 4), item % 4)
            dual.append(u_ref[8 * j : 8 * j + 8, lanes] * factor)
        empty = jnp.zeros((8, LANES), F32)
        below = [jnp.where(x == 0, empty, dual[0]), jnp.where(x == 0, empty, dual[1])]
        middle = [jnp.where(x == 0, dual[i], dual[i + 2]) for i in range(rows // 2)]
        after = [jnp.where(x == 0, dual[outs - 2], empty), jnp.where(x == 0, dual[outs - 1], empty)]
        padded = below + middle + after
        for i in range(rows // 2):
            direct = crossed = None
            for s, (d, e) in taps.items():
                source = padded[i + 2 - s]
                direct = d * source if direct is None else direct + d * source
                crossed = e * source if crossed is None else crossed + e * source
            spread[8 * i : 8 * i + 8, lanes] = direct + swap_halves(crossed)
    result = dot3(halves(spread[:, : cols * NDB]), main_t[...], main_l[...]) + dot3(halves(spread[:, cols * NDB :]), strip_t[var], strip_l[var])
    for t in range(cols // LANES):
        image[t] = result[:, t * LANES : (t + 1) * LANES]
    for c in range(channels):
        for r in range(0, rows, 8):
            for t in range(cols // LANES):
                lanes = slice(t * LANES, (t + 1) * LANES)
                half, inside = divmod(r, rows // 2)
                at = base + 8 * strips + 8 * (inside // 8 * (cols // LANES) + t)
                raw = dirty[c, r : r + 8, lanes]
                estimate = jnp.maximum(raw, 0.0)
                dual = STEP_SPARSE * estimate * scale[half, at : at + 8, :]
                synthesis = dual + image[t, pl.ds(r * channels + c, 8, stride=channels), :]
                step = density[c, r : r + 8, lanes] * estimate - raw + nuclear[c, r : r + 8, lanes] + synthesis
                out[c, r : r + 8, lanes] = jnp.maximum(estimate - STEP_PRIMAL * step, 0.0)


def exchange(values, axis, bit):
    count = lax.axis_size(axis)
    return lax.ppermute(values, axis, [(i, i ^ bit) for i in range(count)])


def vmem(count):
    return [pl.BlockSpec(memory_space=pltpu.VMEM)] * count


def beside_columns(values, facets):
    last, first = values[..., values.shape[-1] - LANES :], values[..., :LANES]
    if facets == 2:
        return exchange(jnp.where(lax.axis_index("fcol") == 0, last, first), "fcol", 1)
    left = lax.ppermute(last, "fcol", [(i, i + 1) for i in range(facets - 1)])
    right = lax.ppermute(first, "fcol", [(i + 1, i) for i in range(facets - 1)])
    return jnp.concatenate([left, right], -1)


def on_device(dirty_image, density):
    channels, rows, cols = dirty_image.shape
    facets, chans = lax.axis_size("fcol"), lax.axis_size("chan")
    nuclear_limit = math.sqrt(rows * cols)
    sparse_limit = SPARSE_SCALE * math.sqrt(channels * chans)
    main, strip, halo = column_tables(cols, facets)
    sides = halo.shape[1] // LANES
    main_t, main_l = split(main)
    strip_t, strip_l = split(strip)
    halo_t, halo_l = split(halo)
    main_back, main_back_l = split(main.T)
    strip_back, strip_back_l = split(strip.transpose(0, 2, 1))

    x = lax.axis_index("frow")
    edge = lax.dynamic_slice_in_dim(dirty_image, (1 - x) * (rows - HALO), HALO, 1)
    above = exchange(edge, "frow", 1)
    other = exchange(dirty_image, "chan", 1)
    beside = beside_columns(dirty_image, facets)
    corner = beside_columns(above, facets)

    window = rows + HALO + 4
    outs = rows // 2 + 2
    tiles = 2 * NDB + 1
    packed = outs * NDB * 2 + 8 * ((outs // 2 + 3) // 4) + rows * cols // LANES // 2
    coefs, norms = pl.pallas_call(
        lambda *refs: analysis_kernel(sides, *refs),
        name="analysis",
        out_shape=(jax.ShapeDtypeStruct((8 * outs, tiles * LANES), F32), jax.ShapeDtypeStruct((2, packed, LANES), F32)),
        in_specs=vmem(10),
        out_specs=tuple(vmem(2)),
        scratch_shapes=[pltpu.VMEM((cols // LANES + sides, window * channels, LANES), F32), pltpu.VMEM((window * channels, tiles * LANES), F32)],
        compiler_params=pltpu.CompilerParams(vmem_limit_bytes=24 * MIB),
    )(dirty_image, above, beside, corner, main_t, main_l, strip_t, strip_l, halo_t, halo_l)

    nuclear = pl.pallas_call(
        lambda *refs: nuclear_kernel(nuclear_limit, *refs),
        name="nuclear",
        out_shape=jax.ShapeDtypeStruct(dirty_image.shape, F32),
        in_specs=vmem(2),
        out_specs=vmem(1)[0],
        scratch_shapes=[pltpu.VMEM((2 * channels, rows, cols), F32), pltpu.VMEM((2 * channels, 2 * channels, LANES), F32)],
        compiler_params=pltpu.CompilerParams(vmem_limit_bytes=16 * MIB),
    )(dirty_image, other)

    total = norms[0] + exchange(norms[1], "chan", 1)
    bit = 2
    while bit < chans:
        total = total + exchange(total, "chan", bit)
        bit *= 2
    totals = jnp.stack([total, exchange(total, "chan", 1)], 0)

    return pl.pallas_call(
        lambda *refs: synthesis_kernel(sparse_limit, *refs),
        name="synthesis",
        out_shape=jax.ShapeDtypeStruct(dirty_image.shape, F32),
        in_specs=vmem(9),
        out_specs=vmem(1)[0],
        scratch_shapes=[
            pltpu.VMEM((2, packed, LANES), F32),
            pltpu.VMEM((4 * rows, tiles * LANES), F32),
            pltpu.VMEM((cols // LANES, 4 * rows, LANES), F32),
        ],
        compiler_params=pltpu.CompilerParams(vmem_limit_bytes=24 * MIB),
    )(dirty_image, density, nuclear, coefs, totals, main_back, main_back_l, strip_back, strip_back_l)


def solution(mesh):
    return jax.shard_map(
        on_device,
        mesh=mesh,
        in_specs=(P("chan", "frow", "fcol"), P("chan", "frow", "fcol")),
        out_specs=P("chan", "frow", "fcol"),
        check_vma=False,
    )
```

```python
import math

import jax
import jax.numpy as jnp
import numpy as np
from jax import lax
from jax.experimental import pallas as pl
from jax.experimental.pallas import tpu as pltpu
from jax.sharding import PartitionSpec as P

DAUBECHIES = (
    (0.7071067811865476, 0.7071067811865476),
    (0.48296291314469025, 0.836516303737469, 0.22414386804185735, -0.12940952255092145),
    (
        0.3326705529509569,
        0.8068915093133388,
        0.4598775021193313,
        -0.13501102001039084,
        -0.08544127388224149,
        0.035226291882100656,
    ),
    (
        0.23037781330885523,
        0.7148465705525415,
        0.6308807679295904,
        -0.02798376941698385,
        -0.18703481171888114,
        0.030841381835986965,
        0.032883011666982945,
        -0.010597401784997278,
    ),
)
NDB = len(DAUBECHIES)
JACOBI_SWEEPS = 6
STEP_PRIMAL = 0.2
STEP_SPARSE = 0.5
SPARSE_SCALE = 0.5
LANES = 128
STRIP = 32
HALO = 8
MIB = 1 << 20
F32 = jnp.float32
BF16 = jnp.bfloat16


def band_taps(family):
    low = DAUBECHIES[family]
    high = [(-1.0) ** k * low[len(low) - 1 - k] for k in range(len(low))]
    return low, high


def phase_taps(family):
    low, high = band_taps(family)
    offset = len(low) // 2 - 1
    table = {}
    for k in range(len(low)):
        s, odd = divmod(k - offset, 2)
        entry = table.setdefault(s, [0.0, 0.0, 0.0, 0.0])
        entry[odd] = low[k]
        entry[2 + odd] = high[k]
    return table


def column_weight(family, band, coefs, pixels):
    taps = band_taps(family)[band]
    k = pixels[:, None] - 2 * coefs[None, :] + len(taps) // 2 - 1
    inside = (k >= 0) & (k < len(taps))
    return np.where(inside, np.asarray(taps)[np.clip(k, 0, len(taps) - 1)], 0.0)


def column_table(cols):
    half = cols // 2
    pixels = np.concatenate([np.arange(cols), np.arange(-LANES, 0), np.arange(cols, cols + LANES)])
    pairs = [(f, b) for b in range(2) for f in range(NDB)]
    beyond = np.array([-2, -1, half, half + 1])
    parts = [column_weight(f, b, np.arange(half), pixels) for f, b in pairs] + [column_weight(f, b, beyond, pixels) for f, b in pairs]
    table = np.concatenate(parts, 1)
    table = jnp.asarray(np.pad(table, ((0, 0), (0, LANES - 4 * len(pairs)))), F32)
    top = table.astype(BF16)
    return jnp.stack([top, (table - top.astype(F32)).astype(BF16)], 0)


def halves(values):
    top = values.astype(BF16)
    return top, (values - top.astype(F32)).astype(BF16)


def dot3(left, right, dims=((1,), (0,))):
    def dot(one, two):
        return lax.dot_general(one, two, (dims, ((), ())), preferred_element_type=F32)

    return dot(left[0], right[1]) + dot(left[1], right[0]) + dot(left[0], right[0])


def side_by_side(ref, tiles):
    return jnp.concatenate([ref[t] for t in tiles], 1)


def swap_halves(values):
    return pltpu.roll(values, 4, 0)


def sublane_taps(first, second):
    rows = lax.broadcasted_iota(jnp.int32, (8, LANES), 0)
    return jnp.where(rows < 4, F32(first), F32(second))


def strip_taps(pick_first, pick_second, s):
    family = lax.broadcasted_iota(jnp.int32, (8, LANES), 1) // 4 % 4
    total = jnp.zeros((8, LANES), F32)
    for f in range(NDB):
        entry = phase_taps(f).get(s)
        if entry is not None:
            total = jnp.where(family == f, sublane_taps(entry[pick_first], entry[pick_second]), total)
    return total


def row_taps(family, cross, scale):
    table = phase_taps(family)
    return {s: (sublane_taps(e[0] * scale, e[3] * scale), sublane_taps(e[cross[0]] * scale, e[cross[1]] * scale)) for s, e in table.items()}


def strip_row_taps(cross, scale):
    column = lax.broadcasted_iota(jnp.int32, (8, LANES), 1) % 4
    place, facets = lax.axis_index("fcol"), lax.axis_size("fcol")
    kept = jnp.where(column < 2, jnp.where(place > 0, F32(scale), F32(0.0)), jnp.where(place < facets - 1, F32(scale), F32(0.0)))
    return {s: (strip_taps(0, 3, s) * kept, strip_taps(*cross, s) * kept) for s in range(-2, 3)}


def filter_rows(taps, pairs, at):
    direct = crossed = None
    for s, (d, e) in taps.items():
        source = pairs[at(s)]
        direct = d * source if direct is None else direct + d * source
        crossed = e * source if crossed is None else crossed + e * source
    return direct + swap_halves(crossed)


def pack4(items):
    rows = lax.broadcasted_iota(jnp.int32, (8, LANES), 0)

    def merge(a, b, step):
        keep = rows % (2 * step) < step
        return jnp.where(keep, a, pltpu.roll(b, step, 0)) + jnp.where(keep, pltpu.roll(a, 8 - step, 0), b)

    return merge(merge(items[0], items[1], 1), merge(items[2], items[3], 1), 2)


def fill_rows(ext, row, count, start, sources):
    channels = 4
    t = 0
    for ref in sources:
        for u in range(ref.shape[-1] // LANES):
            for c in range(channels):
                value = ref[c, pl.ds(start, count), u * LANES : (u + 1) * LANES]
                ext[t, pl.ds(row * channels + c, count, stride=channels), :] = jnp.maximum(value, 0.0)
            t += 1


def filter_columns(ext, table, cols):
    left = halves(side_by_side(ext, range(ext.shape[0])))
    return dot3(left, [table[0], table[1]])


def coefficients(coef, u_ref, count, strip_item):
    tiles = 2 * NDB + 1
    squares = []
    for tile in range(tiles):
        lanes = slice(tile * LANES, (tile + 1) * LANES)
        taps = strip_row_taps((2, 1), STEP_SPARSE) if tile == tiles - 1 else row_taps(tile % NDB, (2, 1), STEP_SPARSE)
        pairs = [coef[8 * i : 8 * i + 8, lanes] for i in range(count + 4)]
        for j in range(count):
            value = filter_rows(taps, pairs, lambda s: j + 2 + s)
            u_ref[8 * j : 8 * j + 8, lanes] = value
            squares.append(value * value)
    packed = []
    for half in range(2):
        flat = squares[half * NDB * count : (half + 1) * NDB * count]
        packed.append([pack4(flat[g : g + 4]) for g in range(0, len(flat), 4)])
        strip = squares[2 * NDB * count + half * (count // 2) : 2 * NDB * count + (half + 1) * (count // 2)]
        items = [jnp.zeros((8, LANES), F32)] * strip_item
        for g in range(0, len(strip), 4):
            total = strip[g]
            for k in range(1, len(strip[g : g + 4])):
                total = total + pltpu.roll(strip[g + k], STRIP * k, 1)
            items.append(total)
        items += [jnp.zeros((8, LANES), F32)] * (4 - len(items))
        packed[half].append(pack4(items))
    return packed


def store_halves(packed, keep, send, base=0):
    y = lax.axis_index("chan") % 2
    for i, (a, b) in enumerate(zip(*packed)):
        keep[base + 8 * i : base + 8 * i + 8, :] = jnp.where(y == 0, a, b)
        send[base + 8 * i : base + 8 * i + 8, :] = jnp.where(y == 0, b, a)


def inner_kernel(own, *refs):
    *beside, table, u_ref, keep, send, ext, coef = refs
    channels, rows, cols = own.shape
    x = lax.axis_index("frow")
    edge = jnp.zeros((ext.shape[0], 4 * channels, LANES), F32)
    ext[:, pl.ds(pl.multiple_of(x * rows * channels, 16), 4 * channels), :] = edge
    fill_rows(ext, 4 * (1 - x), rows, 0, [own, *beside])
    coef[...] = filter_columns(ext, table, cols)
    packed = coefficients(coef, u_ref, rows // 2 - 2, 0)
    for half in range(2):
        for r in range(half * rows // 2, (half + 1) * rows // 2, 8):
            for t in range(cols // LANES):
                total = None
                for c in range(channels):
                    value = STEP_SPARSE * jnp.maximum(own[c, r : r + 8, t * LANES : (t + 1) * LANES], 0.0)
                    total = value * value if total is None else total + value * value
                packed[half].append(total)
    store_halves(packed, keep, send)


def border_kernel(sides, own, above, keep_inner, send_inner, *refs):
    beside, corner = refs[:sides], refs[sides : 2 * sides]
    table, u_ref, keep, send, ext, coef = refs[2 * sides :]
    rows, cols = own.shape[1:]
    x, y = lax.axis_index("frow"), lax.axis_index("chan") % 2
    places = Places(rows, cols)
    fill_rows(ext, HALO * x, HALO, (1 - x) * (rows - HALO), [own, *beside])
    fill_rows(ext, HALO * (1 - x), HALO, 0, [above, *corner])
    coef[...] = filter_columns(ext, table, cols)
    packed = coefficients(coef, u_ref, 4, 2)
    strips = [part.pop() for part in packed]
    store_halves(packed, keep, send, places.border)
    keep[: places.border, :] = keep_inner[...]
    send[: places.border, :] = send_inner[...]
    at = slice(places.strip, places.strip + 8)
    keep[at, :] = keep_inner[at, :] + jnp.where(y == 0, *strips)
    send[at, :] = send_inner[at, :] + jnp.where(y == 0, *strips[::-1])


def pairing_rounds(order):
    players = list(range(order))
    rounds = []
    for _ in range(order - 1):
        rounds.append([(min(a, b), max(a, b)) for a, b in zip(players[: order // 2], players[: order // 2 - 1 : -1])])
        players = [players[0]] + [players[-1]] + players[1:-1]
    return rounds


def down(values):
    for step in (4, 2, 1):
        values = values + pltpu.roll(values, step, 0)
    return values


def nuclear_kernel(limit, own, other, out, group, mix):
    channels, rows, cols = own.shape
    order = 2 * channels
    y = lax.axis_index("chan") % 2
    for c in range(channels):
        group[y * channels + c] = jnp.maximum(own[c], 0.0)
        group[(1 - y) * channels + c] = jnp.maximum(other[c], 0.0)
    blocks = [(slice(r, r + 8), slice(t, t + LANES)) for r in range(0, rows, 8) for t in range(0, cols, LANES)]
    partial = {}
    for at in blocks:
        held = [group[(c, *at)] for c in range(order)]
        for i in range(order):
            for j in range(i + 1):
                term = held[i] * held[j]
                partial[i, j] = partial[i, j] + term if (i, j) in partial else term
    row_sum = {key: jnp.sum(value, axis=0, keepdims=True) for key, value in partial.items()}
    sub = lax.broadcasted_iota(jnp.int32, (order, LANES), 0)
    turned, vectors, diag = [], [], []
    for j in range(order):
        stacked = jnp.concatenate([row_sum[max(i, j), min(i, j)] for i in range(order)], 0)
        column = jnp.broadcast_to(jnp.sum(stacked, axis=1, keepdims=True), (order, LANES))
        turned.append(column)
        unit = jnp.where(sub == j, F32(1.0), F32(0.0))
        vectors.append(unit)
        diag.append(down(column * unit))

    rounds = pairing_rounds(order)

    def sweep(_, state):
        turned, vectors, diag = (list(part) for part in state)
        for pairs in rounds:
            for p, q in pairs:
                coupling = down(vectors[p] * turned[q])
                spread = diag[q] - diag[p]
                square = spread * spread + 4.0 * coupling * coupling
                positive = square > 0.0
                inverse = jnp.where(positive, lax.rsqrt(jnp.where(positive, square, 1.0)), 0.0)
                cosine2 = jnp.where(positive, 0.5 + 0.5 * jnp.abs(spread) * inverse, 1.0)
                other = lax.rsqrt(cosine2)
                c = cosine2 * other
                s = jnp.where(spread >= 0.0, coupling, -coupling) * inverse * other
                shift = s * other * coupling
                diag[p], diag[q] = diag[p] - shift, diag[q] + shift
                turned[p], turned[q] = c * turned[p] - s * turned[q], s * turned[p] + c * turned[q]
                vectors[p], vectors[q] = c * vectors[p] - s * vectors[q], s * vectors[p] + c * vectors[q]
        return tuple(turned), tuple(vectors), tuple(diag)

    turned, vectors, _ = lax.fori_loop(0, JACOBI_SWEEPS, sweep, (tuple(turned), tuple(vectors), tuple(diag)))
    weighted = []
    for j in range(order):
        value = down(vectors[j] * turned[j])
        weighted.append(vectors[j] * (limit / jnp.maximum(jnp.sqrt(jnp.maximum(value, 0.0)), limit)))
    for k in range(order):
        total = None
        for j in range(order):
            term = weighted[j] * jnp.broadcast_to(vectors[j][k : k + 1, :], (order, LANES))
            total = term if total is None else total + term
        mix[k] = total
    for i in range(channels):
        row = [jnp.broadcast_to(mix[k, pl.ds(y * channels + i, 1), :], (order, LANES)) for k in range(order)]
        for at in blocks:
            total = None
            for k in range(order):
                term = row[k] * group[(k, *at)]
                total = term if total is None else total + term
            out[(i, *at)] = total


def scales(limit, norms):
    return limit * lax.rsqrt(jnp.maximum(norms, limit * limit))


def widen(scale, at, item):
    sub = lax.broadcasted_iota(jnp.int32, (8, LANES), 0)
    first = jnp.broadcast_to(scale[at + item : at + item + 1, :], (8, LANES))
    second = jnp.broadcast_to(scale[at + 4 + item : at + 5 + item, :], (8, LANES))
    return jnp.where(sub < 4, first, second)


def spread_rows(inner, border, taps, spread, lanes):
    x = lax.axis_index("frow")
    empty = jnp.zeros((8, LANES), F32)
    count = len(inner)
    upper = [empty, empty, *inner, *border]
    lower = [*border, *inner, empty, empty]
    padded = [jnp.where(x == 0, a, b) for a, b in zip(upper, lower)]
    for i in range(count + 2):
        spread[8 * i : 8 * i + 8, lanes] = filter_rows(taps, padded, lambda s: i + 2 - s)


class Places:
    def __init__(self, rows, cols):
        self.inner = rows // 2 - 2
        self.strip = 2 * NDB * self.inner
        self.dirac = self.strip + 8
        self.border = self.dirac + rows * cols // LANES // 2
        self.all = self.border + 2 * NDB * 4


def half_duals(places, half, scale, u_inner, u_border, spread):
    for family in range(NDB):
        if isinstance(half, int):
            lanes = slice((half * NDB + family) * LANES, (half * NDB + family + 1) * LANES)
        else:
            lanes = pl.ds(pl.multiple_of((half * NDB + family) * LANES, LANES), LANES)
        duals = []
        for ref, base, count in ((u_inner, 0, places.inner), (u_border, places.border, 4)):
            items = [(base + 8 * ((family * count + j) // 4), (family * count + j) % 4) for j in range(count)]
            duals.append([ref[8 * j : 8 * j + 8, lanes] * widen(scale, *items[j]) for j in range(count)])
        spread_rows(*duals, row_taps(family, (1, 2), 1.0), spread, slice(family * LANES, (family + 1) * LANES))


def first_kernel(limit, raw, density, nuclear, u_inner, u_border, mine, table, step, spread, scale):
    channels, rows, cols = raw.shape
    y = lax.axis_index("chan") % 2
    scale[...] = scales(limit, mine[...])
    half_duals(Places(rows, cols), y, scale, u_inner, u_border, spread)
    lanes = pl.ds(pl.multiple_of(y * NDB * LANES, NDB * LANES), NDB * LANES)
    result = dot3(halves(spread[...]), [table[i, :cols, lanes] for i in range(2)], ((1,), (1,)))
    for t in range(cols // LANES):
        step[cols // LANES + t] = result[:, t * LANES : (t + 1) * LANES]
    for c in range(channels):
        for t in range(cols // LANES):
            lanes = slice(t * LANES, (t + 1) * LANES)
            estimate = jnp.maximum(raw[c, :, lanes], 0.0)
            step[t, c * rows : (c + 1) * rows, :] = density[c, :, lanes] * estimate - raw[c, :, lanes] + nuclear[c, :, lanes]


def second_kernel(limit, raw, step, u_inner, u_border, mine, theirs, table, out, spread, image, scale):
    channels, rows, cols = raw.shape
    y = lax.axis_index("chan") % 2
    places = Places(rows, cols)
    scale[y] = scales(limit, mine[...])
    scale[1 - y] = scales(limit, theirs[...])
    half_duals(places, 1 - y, scale.at[1 - y], u_inner, u_border, spread)
    main = 2 * NDB * LANES
    duals = []
    for ref, item, count in ((u_inner, 0, places.inner), (u_border, 2, 4)):
        rolled = []
        for j in range(count):
            half, k = divmod(j, count // 2)
            factor = widen(scale.at[half], places.strip, item + k // 4)
            factor = factor if k % 4 == 0 else pltpu.roll(factor, LANES - STRIP * (k % 4), 1)
            rolled.append(ref[8 * j : 8 * j + 8, main:] * factor)
        duals.append(rolled)
    spread_rows(*duals, strip_row_taps((1, 2), 1.0), spread, slice(NDB * LANES, (NDB + 1) * LANES))
    lanes = pl.ds(pl.multiple_of((1 - y) * NDB * LANES, NDB * LANES), NDB * LANES)
    left = halves(spread[...])
    right = [jnp.concatenate([table[i, :cols, lanes], table[i, :cols, main:]], 1) for i in range(2)]
    result = dot3(left, right, ((1,), (1,)))
    for t in range(cols // LANES):
        image[t] = result[:, t * LANES : (t + 1) * LANES] + step[cols // LANES + t]
    for c in range(channels):
        for r in range(0, rows, 8):
            for t in range(cols // LANES):
                lanes = slice(t * LANES, (t + 1) * LANES)
                half, inside = divmod(r, rows // 2)
                at = places.dirac + 8 * (inside // 8 * (cols // LANES) + t)
                estimate = jnp.maximum(raw[c, r : r + 8, lanes], 0.0)
                dual = STEP_SPARSE * estimate * scale[half, at : at + 8, :]
                synthesis = dual + image[t, pl.ds(r * channels + c, 8, stride=channels), :]
                total = step[t, c * rows + r : c * rows + r + 8, :] + synthesis
                out[c, r : r + 8, lanes] = jnp.maximum(estimate - STEP_PRIMAL * total, 0.0)


def sent_tiles(cols):
    if lax.axis_size("fcol") == 2:
        return [pl.ds(pl.multiple_of((1 - lax.axis_index("fcol")) * (cols - LANES), LANES), LANES)]
    return [slice(cols - LANES, cols), slice(0, LANES)]


def edges_kernel(sides, dirty, own, edge, *refs):
    wings, corners = refs[:sides], refs[sides : 2 * sides]
    rows, cols = dirty.shape[1:]
    start = pl.ds(pl.multiple_of((1 - lax.axis_index("frow")) * (rows - HALO), HALO), HALO)
    own[...] = dirty[...]
    edge[...] = dirty[:, start, :]
    for wing, corner, lanes in zip(wings, corners, sent_tiles(cols)):
        wing[...] = dirty[:, :, lanes]
        corner[...] = dirty[:, start, lanes]


def load_kernel(sides, table, near, sems):
    if sides == 1:
        cols = table.shape[1] - 2 * LANES
        beyond = pl.multiple_of(cols + (1 - lax.axis_index("fcol")) * LANES, LANES)
        loads = [pltpu.make_async_copy(table.at[:, :cols, :], near.at[:, :cols, :], sems.at[0])]
        loads.append(pltpu.make_async_copy(table.at[:, pl.ds(beyond, LANES), :], near.at[:, cols:, :], sems.at[1]))
    else:
        loads = [pltpu.make_async_copy(table, near, sems.at[0])]
    for load in loads:
        load.start()
    for load in loads:
        load.wait()


def add_kernel(one, two, *refs):
    refs[-1][...] = one[...] + two[...]


def add_and_copy_kernel(one, two, image, total, again):
    total[...] = one[...] + two[...]
    again[...] = image[...]


def exchange(values, axis, bit):
    count = lax.axis_size(axis)
    return lax.ppermute(values, axis, [(i, i ^ bit) for i in range(count)])


def vmem(count):
    return [pl.BlockSpec(memory_space=pltpu.VMEM)] * count


def call(kernel, name, shapes, operands, scratch=(), limit=16, later=()):
    many = [jax.ShapeDtypeStruct(shape, F32) if isinstance(shape, tuple) else shape for shape in shapes]
    results = pl.pallas_call(
        kernel,
        name=name,
        out_shape=many,
        in_specs=vmem(len(operands)) + [pl.BlockSpec(memory_space=pl.ANY)] * len(later),
        out_specs=vmem(len(many)),
        scratch_shapes=[pltpu.VMEM(shape, F32) for shape in scratch],
        compiler_params=pltpu.CompilerParams(vmem_limit_bytes=limit * MIB),
    )(*operands, *later)
    return results if len(results) > 1 else results[0]


def to_neighbours(wings, other=None):
    facets = lax.axis_size("fcol")
    axes, flips = ("fcol", [0]) if other is None else (("frow", "fcol"), [0, 1])

    def pairs(moves):
        if other is None:
            return moves
        return [(f * facets + i, (1 - f) * facets + j) for f in flips for i, j in moves]

    if facets == 2:
        return [lax.ppermute(wings[0], axes, pairs([(0, 1), (1, 0)]))]
    return [
        lax.ppermute(wings[0], axes, pairs([(i, i + 1) for i in range(facets - 1)])),
        lax.ppermute(wings[1], axes, pairs([(i + 1, i) for i in range(facets - 1)])),
    ]


def on_device(dirty_image, density):
    channels, rows, cols = dirty_image.shape
    facets, chans = lax.axis_size("fcol"), lax.axis_size("chan")
    nuclear_limit = math.sqrt(rows * cols)
    sparse_limit = SPARSE_SCALE * math.sqrt(channels * chans)
    table = column_table(cols)
    sides = 1 if facets == 2 else 2
    places, tiles = Places(rows, cols), 2 * NDB + 1
    lane_tiles = cols // LANES + sides

    own, edge, *around = call(
        lambda *refs: edges_kernel(sides, *refs),
        "edges",
        [dirty_image.shape, (channels, HALO, cols)] + [(channels, rows, LANES)] * sides + [(channels, HALO, LANES)] * sides,
        [dirty_image],
    )
    near = pl.pallas_call(
        lambda *refs: load_kernel(sides, *refs),
        name="load",
        out_shape=jax.ShapeDtypeStruct((2, cols + sides * LANES, tiles * LANES), BF16),
        in_specs=[pl.BlockSpec(memory_space=pltpu.HBM)],
        out_specs=vmem(1)[0],
        scratch_shapes=[pltpu.SemaphoreType.DMA((2,))],
        compiler_params=pltpu.CompilerParams(vmem_limit_bytes=16 * MIB),
    )(table)
    beside = to_neighbours(around[:sides])
    above = exchange(edge, "frow", 1)
    corner = to_neighbours(around[sides:], "frow")
    u_inner, inner_keep, inner_send = call(
        inner_kernel,
        "inner",
        [(8 * places.inner, tiles * LANES), (places.border, LANES), (places.border, LANES)],
        [own, *beside, near],
        [(lane_tiles, 8 * (places.inner + 4), LANES), (8 * (places.inner + 4), tiles * LANES)],
        24,
    )
    u_border, keep, send = call(
        lambda *refs: border_kernel(sides, *refs),
        "border",
        [(8 * 4, tiles * LANES), (places.all, LANES), (places.all, LANES)],
        [own, above, inner_keep, inner_send, *beside, *corner, near],
        [(lane_tiles, 8 * 8, LANES), (8 * 8, tiles * LANES)],
        24,
    )
    received = exchange(send, "chan", 1)
    total, again = call(add_and_copy_kernel, "add", [(places.all, LANES), dirty_image.shape], [keep, received, own])
    other = exchange(again, "chan", 1)
    nuclear = call(
        lambda *refs: nuclear_kernel(nuclear_limit, *refs),
        "nuclear",
        [dirty_image.shape],
        [own, other],
        [(2 * channels, rows, cols), (2 * channels, 2 * channels, LANES)],
    )
    bit = 2
    while bit < chans:
        received = exchange(total, "chan", bit)
        total = call(add_kernel, "add", [(places.all, LANES)], [total, received], later=[other if 2 * bit < chans else nuclear])
        bit *= 2
    theirs = exchange(total, "chan", 1)
    step = call(
        lambda *refs: first_kernel(sparse_limit, *refs),
        "first",
        [(2 * cols // LANES, channels * rows, LANES)],
        [own, density, nuclear, u_inner, u_border, total, near],
        [(4 * rows, NDB * LANES), (places.all, LANES)],
        24,
    )
    return call(
        lambda *refs: second_kernel(sparse_limit, *refs),
        "second",
        [dirty_image.shape],
        [own, step, u_inner, u_border, total, theirs, near],
        [(4 * rows, (NDB + 1) * LANES), (cols // LANES, 4 * rows, LANES), (2, places.all, LANES)],
        24,
    )


def solution(mesh):
    return jax.shard_map(
        on_device,
        mesh=mesh,
        in_specs=(P("chan", "frow", "fcol"), P("chan", "frow", "fcol")),
        out_specs=P("chan", "frow", "fcol"),
        check_vma=False,
    )
```

```python
import math

import jax
import jax.numpy as jnp
import numpy as np
from jax import lax
from jax.experimental import pallas as pl
from jax.experimental.pallas import tpu as pltpu
from jax.sharding import PartitionSpec as P

DAUBECHIES = (
    (0.7071067811865476, 0.7071067811865476),
    (0.48296291314469025, 0.836516303737469, 0.22414386804185735, -0.12940952255092145),
    (
        0.3326705529509569,
        0.8068915093133388,
        0.4598775021193313,
        -0.13501102001039084,
        -0.08544127388224149,
        0.035226291882100656,
    ),
    (
        0.23037781330885523,
        0.7148465705525415,
        0.6308807679295904,
        -0.02798376941698385,
        -0.18703481171888114,
        0.030841381835986965,
        0.032883011666982945,
        -0.010597401784997278,
    ),
)
NDB = len(DAUBECHIES)
JACOBI_SWEEPS = 6
STEP_PRIMAL = 0.2
STEP_SPARSE = 0.5
SPARSE_SCALE = 0.5
LANES = 128
STRIP = 32
NEAR = 16
HALO = 8
MIB = 1 << 20
F32 = jnp.float32
BF16 = jnp.bfloat16


def band_taps(family):
    low = DAUBECHIES[family]
    high = [(-1.0) ** k * low[len(low) - 1 - k] for k in range(len(low))]
    return low, high


def phase_taps(family):
    low, high = band_taps(family)
    offset = len(low) // 2 - 1
    table = {}
    for k in range(len(low)):
        s, odd = divmod(k - offset, 2)
        entry = table.setdefault(s, [0.0, 0.0, 0.0, 0.0])
        entry[odd] = low[k]
        entry[2 + odd] = high[k]
    return table


def column_weight(family, band, coefs, pixels):
    taps = band_taps(family)[band]
    k = pixels[:, None] - 2 * coefs[None, :] + len(taps) // 2 - 1
    inside = (k >= 0) & (k < len(taps))
    return np.where(inside, np.asarray(taps)[np.clip(k, 0, len(taps) - 1)], 0.0)


def column_table(cols):
    half = cols // 2
    pixels = np.concatenate([np.arange(cols), np.arange(-NEAR, 0), np.arange(cols, cols + NEAR)])
    pairs = [(f, b) for b in range(2) for f in range(NDB)]
    beyond = np.array([-2, -1, half, half + 1])
    parts = [column_weight(f, b, np.arange(half), pixels) for f, b in pairs] + [column_weight(f, b, beyond, pixels) for f, b in pairs]
    table = np.concatenate(parts, 1)
    table = jnp.asarray(np.pad(table, ((0, 0), (0, LANES - 4 * len(pairs)))), F32)
    top = table.astype(BF16)
    return jnp.stack([top, (table - top.astype(F32)).astype(BF16)], 0)


def halves(values):
    top = values.astype(BF16)
    return top, (values - top.astype(F32)).astype(BF16)


def dot3(left, right, dims=((1,), (0,))):
    def dot(one, two):
        return lax.dot_general(one, two, (dims, ((), ())), preferred_element_type=F32)

    count = left[0].shape[0]
    both = dot(jnp.concatenate(left, 0), right[0])
    return both[:count] + (both[count:] + dot(left[0], right[1]))


def side_by_side(ref, tiles):
    return jnp.concatenate([ref[t] for t in tiles], 1)


def swap_halves(values):
    return pltpu.roll(values, 4, 0)


def sublane_taps(first, second):
    rows = lax.broadcasted_iota(jnp.int32, (8, LANES), 0)
    return jnp.where(rows < 4, F32(first), F32(second))


def strip_taps(pick_first, pick_second, s):
    family = lax.broadcasted_iota(jnp.int32, (8, LANES), 1) // 4 % 4
    total = jnp.zeros((8, LANES), F32)
    for f in range(NDB):
        entry = phase_taps(f).get(s)
        if entry is not None:
            total = jnp.where(family == f, sublane_taps(entry[pick_first], entry[pick_second]), total)
    return total


def row_taps(family, cross, scale):
    table = phase_taps(family)
    return {s: (sublane_taps(e[0] * scale, e[3] * scale), sublane_taps(e[cross[0]] * scale, e[cross[1]] * scale)) for s, e in table.items()}


def strip_row_taps(cross, scale):
    column = lax.broadcasted_iota(jnp.int32, (8, LANES), 1) % 4
    place, facets = lax.axis_index("fcol"), lax.axis_size("fcol")
    kept = jnp.where(column < 2, jnp.where(place > 0, F32(scale), F32(0.0)), jnp.where(place < facets - 1, F32(scale), F32(0.0)))
    return {s: (strip_taps(0, 3, s) * kept, strip_taps(*cross, s) * kept) for s in range(-2, 3)}


def filter_rows(taps, pairs, at):
    direct = crossed = None
    for s, (d, e) in taps.items():
        source = pairs[at(s)]
        direct = d * source if direct is None else direct + d * source
        crossed = e * source if crossed is None else crossed + e * source
    return direct + swap_halves(crossed)


def pack4(items):
    rows = lax.broadcasted_iota(jnp.int32, (8, LANES), 0)

    def merge(a, b, step):
        keep = rows % (2 * step) < step
        return jnp.where(keep, a, pltpu.roll(b, step, 0)) + jnp.where(keep, pltpu.roll(a, 8 - step, 0), b)

    return merge(merge(items[0], items[1], 1), merge(items[2], items[3], 1), 2)


def near_columns(sources, c, at):
    def last(ref):
        return pltpu.roll(ref[c, at, ref.shape[2] - LANES :], NEAR, 1)

    if len(sources) == 1:
        return [jnp.where(lax.axis_index("fcol") == 0, sources[0][c, at, :LANES], last(sources[0]))]
    return [last(sources[0]), sources[1][c, at, :LANES]]


def fill_rows(ext, row, count, start, own, around):
    channels, _, cols = own.shape
    rows = pl.ds(start, count)
    for c in range(channels):
        at = pl.ds(row * channels + c, count, stride=channels)
        for t in range(cols // LANES):
            ext[t, at, :] = jnp.maximum(own[c, rows, t * LANES : (t + 1) * LANES], 0.0)
        for t, value in enumerate(near_columns(around, c, rows)):
            ext[cols // LANES + t, at, :] = jnp.maximum(value, 0.0)


def filter_columns(ext, table, cols, lanes):
    tiles = cols // LANES
    total = dot3(halves(side_by_side(ext, range(tiles))), [table[i, :cols, lanes] for i in range(2)])
    if ext.shape[0] - tiles == 1:
        starts = [pl.multiple_of(cols + (1 - lax.axis_index("fcol")) * NEAR, NEAR)]
    else:
        starts = [cols, cols + NEAR]
    for t, start in enumerate(starts):
        total += dot3(halves(ext[tiles + t][:, :NEAR]), [table[i, pl.ds(start, NEAR), lanes] for i in range(2)])
    return total


def coefficients(coef, first, tiles, u_ref, count):
    squares = []
    for tile in tiles:
        lanes = slice((tile - first) * LANES, (tile - first + 1) * LANES)
        taps = strip_row_taps((2, 1), STEP_SPARSE) if tile == 2 * NDB else row_taps(tile % NDB, (2, 1), STEP_SPARSE)
        pairs = [coef[8 * i : 8 * i + 8, lanes] for i in range(count + 4)]
        for j in range(count):
            value = filter_rows(taps, pairs, lambda s: j + 2 + s)
            u_ref[8 * j : 8 * j + 8, tile * LANES : (tile + 1) * LANES] = value
            squares.append(value * value)
    return squares


def pack_half(squares):
    return [pack4(squares[g : g + 4]) for g in range(0, len(squares), 4)]


def pack_strip(squares, item):
    packed = []
    count = len(squares) // 2
    for half in range(2):
        strip = squares[half * count : (half + 1) * count]
        items = [jnp.zeros((8, LANES), F32)] * item
        for g in range(0, count, 4):
            total = strip[g]
            for k in range(1, len(strip[g : g + 4])):
                total = total + pltpu.roll(strip[g + k], STRIP * k, 1)
            items.append(total)
        items += [jnp.zeros((8, LANES), F32)] * (4 - len(items))
        packed.append(pack4(items))
    return packed


def store_halves(packed, keep, send, base=0):
    y = lax.axis_index("chan") % 2
    for i, (a, b) in enumerate(zip(*packed)):
        keep[base + 8 * i : base + 8 * i + 8, :] = jnp.where(y == 0, a, b)
        send[base + 8 * i : base + 8 * i + 8, :] = jnp.where(y == 0, b, a)


def inner_kernel(own, *refs):
    *around, table, u_ref, keep, send, ext, coef = refs
    channels, rows, cols = own.shape
    x = lax.axis_index("frow")
    edge = jnp.zeros((ext.shape[0], 4 * channels, LANES), F32)
    ext[:, pl.ds(pl.multiple_of(x * rows * channels, 16), 4 * channels), :] = edge
    fill_rows(ext, 4 * (1 - x), rows, 0, own, around)
    coef[...] = filter_columns(ext, table, cols, slice(0, coef.shape[1]))
    count = rows // 2 - 2
    squares = coefficients(coef, 0, range(2 * NDB + 1), u_ref, count)
    strips = pack_strip(squares[2 * NDB * count :], 0)
    packed = []
    for i in range(2):
        packed.append(pack_half(squares[i * NDB * count : (i + 1) * NDB * count]) + [strips[i]])
        for r in range(i * rows // 2, (i + 1) * rows // 2, 8):
            for t in range(cols // LANES):
                total = None
                for c in range(channels):
                    value = STEP_SPARSE * jnp.maximum(own[c, r : r + 8, t * LANES : (t + 1) * LANES], 0.0)
                    total = value * value if total is None else total + value * value
                packed[i].append(total)
    store_halves(packed, keep, send)


def border_kernel(sides, own, above, keep_inner, send_inner, *refs):
    around = refs[:sides]
    table, u_ref, keep, send, ext, coef = refs[sides:]
    channels, rows, cols = own.shape
    x, y = lax.axis_index("frow"), lax.axis_index("chan") % 2
    places = Places(rows, cols)
    fill_rows(ext, HALO * x, HALO, pl.multiple_of((1 - x) * (rows - HALO), HALO), own, around)
    for c in range(channels):
        at = pl.ds(HALO * (1 - x) * channels + c, HALO, stride=channels)
        for t in range(cols // LANES):
            start = (c * (cols // LANES) + t) * HALO
            ext[t, at, :] = jnp.maximum(above[start : start + HALO, :], 0.0)
        for t in range(sides):
            start = (channels * (cols // LANES) + t) * HALO
            corner = jnp.maximum(above[start : start + HALO, :], 0.0)
            ext[cols // LANES + t, at, :] = corner if c == 0 else pltpu.roll(corner, LANES - NEAR * c, 1)
    coef[...] = filter_columns(ext, table, cols, slice(0, coef.shape[1]))
    squares = coefficients(coef, 0, range(2 * NDB + 1), u_ref, 4)
    strips = pack_strip(squares[8 * NDB :], 2)
    store_halves([pack_half(squares[: 4 * NDB]), pack_half(squares[4 * NDB : 8 * NDB])], keep, send, places.border)
    keep[: places.border, :] = keep_inner[...]
    send[: places.border, :] = send_inner[...]
    at = slice(places.strip, places.strip + 8)
    keep[at, :] = keep_inner[at, :] + jnp.where(y == 0, *strips)
    send[at, :] = send_inner[at, :] + jnp.where(y == 0, *strips[::-1])


def pairing_rounds(order):
    players = list(range(order))
    rounds = []
    for _ in range(order - 1):
        rounds.append([(min(a, b), max(a, b)) for a, b in zip(players[: order // 2], players[: order // 2 - 1 : -1])])
        players = [players[0]] + [players[-1]] + players[1:-1]
    return rounds


def down(values):
    for step in (4, 2, 1):
        values = values + pltpu.roll(values, step, 0)
    return values


def nuclear_kernel(limit, own, other, out, group, mix):
    channels, rows, cols = own.shape
    order = 2 * channels
    y = lax.axis_index("chan") % 2
    for c in range(channels):
        group[y * channels + c] = jnp.maximum(own[c], 0.0)
        group[(1 - y) * channels + c] = jnp.maximum(other[c], 0.0)
    blocks = [(slice(r, r + 8), slice(t, t + LANES)) for r in range(0, rows, 8) for t in range(0, cols, LANES)]
    partial = {}
    for at in blocks:
        held = [group[(c, *at)] for c in range(order)]
        for i in range(order):
            for j in range(i + 1):
                term = held[i] * held[j]
                partial[i, j] = partial[i, j] + term if (i, j) in partial else term
    row_sum = {key: jnp.sum(value, axis=0, keepdims=True) for key, value in partial.items()}
    sub = lax.broadcasted_iota(jnp.int32, (order, LANES), 0)
    turned, vectors, diag = [], [], []
    for j in range(order):
        stacked = jnp.concatenate([row_sum[max(i, j), min(i, j)] for i in range(order)], 0)
        column = jnp.broadcast_to(jnp.sum(stacked, axis=1, keepdims=True), (order, LANES))
        turned.append(column)
        unit = jnp.where(sub == j, F32(1.0), F32(0.0))
        vectors.append(unit)
        diag.append(down(column * unit))

    rounds = pairing_rounds(order)

    def sweep(_, state):
        turned, vectors, diag = (list(part) for part in state)
        for pairs in rounds:
            for p, q in pairs:
                coupling = down(vectors[p] * turned[q])
                spread = diag[q] - diag[p]
                square = spread * spread + 4.0 * coupling * coupling
                positive = square > 0.0
                inverse = jnp.where(positive, lax.rsqrt(jnp.where(positive, square, 1.0)), 0.0)
                cosine2 = jnp.where(positive, 0.5 + 0.5 * jnp.abs(spread) * inverse, 1.0)
                other = lax.rsqrt(cosine2)
                c = cosine2 * other
                s = jnp.where(spread >= 0.0, coupling, -coupling) * inverse * other
                shift = s * other * coupling
                diag[p], diag[q] = diag[p] - shift, diag[q] + shift
                turned[p], turned[q] = c * turned[p] - s * turned[q], s * turned[p] + c * turned[q]
                vectors[p], vectors[q] = c * vectors[p] - s * vectors[q], s * vectors[p] + c * vectors[q]
        return tuple(turned), tuple(vectors), tuple(diag)

    turned, vectors, _ = lax.fori_loop(0, JACOBI_SWEEPS, sweep, (tuple(turned), tuple(vectors), tuple(diag)))
    weighted = []
    for j in range(order):
        value = down(vectors[j] * turned[j])
        weighted.append(vectors[j] * (limit / jnp.maximum(jnp.sqrt(jnp.maximum(value, 0.0)), limit)))
    for k in range(order):
        total = None
        for j in range(order):
            term = weighted[j] * jnp.broadcast_to(vectors[j][k : k + 1, :], (order, LANES))
            total = term if total is None else total + term
        mix[k] = total
    for i in range(channels):
        row = [jnp.broadcast_to(mix[k, pl.ds(y * channels + i, 1), :], (order, LANES)) for k in range(order)]
        for at in blocks:
            total = None
            for k in range(order):
                term = row[k] * group[(k, *at)]
                total = term if total is None else total + term
            out[(i, *at)] = total


def scales(limit, norms):
    return limit * lax.rsqrt(jnp.maximum(norms, limit * limit))


def widen(scale, at, item):
    sub = lax.broadcasted_iota(jnp.int32, (8, LANES), 0)
    first = jnp.broadcast_to(scale[at + item : at + item + 1, :], (8, LANES))
    second = jnp.broadcast_to(scale[at + 4 + item : at + 5 + item, :], (8, LANES))
    return jnp.where(sub < 4, first, second)


def spread_rows(inner, border, taps, spread, lanes):
    x = lax.axis_index("frow")
    empty = jnp.zeros((8, LANES), F32)
    count = len(inner)
    upper = [empty, empty, *inner, *border]
    lower = [*border, *inner, empty, empty]
    padded = [jnp.where(x == 0, a, b) for a, b in zip(upper, lower)]
    for i in range(count + 2):
        spread[8 * i : 8 * i + 8, lanes] = filter_rows(taps, padded, lambda s: i + 2 - s)


class Places:
    def __init__(self, rows, cols):
        self.inner = rows // 2 - 2
        self.strip = 2 * NDB * self.inner
        self.dirac = self.strip + 8
        self.border = self.dirac + rows * cols // LANES // 2
        self.all = self.border + 2 * NDB * 4


def half_duals(places, half, scale, u_inner, u_border, spread):
    for family in range(NDB):
        if isinstance(half, int):
            lanes = slice((half * NDB + family) * LANES, (half * NDB + family + 1) * LANES)
        else:
            lanes = pl.ds(pl.multiple_of((half * NDB + family) * LANES, LANES), LANES)
        duals = []
        for ref, base, count in ((u_inner, 0, places.inner), (u_border, places.border, 4)):
            items = [(base + 8 * ((family * count + j) // 4), (family * count + j) % 4) for j in range(count)]
            duals.append([ref[8 * j : 8 * j + 8, lanes] * widen(scale, *items[j]) for j in range(count)])
        spread_rows(*duals, row_taps(family, (1, 2), 1.0), spread, slice(family * LANES, (family + 1) * LANES))


def first_kernel(limit, raw, density, nuclear, u_inner, u_border, mine, table, step, spread, scale):
    channels, rows, cols = raw.shape
    y = lax.axis_index("chan") % 2
    scale[...] = scales(limit, mine[...])
    half_duals(Places(rows, cols), y, scale, u_inner, u_border, spread)
    lanes = pl.ds(pl.multiple_of(y * NDB * LANES, NDB * LANES), NDB * LANES)
    result = dot3(halves(spread[...]), [table[i, :cols, lanes] for i in range(2)], ((1,), (1,)))
    for t in range(cols // LANES):
        step[cols // LANES + t] = result[:, t * LANES : (t + 1) * LANES]
    for c in range(channels):
        for t in range(cols // LANES):
            lanes = slice(t * LANES, (t + 1) * LANES)
            estimate = jnp.maximum(raw[c, :, lanes], 0.0)
            step[t, c * rows : (c + 1) * rows, :] = density[c, :, lanes] * estimate - raw[c, :, lanes] + nuclear[c, :, lanes]


def second_kernel(limit, raw, step, u_inner, u_border, mine, theirs, table, out, spread, image, scale):
    channels, rows, cols = raw.shape
    y = lax.axis_index("chan") % 2
    places = Places(rows, cols)
    scale[y] = scales(limit, mine[...])
    scale[1 - y] = scales(limit, theirs[...])
    half_duals(places, 1 - y, scale.at[1 - y], u_inner, u_border, spread)
    main = 2 * NDB * LANES
    duals = []
    for ref, item, count in ((u_inner, 0, places.inner), (u_border, 2, 4)):
        rolled = []
        for j in range(count):
            half, k = divmod(j, count // 2)
            factor = widen(scale.at[half], places.strip, item + k // 4)
            factor = factor if k % 4 == 0 else pltpu.roll(factor, LANES - STRIP * (k % 4), 1)
            rolled.append(ref[8 * j : 8 * j + 8, main:] * factor)
        duals.append(rolled)
    spread_rows(*duals, strip_row_taps((1, 2), 1.0), spread, slice(NDB * LANES, (NDB + 1) * LANES))
    lanes = pl.ds(pl.multiple_of((1 - y) * NDB * LANES, NDB * LANES), NDB * LANES)
    left = halves(spread[...])
    right = [jnp.concatenate([table[i, :cols, lanes], table[i, :cols, main:]], 1) for i in range(2)]
    result = dot3(left, right, ((1,), (1,)))
    for t in range(cols // LANES):
        image[t] = result[:, t * LANES : (t + 1) * LANES] + step[cols // LANES + t]
    for c in range(channels):
        for r in range(0, rows, 8):
            for t in range(cols // LANES):
                lanes = slice(t * LANES, (t + 1) * LANES)
                half, inside = divmod(r, rows // 2)
                at = places.dirac + 8 * (inside // 8 * (cols // LANES) + t)
                estimate = jnp.maximum(raw[c, r : r + 8, lanes], 0.0)
                dual = STEP_SPARSE * estimate * scale[half, at : at + 8, :]
                synthesis = dual + image[t, pl.ds(r * channels + c, 8, stride=channels), :]
                total = step[t, c * rows + r : c * rows + r + 8, :] + synthesis
                out[c, r : r + 8, lanes] = jnp.maximum(estimate - STEP_PRIMAL * total, 0.0)


def hold_kernel(dirty, own):
    own[...] = dirty[...]


def rows_kernel(own, *refs):
    *around, edge = refs
    channels, rows, cols = own.shape
    start = pl.ds(pl.multiple_of((1 - lax.axis_index("frow")) * (rows - HALO), HALO), HALO)
    at = 0
    for c in range(channels):
        for t in range(cols // LANES):
            edge[at : at + HALO, :] = own[c, start, t * LANES : (t + 1) * LANES]
            at += HALO
    lane = lax.broadcasted_iota(jnp.int32, (HALO, LANES), 1) // NEAR
    totals = near_columns(around, 0, start)
    for c in range(1, channels):
        parts = near_columns(around, c, start)
        totals = [jnp.where(lane == c, pltpu.roll(part, NEAR * c, 1), total) for part, total in zip(parts, totals)]
    for total in totals:
        edge[at : at + HALO, :] = total
        at += HALO


def add_kernel(one, two, *refs):
    refs[-1][...] = one[...] + two[...]


def exchange(values, axis, bit):
    count = lax.axis_size(axis)
    return lax.ppermute(values, axis, [(i, i ^ bit) for i in range(count)])


def vmem(count):
    return [pl.BlockSpec(memory_space=pltpu.VMEM)] * count


def call(kernel, name, shapes, operands, scratch=(), limit=16, later=()):
    many = [jax.ShapeDtypeStruct(shape, F32) if isinstance(shape, tuple) else shape for shape in shapes]
    results = pl.pallas_call(
        kernel,
        name=name,
        out_shape=many,
        in_specs=vmem(len(operands)) + [pl.BlockSpec(memory_space=pl.ANY)] * len(later),
        out_specs=vmem(len(many)),
        scratch_shapes=[pltpu.VMEM(shape, F32) for shape in scratch],
        compiler_params=pltpu.CompilerParams(vmem_limit_bytes=limit * MIB),
    )(*operands, *later)
    return results if len(results) > 1 else results[0]


def from_neighbours(values):
    facets = lax.axis_size("fcol")
    if facets == 2:
        return [exchange(values, "fcol", 1)]
    return [
        lax.ppermute(values, "fcol", [(i, i + 1) for i in range(facets - 1)]),
        lax.ppermute(values, "fcol", [(i + 1, i) for i in range(facets - 1)]),
    ]


def on_device(dirty_image, density):
    channels, rows, cols = dirty_image.shape
    facets, chans = lax.axis_size("fcol"), lax.axis_size("chan")
    nuclear_limit = math.sqrt(rows * cols)
    sparse_limit = SPARSE_SCALE * math.sqrt(channels * chans)
    table = column_table(cols)
    sides = 1 if facets == 2 else 2
    places, tiles = Places(rows, cols), 2 * NDB + 1
    lane_tiles = cols // LANES + sides

    around = from_neighbours(dirty_image)
    own = call(hold_kernel, "hold", [dirty_image.shape], [dirty_image])
    edge = call(rows_kernel, "rows", [((channels * (cols // LANES) + sides) * HALO, LANES)], [own, *around])
    above = exchange(edge, "frow", 1)
    u_inner, keep, send = call(
        inner_kernel,
        "inner",
        [(8 * places.inner, tiles * LANES), (places.border, LANES), (places.border, LANES)],
        [own, *around, table],
        [(lane_tiles, 8 * (places.inner + 4), LANES), (8 * (places.inner + 4), tiles * LANES)],
        24,
    )
    u_border, keep, send = call(
        lambda *refs: border_kernel(sides, *refs),
        "border",
        [(8 * 4, tiles * LANES), (places.all, LANES), (places.all, LANES)],
        [own, above, keep, send, *around, table],
        [(lane_tiles, 8 * 8, LANES), (8 * 8, tiles * LANES)],
        24,
    )
    received = exchange(send, "chan", 1)
    total = call(add_kernel, "add", [(places.all, LANES)], [keep, received])
    other = exchange(own, "chan", 1)
    nuclear = call(
        lambda *refs: nuclear_kernel(nuclear_limit, *refs),
        "nuclear",
        [dirty_image.shape],
        [own, other],
        [(2 * channels, rows, cols), (2 * channels, 2 * channels, LANES)],
    )
    bit = 2
    while bit < chans:
        received = exchange(total, "chan", bit)
        total = call(add_kernel, "add", [(places.all, LANES)], [total, received], later=[] if 2 * bit < chans else [nuclear])
        bit *= 2
    theirs = exchange(total, "chan", 1)
    step = call(
        lambda *refs: first_kernel(sparse_limit, *refs),
        "first",
        [(2 * cols // LANES, channels * rows, LANES)],
        [own, density, nuclear, u_inner, u_border, total, table],
        [(4 * rows, NDB * LANES), (places.all, LANES)],
        24,
    )
    return call(
        lambda *refs: second_kernel(sparse_limit, *refs),
        "second",
        [dirty_image.shape],
        [own, step, u_inner, u_border, total, theirs, table],
        [(4 * rows, (NDB + 1) * LANES), (cols // LANES, 4 * rows, LANES), (2, places.all, LANES)],
        24,
    )


def solution(mesh):
    return jax.shard_map(
        on_device,
        mesh=mesh,
        in_specs=(P("chan", "frow", "fcol"), P("chan", "frow", "fcol")),
        out_specs=P("chan", "frow", "fcol"),
        check_vma=False,
    )
```

```python
import math

import jax
import jax.numpy as jnp
from jax import lax
from jax.experimental import pallas as pl
from jax.experimental.pallas import tpu as pltpu
from jax.sharding import PartitionSpec as P

DAUBECHIES = (
    (0.7071067811865476, 0.7071067811865476),
    (0.48296291314469025, 0.836516303737469, 0.22414386804185735, -0.12940952255092145),
    (
        0.3326705529509569,
        0.8068915093133388,
        0.4598775021193313,
        -0.13501102001039084,
        -0.08544127388224149,
        0.035226291882100656,
    ),
    (
        0.23037781330885523,
        0.7148465705525415,
        0.6308807679295904,
        -0.02798376941698385,
        -0.18703481171888114,
        0.030841381835986965,
        0.032883011666982945,
        -0.010597401784997278,
    ),
)
NDB = len(DAUBECHIES)
JACOBI_SWEEPS = 6
STEP_PRIMAL = 0.2
STEP_SPARSE = 0.5
SPARSE_SCALE = 0.5
LANES = 128
STRIP = 32
NEAR = 16
HALO = 8
MIB = 1 << 20
F32 = jnp.float32
BF16 = jnp.bfloat16


def band_taps(family):
    low = DAUBECHIES[family]
    high = [(-1.0) ** k * low[len(low) - 1 - k] for k in range(len(low))]
    return low, high


def phase_taps(family):
    low, high = band_taps(family)
    offset = len(low) // 2 - 1
    table = {}
    for k in range(len(low)):
        s, odd = divmod(k - offset, 2)
        entry = table.setdefault(s, [0.0, 0.0, 0.0, 0.0])
        entry[odd] = low[k]
        entry[2 + odd] = high[k]
    return table


def halves(values):
    top = values.astype(BF16)
    return top, (values - top.astype(F32)).astype(BF16)


def dot3(left, right, dims=((1,), (0,))):
    def dot(one, two):
        return lax.dot_general(one, two, (dims, ((), ())), preferred_element_type=F32)

    count = left[0].shape[0]
    both = dot(jnp.concatenate(left, 0), right[0])
    return both[:count] + (both[count:] + dot(left[0], right[1]))


def side_by_side(ref, tiles):
    return jnp.concatenate([ref[t] for t in tiles], 1)


def swap_halves(values):
    return pltpu.roll(values, 4, 0)


def sublane_taps(first, second):
    rows = lax.broadcasted_iota(jnp.int32, (8, LANES), 0)
    return jnp.where(rows < 4, F32(first), F32(second))


def strip_taps(pick_first, pick_second, s):
    family = lax.broadcasted_iota(jnp.int32, (8, LANES), 1) // 4 % 4
    total = jnp.zeros((8, LANES), F32)
    for f in range(NDB):
        entry = phase_taps(f).get(s)
        if entry is not None:
            total = jnp.where(family == f, sublane_taps(entry[pick_first], entry[pick_second]), total)
    return total


def row_taps(family, cross, scale):
    table = phase_taps(family)
    return {s: (sublane_taps(e[0] * scale, e[3] * scale), sublane_taps(e[cross[0]] * scale, e[cross[1]] * scale)) for s, e in table.items()}


def strip_row_taps(cross, scale):
    column = lax.broadcasted_iota(jnp.int32, (8, LANES), 1) % 4
    place, facets = lax.axis_index("fcol"), lax.axis_size("fcol")
    kept = jnp.where(column < 2, jnp.where(place > 0, F32(scale), F32(0.0)), jnp.where(place < facets - 1, F32(scale), F32(0.0)))
    return {s: (strip_taps(0, 3, s) * kept, strip_taps(*cross, s) * kept) for s in range(-2, 3)}


def filter_rows(taps, pairs, at):
    direct = crossed = None
    for s, (d, e) in taps.items():
        source = pairs[at(s)]
        direct = d * source if direct is None else direct + d * source
        crossed = e * source if crossed is None else crossed + e * source
    return direct + swap_halves(crossed)


def pack4(items):
    rows = lax.broadcasted_iota(jnp.int32, (8, LANES), 0)

    def merge(a, b, step):
        keep = rows % (2 * step) < step
        return jnp.where(keep, a, pltpu.roll(b, step, 0)) + jnp.where(keep, pltpu.roll(a, 8 - step, 0), b)

    return merge(merge(items[0], items[1], 1), merge(items[2], items[3], 1), 2)


def near_columns(sources, c, at):
    def last(ref):
        return pltpu.roll(ref[c, at, ref.shape[2] - LANES :], NEAR, 1)

    if len(sources) == 1:
        return [jnp.where(lax.axis_index("fcol") == 0, sources[0][c, at, :LANES], last(sources[0]))]
    return [last(sources[0]), sources[1][c, at, :LANES]]


def fill_rows(ext, row, count, start, own, around):
    channels, _, cols = own.shape
    rows = pl.ds(start, count)
    for c in range(channels):
        at = pl.ds(row * channels + c, count, stride=channels)
        for t in range(cols // LANES):
            ext[t, at, :] = jnp.maximum(own[c, rows, t * LANES : (t + 1) * LANES], 0.0)
        for t, value in enumerate(near_columns(around, c, rows)):
            ext[cols // LANES + t, at, :] = jnp.maximum(value, 0.0)


def filter_columns(ext, table, cols, lanes):
    tiles = cols // LANES
    total = dot3(halves(side_by_side(ext, range(tiles))), [table[i, :cols, lanes] for i in range(2)])
    if ext.shape[0] - tiles == 1:
        starts = [pl.multiple_of(cols + (1 - lax.axis_index("fcol")) * NEAR, NEAR)]
    else:
        starts = [cols, cols + NEAR]
    for t, start in enumerate(starts):
        total += dot3(halves(ext[tiles + t][:, :NEAR]), [table[i, pl.ds(start, NEAR), lanes] for i in range(2)])
    return total


def coefficients(coef, first, tiles, u_ref, count):
    squares = []
    for tile in tiles:
        lanes = slice((tile - first) * LANES, (tile - first + 1) * LANES)
        taps = strip_row_taps((2, 1), STEP_SPARSE) if tile == 2 * NDB else row_taps(tile % NDB, (2, 1), STEP_SPARSE)
        pairs = [coef[8 * i : 8 * i + 8, lanes] for i in range(count + 4)]
        for j in range(count):
            value = filter_rows(taps, pairs, lambda s: j + 2 + s)
            u_ref[8 * j : 8 * j + 8, tile * LANES : (tile + 1) * LANES] = value
            squares.append(value * value)
    return squares


def pack_half(squares):
    return [pack4(squares[g : g + 4]) for g in range(0, len(squares), 4)]


def pack_strip(squares, item):
    packed = []
    count = len(squares) // 2
    for half in range(2):
        strip = squares[half * count : (half + 1) * count]
        items = [jnp.zeros((8, LANES), F32)] * item
        for g in range(0, count, 4):
            total = strip[g]
            for k in range(1, len(strip[g : g + 4])):
                total = total + pltpu.roll(strip[g + k], STRIP * k, 1)
            items.append(total)
        items += [jnp.zeros((8, LANES), F32)] * (4 - len(items))
        packed.append(pack4(items))
    return packed


def store_halves(packed, keep, send, base=0):
    y = lax.axis_index("chan") % 2
    for i, (a, b) in enumerate(zip(*packed)):
        keep[base + 8 * i : base + 8 * i + 8, :] = jnp.where(y == 0, a, b)
        send[base + 8 * i : base + 8 * i + 8, :] = jnp.where(y == 0, b, a)


def inner_kernel(own, *refs):
    *around, table, u_ref, keep, send, keep_more, send_more, ext, coef = refs
    channels, rows, cols = own.shape
    x = lax.axis_index("frow")
    edge = jnp.zeros((ext.shape[0], 4 * channels, LANES), F32)
    ext[:, pl.ds(pl.multiple_of(x * rows * channels, 16), 4 * channels), :] = edge
    fill_rows(ext, 4 * (1 - x), rows, 0, own, around)
    coef[...] = filter_columns(ext, table, cols, slice(0, coef.shape[1]))
    count = rows // 2 - 2
    squares = coefficients(coef, 0, range(2 * NDB + 1), u_ref, count)
    store_halves([pack_half(squares[i * NDB * count : (i + 1) * NDB * count]) for i in range(2)], keep, send)
    packed = [[strip] for strip in pack_strip(squares[2 * NDB * count :], 0)]
    for i in range(2):
        for r in range(i * rows // 2, (i + 1) * rows // 2, 8):
            for t in range(cols // LANES):
                total = None
                for c in range(channels):
                    value = STEP_SPARSE * jnp.maximum(own[c, r : r + 8, t * LANES : (t + 1) * LANES], 0.0)
                    total = value * value if total is None else total + value * value
                packed[i].append(total)
    store_halves(packed, keep_more, send_more)


def border_kernel(sides, own, above, keep_more, send_more, *refs):
    around = refs[:sides]
    table, u_ref, keep, send, ext, coef = refs[sides:]
    channels, rows, cols = own.shape
    x, y = lax.axis_index("frow"), lax.axis_index("chan") % 2
    places = Places(rows, cols)
    fill_rows(ext, HALO * x, HALO, pl.multiple_of((1 - x) * (rows - HALO), HALO), own, around)
    for c in range(channels):
        at = pl.ds(HALO * (1 - x) * channels + c, HALO, stride=channels)
        for t in range(cols // LANES):
            start = (c * (cols // LANES) + t) * HALO
            ext[t, at, :] = jnp.maximum(above[start : start + HALO, :], 0.0)
        for t in range(sides):
            start = (channels * (cols // LANES) + t) * HALO
            corner = jnp.maximum(above[start : start + HALO, :], 0.0)
            ext[cols // LANES + t, at, :] = corner if c == 0 else pltpu.roll(corner, LANES - NEAR * c, 1)
    coef[...] = filter_columns(ext, table, cols, slice(0, coef.shape[1]))
    squares = coefficients(coef, 0, range(2 * NDB + 1), u_ref, 4)
    strips = pack_strip(squares[8 * NDB :], 2)
    store_halves([pack_half(squares[: 4 * NDB]), pack_half(squares[4 * NDB : 8 * NDB])], keep, send, places.border - places.strip)
    keep[: places.border - places.strip, :] = keep_more[...]
    send[: places.border - places.strip, :] = send_more[...]
    keep[:8, :] = keep_more[:8, :] + jnp.where(y == 0, *strips)
    send[:8, :] = send_more[:8, :] + jnp.where(y == 0, *strips[::-1])


def pairing_rounds(order):
    players = list(range(order))
    rounds = []
    for _ in range(order - 1):
        rounds.append([(min(a, b), max(a, b)) for a, b in zip(players[: order // 2], players[: order // 2 - 1 : -1])])
        players = [players[0]] + [players[-1]] + players[1:-1]
    return rounds


def down(values):
    for step in (4, 2, 1):
        values = values + pltpu.roll(values, step, 0)
    return values


def nuclear_kernel(limit, own, other, out, group, mix):
    channels, rows, cols = own.shape
    order = 2 * channels
    y = lax.axis_index("chan") % 2
    for c in range(channels):
        group[y * channels + c] = jnp.maximum(own[c], 0.0)
        group[(1 - y) * channels + c] = jnp.maximum(other[c], 0.0)
    blocks = [(slice(r, r + 8), slice(t, t + LANES)) for r in range(0, rows, 8) for t in range(0, cols, LANES)]
    partial = {}
    for at in blocks:
        held = [group[(c, *at)] for c in range(order)]
        for i in range(order):
            for j in range(i + 1):
                term = held[i] * held[j]
                partial[i, j] = partial[i, j] + term if (i, j) in partial else term
    row_sum = {key: jnp.sum(value, axis=0, keepdims=True) for key, value in partial.items()}
    sub = lax.broadcasted_iota(jnp.int32, (order, LANES), 0)
    turned, vectors, diag = [], [], []
    for j in range(order):
        stacked = jnp.concatenate([row_sum[max(i, j), min(i, j)] for i in range(order)], 0)
        column = jnp.broadcast_to(jnp.sum(stacked, axis=1, keepdims=True), (order, LANES))
        turned.append(column)
        unit = jnp.where(sub == j, F32(1.0), F32(0.0))
        vectors.append(unit)
        diag.append(down(column * unit))

    rounds = pairing_rounds(order)

    def sweep(_, state):
        turned, vectors, diag = (list(part) for part in state)
        for pairs in rounds:
            for p, q in pairs:
                coupling = down(vectors[p] * turned[q])
                spread = diag[q] - diag[p]
                square = spread * spread + 4.0 * coupling * coupling
                positive = square > 0.0
                inverse = jnp.where(positive, lax.rsqrt(jnp.where(positive, square, 1.0)), 0.0)
                cosine2 = jnp.where(positive, 0.5 + 0.5 * jnp.abs(spread) * inverse, 1.0)
                other = lax.rsqrt(cosine2)
                c = cosine2 * other
                s = jnp.where(spread >= 0.0, coupling, -coupling) * inverse * other
                shift = s * other * coupling
                diag[p], diag[q] = diag[p] - shift, diag[q] + shift
                turned[p], turned[q] = c * turned[p] - s * turned[q], s * turned[p] + c * turned[q]
                vectors[p], vectors[q] = c * vectors[p] - s * vectors[q], s * vectors[p] + c * vectors[q]
        return tuple(turned), tuple(vectors), tuple(diag)

    turned, vectors, _ = lax.fori_loop(0, JACOBI_SWEEPS, sweep, (tuple(turned), tuple(vectors), tuple(diag)))
    weighted = []
    for j in range(order):
        value = down(vectors[j] * turned[j])
        weighted.append(vectors[j] * (limit / jnp.maximum(jnp.sqrt(jnp.maximum(value, 0.0)), limit)))
    for k in range(order):
        total = None
        for j in range(order):
            term = weighted[j] * jnp.broadcast_to(vectors[j][k : k + 1, :], (order, LANES))
            total = term if total is None else total + term
        mix[k] = total
    for i in range(channels):
        row = [jnp.broadcast_to(mix[k, pl.ds(y * channels + i, 1), :], (order, LANES)) for k in range(order)]
        for at in blocks:
            total = None
            for k in range(order):
                term = row[k] * group[(k, *at)]
                total = term if total is None else total + term
            out[(i, *at)] = total


def scales(limit, norms):
    return limit * lax.rsqrt(jnp.maximum(norms, limit * limit))


def widen(scale, at, item):
    sub = lax.broadcasted_iota(jnp.int32, (8, LANES), 0)
    first = jnp.broadcast_to(scale[at + item : at + item + 1, :], (8, LANES))
    second = jnp.broadcast_to(scale[at + 4 + item : at + 5 + item, :], (8, LANES))
    return jnp.where(sub < 4, first, second)


def spread_rows(inner, border, taps, spread, lanes):
    x = lax.axis_index("frow")
    empty = jnp.zeros((8, LANES), F32)
    count = len(inner)
    upper = [empty, empty, *inner, *border]
    lower = [*border, *inner, empty, empty]
    padded = [jnp.where(x == 0, a, b) for a, b in zip(upper, lower)]
    for i in range(count + 2):
        spread[8 * i : 8 * i + 8, lanes] = filter_rows(taps, padded, lambda s: i + 2 - s)


class Places:
    def __init__(self, rows, cols):
        self.inner = rows // 2 - 2
        self.strip = 2 * NDB * self.inner
        self.dirac = self.strip + 8
        self.border = self.dirac + rows * cols // LANES // 2
        self.all = self.border + 2 * NDB * 4


def half_duals(places, half, scale, u_inner, u_border, spread):
    for family in range(NDB):
        if isinstance(half, int):
            lanes = slice((half * NDB + family) * LANES, (half * NDB + family + 1) * LANES)
        else:
            lanes = pl.ds(pl.multiple_of((half * NDB + family) * LANES, LANES), LANES)
        duals = []
        for ref, base, count in ((u_inner, 0, places.inner), (u_border, places.border, 4)):
            items = [(base + 8 * ((family * count + j) // 4), (family * count + j) % 4) for j in range(count)]
            duals.append([ref[8 * j : 8 * j + 8, lanes] * widen(scale, *items[j]) for j in range(count)])
        spread_rows(*duals, row_taps(family, (1, 2), 1.0), spread, slice(family * LANES, (family + 1) * LANES))


def first_kernel(limit, raw, density, nuclear, u_inner, u_border, mine, table, step, spread, scale):
    channels, rows, cols = raw.shape
    y = lax.axis_index("chan") % 2
    scale[...] = scales(limit, mine[...])
    half_duals(Places(rows, cols), y, scale, u_inner, u_border, spread)
    lanes = pl.ds(pl.multiple_of(y * NDB * LANES, NDB * LANES), NDB * LANES)
    result = dot3(halves(spread[...]), [table[i, :cols, lanes] for i in range(2)], ((1,), (1,)))
    for t in range(cols // LANES):
        step[cols // LANES + t] = result[:, t * LANES : (t + 1) * LANES]
    for c in range(channels):
        for t in range(cols // LANES):
            lanes = slice(t * LANES, (t + 1) * LANES)
            estimate = jnp.maximum(raw[c, :, lanes], 0.0)
            step[t, c * rows : (c + 1) * rows, :] = density[c, :, lanes] * estimate - raw[c, :, lanes] + nuclear[c, :, lanes]


def second_kernel(limit, raw, step, u_inner, u_border, mine, theirs, table, out, spread, image, scale):
    channels, rows, cols = raw.shape
    y = lax.axis_index("chan") % 2
    places = Places(rows, cols)
    scale[y] = scales(limit, mine[...])
    scale[1 - y] = scales(limit, theirs[...])
    half_duals(places, 1 - y, scale.at[1 - y], u_inner, u_border, spread)
    main = 2 * NDB * LANES
    duals = []
    for ref, item, count in ((u_inner, 0, places.inner), (u_border, 2, 4)):
        rolled = []
        for j in range(count):
            half, k = divmod(j, count // 2)
            factor = widen(scale.at[half], places.strip, item + k // 4)
            factor = factor if k % 4 == 0 else pltpu.roll(factor, LANES - STRIP * (k % 4), 1)
            rolled.append(ref[8 * j : 8 * j + 8, main:] * factor)
        duals.append(rolled)
    spread_rows(*duals, strip_row_taps((1, 2), 1.0), spread, slice(NDB * LANES, (NDB + 1) * LANES))
    lanes = pl.ds(pl.multiple_of((1 - y) * NDB * LANES, NDB * LANES), NDB * LANES)
    left = halves(spread[...])
    right = [jnp.concatenate([table[i, :cols, lanes], table[i, :cols, main:]], 1) for i in range(2)]
    result = dot3(left, right, ((1,), (1,)))
    for t in range(cols // LANES):
        image[t] = result[:, t * LANES : (t + 1) * LANES] + step[cols // LANES + t]
    for c in range(channels):
        for r in range(0, rows, 8):
            for t in range(cols // LANES):
                lanes = slice(t * LANES, (t + 1) * LANES)
                half, inside = divmod(r, rows // 2)
                at = places.dirac + 8 * (inside // 8 * (cols // LANES) + t)
                estimate = jnp.maximum(raw[c, r : r + 8, lanes], 0.0)
                dual = STEP_SPARSE * estimate * scale[half, at : at + 8, :]
                synthesis = dual + image[t, pl.ds(r * channels + c, 8, stride=channels), :]
                total = step[t, c * rows + r : c * rows + r + 8, :] + synthesis
                out[c, r : r + 8, lanes] = jnp.maximum(estimate - STEP_PRIMAL * total, 0.0)


def fixed_taps(family, band, index):
    total = jnp.zeros(index.shape, F32)
    for k, tap in enumerate(band_taps(family)[band]):
        total = jnp.where(index == k, F32(tap), total)
    return total


def hold_kernel(dirty, own, table):
    own[...] = dirty[...]
    cols = dirty.shape[2]
    blocks = cols // NEAR
    rows = {block: block * NEAR for block in range(blocks)} | {-1: cols, blocks: cols + NEAR}
    row = lax.broadcasted_iota(jnp.int32, (NEAR, LANES), 0)
    lane = lax.broadcasted_iota(jnp.int32, (NEAR, LANES), 1)

    def put(block, tile, value):
        at, lanes = slice(rows[block], rows[block] + NEAR), slice(tile * LANES, (tile + 1) * LANES)
        top = value.astype(BF16)
        table[0, at, lanes] = top
        table[1, at, lanes] = (value - top.astype(F32)).astype(BF16)

    pairs = [(f, b) for b in range(2) for f in range(NDB)]
    for tile, (f, b) in enumerate(pairs):
        base = fixed_taps(f, b, row - 2 * (lane - 2) + len(DAUBECHIES[f]) // 2 - 1)
        for block in rows:
            value = pltpu.roll(base, (block * NEAR // 2 - 2) % LANES, 1)
            if block <= 0:
                value = jnp.where(lane < LANES // 2, value, 0.0)
            if block >= blocks - 1:
                value = jnp.where(lane < LANES // 2, 0.0, value)
            put(block, tile, value)
    column = lane % 4
    position = jnp.where(column < 2, column - 2, column + cols // 2 - 2)
    for block in rows:
        value = jnp.zeros((NEAR, LANES), F32)
        if block in (-1, 0, blocks - 1, blocks):
            for tile, (f, b) in enumerate(pairs):
                part = fixed_taps(f, b, row + block * NEAR - 2 * position + len(DAUBECHIES[f]) // 2 - 1)
                value = jnp.where(lane // 4 == tile, part, value)
        put(block, len(pairs), value)


def rows_kernel(own, *refs):
    *around, edge = refs
    channels, rows, cols = own.shape
    start = pl.ds(pl.multiple_of((1 - lax.axis_index("frow")) * (rows - HALO), HALO), HALO)
    at = 0
    for c in range(channels):
        for t in range(cols // LANES):
            edge[at : at + HALO, :] = own[c, start, t * LANES : (t + 1) * LANES]
            at += HALO
    lane = lax.broadcasted_iota(jnp.int32, (HALO, LANES), 1) // NEAR
    totals = near_columns(around, 0, start)
    for c in range(1, channels):
        parts = near_columns(around, c, start)
        totals = [jnp.where(lane == c, pltpu.roll(part, NEAR * c, 1), total) for part, total in zip(parts, totals)]
    for total in totals:
        edge[at : at + HALO, :] = total
        at += HALO


def add_kernel(one, two, *refs):
    refs[-1][...] = one[...] + two[...]


def add_parts_kernel(one, two, three, four, out):
    count = one.shape[0]
    out[:count, :] = one[...] + two[...]
    out[count:, :] = three[...] + four[...]


def exchange(values, axis, bit):
    count = lax.axis_size(axis)
    return lax.ppermute(values, axis, [(i, i ^ bit) for i in range(count)])


def vmem(count):
    return [pl.BlockSpec(memory_space=pltpu.VMEM)] * count


def call(kernel, name, shapes, operands, scratch=(), limit=16, later=()):
    many = [jax.ShapeDtypeStruct(shape, F32) if isinstance(shape, tuple) else shape for shape in shapes]
    results = pl.pallas_call(
        kernel,
        name=name,
        out_shape=many,
        in_specs=vmem(len(operands)) + [pl.BlockSpec(memory_space=pl.ANY)] * len(later),
        out_specs=vmem(len(many)),
        scratch_shapes=[pltpu.VMEM(shape, F32) for shape in scratch],
        compiler_params=pltpu.CompilerParams(vmem_limit_bytes=limit * MIB),
    )(*operands, *later)
    return results if len(results) > 1 else results[0]


def from_neighbours(values):
    facets = lax.axis_size("fcol")
    if facets == 2:
        return [exchange(values, "fcol", 1)]
    return [
        lax.ppermute(values, "fcol", [(i, i + 1) for i in range(facets - 1)]),
        lax.ppermute(values, "fcol", [(i + 1, i) for i in range(facets - 1)]),
    ]


def on_device(dirty_image, density):
    channels, rows, cols = dirty_image.shape
    facets, chans = lax.axis_size("fcol"), lax.axis_size("chan")
    nuclear_limit = math.sqrt(rows * cols)
    sparse_limit = SPARSE_SCALE * math.sqrt(channels * chans)
    sides = 1 if facets == 2 else 2
    places, tiles = Places(rows, cols), 2 * NDB + 1
    lane_tiles = cols // LANES + sides

    around = from_neighbours(dirty_image)
    near = jax.ShapeDtypeStruct((2, cols + 2 * NEAR, tiles * LANES), BF16)
    own, near = call(hold_kernel, "hold", [dirty_image.shape, near], [dirty_image])
    edge = call(rows_kernel, "rows", [((channels * (cols // LANES) + sides) * HALO, LANES)], [own, *around])
    above = exchange(edge, "frow", 1)
    main, more = (places.strip, LANES), (places.border - places.strip, LANES)
    u_inner, keep, send, keep_more, send_more = call(
        inner_kernel,
        "inner",
        [(8 * places.inner, tiles * LANES), main, main, more, more],
        [own, *around, near],
        [(lane_tiles, 8 * (places.inner + 4), LANES), (8 * (places.inner + 4), tiles * LANES)],
        24,
    )
    received = exchange(send, "chan", 1)
    u_border, keep_more, send_more = call(
        lambda *refs: border_kernel(sides, *refs),
        "border",
        [(8 * 4, tiles * LANES)] + [(places.all - places.strip, LANES)] * 2,
        [own, above, keep_more, send_more, *around, near],
        [(lane_tiles, 8 * 8, LANES), (8 * 8, tiles * LANES)],
        24,
    )
    received_more = exchange(send_more, "chan", 1)
    total = call(add_parts_kernel, "add", [(places.all, LANES)], [keep, received, keep_more, received_more])
    other = exchange(own, "chan", 1)
    nuclear = call(
        lambda *refs: nuclear_kernel(nuclear_limit, *refs),
        "nuclear",
        [dirty_image.shape],
        [own, other],
        [(2 * channels, rows, cols), (2 * channels, 2 * channels, LANES)],
    )
    bit = 2
    while bit < chans:
        received = exchange(total, "chan", bit)
        total = call(add_kernel, "add", [(places.all, LANES)], [total, received], later=[] if 2 * bit < chans else [nuclear])
        bit *= 2
    theirs = exchange(total, "chan", 1)
    step = call(
        lambda *refs: first_kernel(sparse_limit, *refs),
        "first",
        [(2 * cols // LANES, channels * rows, LANES)],
        [own, density, nuclear, u_inner, u_border, total, near],
        [(4 * rows, NDB * LANES), (places.all, LANES)],
        24,
    )
    return call(
        lambda *refs: second_kernel(sparse_limit, *refs),
        "second",
        [dirty_image.shape],
        [own, step, u_inner, u_border, total, theirs, near],
        [(4 * rows, (NDB + 1) * LANES), (cols // LANES, 4 * rows, LANES), (2, places.all, LANES)],
        24,
    )


def solution(mesh):
    return jax.shard_map(
        on_device,
        mesh=mesh,
        in_specs=(P("chan", "frow", "fcol"), P("chan", "frow", "fcol")),
        out_specs=P("chan", "frow", "fcol"),
        check_vma=False,
    )
```

```python
import math

import jax
import jax.numpy as jnp
from jax import lax
from jax.experimental import pallas as pl
from jax.experimental.pallas import tpu as pltpu
from jax.sharding import PartitionSpec as P

DAUBECHIES = (
    (0.7071067811865476, 0.7071067811865476),
    (0.48296291314469025, 0.836516303737469, 0.22414386804185735, -0.12940952255092145),
    (
        0.3326705529509569,
        0.8068915093133388,
        0.4598775021193313,
        -0.13501102001039084,
        -0.08544127388224149,
        0.035226291882100656,
    ),
    (
        0.23037781330885523,
        0.7148465705525415,
        0.6308807679295904,
        -0.02798376941698385,
        -0.18703481171888114,
        0.030841381835986965,
        0.032883011666982945,
        -0.010597401784997278,
    ),
)
NDB = len(DAUBECHIES)
JACOBI_SWEEPS = 6
STEP_PRIMAL = 0.2
STEP_SPARSE = 0.5
SPARSE_SCALE = 0.5
LANES = 128
BORDER_ROWS = [2 + len(taps) // 4 for taps in DAUBECHIES]
STRIP = 32
NEAR = 16
HALO = 8
MIB = 1 << 20
F32 = jnp.float32
BF16 = jnp.bfloat16


def band_taps(family):
    low = DAUBECHIES[family]
    high = [(-1.0) ** k * low[len(low) - 1 - k] for k in range(len(low))]
    return low, high


def phase_taps(family):
    low, high = band_taps(family)
    offset = len(low) // 2 - 1
    table = {}
    for k in range(len(low)):
        s, odd = divmod(k - offset, 2)
        entry = table.setdefault(s, [0.0, 0.0, 0.0, 0.0])
        entry[odd] = low[k]
        entry[2 + odd] = high[k]
    return table


def halves(values):
    top = values.astype(BF16)
    return top, (values - top.astype(F32)).astype(BF16)


def dot3(left, right, dims=((1,), (0,))):
    def dot(one, two):
        return lax.dot_general(one, two, (dims, ((), ())), preferred_element_type=F32)

    count = left[0].shape[0]
    both = dot(jnp.concatenate(left, 0), right[0])
    return both[:count] + (both[count:] + dot(left[0], right[1]))


def side_by_side(ref, tiles):
    return jnp.concatenate([ref[t] for t in tiles], 1)


def swap_halves(values):
    return pltpu.roll(values, 4, 0)


def sublane_taps(first, second):
    rows = lax.broadcasted_iota(jnp.int32, (8, LANES), 0)
    return jnp.where(rows < 4, F32(first), F32(second))


def strip_taps(pick_first, pick_second, s):
    family = lax.broadcasted_iota(jnp.int32, (8, LANES), 1) // 4 % 4
    total = jnp.zeros((8, LANES), F32)
    for f in range(NDB):
        entry = phase_taps(f).get(s)
        if entry is not None:
            total = jnp.where(family == f, sublane_taps(entry[pick_first], entry[pick_second]), total)
    return total


def row_taps(family, cross, scale):
    table = phase_taps(family)
    return {s: (sublane_taps(e[0] * scale, e[3] * scale), sublane_taps(e[cross[0]] * scale, e[cross[1]] * scale)) for s, e in table.items()}


def strip_row_taps(cross, scale):
    column = lax.broadcasted_iota(jnp.int32, (8, LANES), 1) % 4
    place, facets = lax.axis_index("fcol"), lax.axis_size("fcol")
    kept = jnp.where(column < 2, jnp.where(place > 0, F32(scale), F32(0.0)), jnp.where(place < facets - 1, F32(scale), F32(0.0)))
    return {s: (strip_taps(0, 3, s) * kept, strip_taps(*cross, s) * kept) for s in range(-2, 3)}


def filter_rows(taps, pairs, at):
    direct = crossed = None
    for s, (d, e) in taps.items():
        source = pairs[at(s)]
        direct = d * source if direct is None else direct + d * source
        crossed = e * source if crossed is None else crossed + e * source
    return direct + swap_halves(crossed)


def pack4(items):
    rows = lax.broadcasted_iota(jnp.int32, (8, LANES), 0)

    def merge(a, b, step):
        keep = rows % (2 * step) < step
        return jnp.where(keep, a, pltpu.roll(b, step, 0)) + jnp.where(keep, pltpu.roll(a, 8 - step, 0), b)

    return merge(merge(items[0], items[1], 1), merge(items[2], items[3], 1), 2)


def near_columns(sources, c, at):
    def last(ref):
        return pltpu.roll(ref[c, at, ref.shape[2] - LANES :], NEAR, 1)

    if len(sources) == 1:
        return [jnp.where(lax.axis_index("fcol") == 0, sources[0][c, at, :LANES], last(sources[0]))]
    return [last(sources[0]), sources[1][c, at, :LANES]]


def fill_rows(ext, row, count, start, own, around):
    channels, _, cols = own.shape
    rows = pl.ds(start, count)
    for c in range(channels):
        at = pl.ds(row * channels + c, count, stride=channels)
        for t in range(cols // LANES):
            ext[t, at, :] = jnp.maximum(own[c, rows, t * LANES : (t + 1) * LANES], 0.0)
        for t, value in enumerate(near_columns(around, c, rows)):
            ext[cols // LANES + t, at, :] = jnp.maximum(value, 0.0)


def filter_columns(ext, table, cols, coef):
    tiles, main = cols // LANES, 2 * NDB * LANES
    coef[...] = dot3(halves(side_by_side(ext, range(tiles))), [table[i, :cols, :] for i in range(2)])
    place = lax.axis_index("fcol")
    lane = lax.broadcasted_iota(jnp.int32, (ext.shape[1], LANES), 1)
    right = [place == 0] if ext.shape[0] - tiles == 1 else [False, True]
    for t, last in enumerate(right):
        start = cols + NEAR * t if len(right) > 1 else pl.multiple_of(cols + NEAR * (1 - place), NEAR)
        rows = pl.ds(start, NEAR)
        weights = [jnp.concatenate([table[i, rows, :LANES], table[i, rows, main:]], 1) for i in range(2)]
        part = dot3(halves(ext[tiles + t][:, :NEAR]), weights)
        coef[:, main:] += part[:, LANES:]
        first = jnp.where(last, LANES - 2, 0)
        for tile in range(2 * NDB):
            turn = lax.rem(jnp.where(last, LANES - NEAR, 0) + LANES - NEAR * tile, LANES)
            moved = pltpu.roll(part[:, :LANES], turn, 1)
            coef[:, tile * LANES : (tile + 1) * LANES] += jnp.where((lane >= first) & (lane < first + 2), moved, 0.0)


def coefficients(coef, first, tiles, u_ref, count):
    squares = []
    for tile in tiles:
        lanes = slice((tile - first) * LANES, (tile - first + 1) * LANES)
        taps = strip_row_taps((2, 1), STEP_SPARSE) if tile == 2 * NDB else row_taps(tile % NDB, (2, 1), STEP_SPARSE)
        pairs = [coef[8 * i : 8 * i + 8, lanes] for i in range(count + 4)]
        for j in range(count):
            value = filter_rows(taps, pairs, lambda s: j + 2 + s)
            u_ref[8 * j : 8 * j + 8, tile * LANES : (tile + 1) * LANES] = value
            squares.append(value * value)
    return squares


def pack_half(squares):
    return [pack4(squares[g : g + 4]) for g in range(0, len(squares), 4)]


def pack_strip(squares, item):
    packed = []
    count = len(squares) // 2
    for half in range(2):
        strip = squares[half * count : (half + 1) * count]
        items = [jnp.zeros((8, LANES), F32)] * item
        for g in range(0, count, 4):
            total = strip[g]
            for k in range(1, len(strip[g : g + 4])):
                total = total + pltpu.roll(strip[g + k], STRIP * k, 1)
            items.append(total)
        items += [jnp.zeros((8, LANES), F32)] * (4 - len(items))
        packed.append(pack4(items))
    return packed


def store_halves(packed, keep, send, base=0):
    y = lax.axis_index("chan") % 2
    for i, (a, b) in enumerate(zip(*packed)):
        keep[base + 8 * i : base + 8 * i + 8, :] = jnp.where(y == 0, a, b)
        send[base + 8 * i : base + 8 * i + 8, :] = jnp.where(y == 0, b, a)


def inner_kernel(own, *refs):
    *around, table, u_ref, keep, send, keep_more, send_more, ext, coef = refs
    channels, rows, cols = own.shape
    x = lax.axis_index("frow")
    edge = jnp.zeros((ext.shape[0], 4 * channels, LANES), F32)
    ext[:, pl.ds(pl.multiple_of(x * rows * channels, 16), 4 * channels), :] = edge
    fill_rows(ext, 4 * (1 - x), rows, 0, own, around)
    filter_columns(ext, table, cols, coef)
    count = rows // 2 - 2
    squares = coefficients(coef, 0, range(2 * NDB + 1), u_ref, count)
    store_halves([pack_half(squares[i * NDB * count : (i + 1) * NDB * count]) for i in range(2)], keep, send)
    packed = [[strip] for strip in pack_strip(squares[2 * NDB * count :], 0)]
    for i in range(2):
        for r in range(i * rows // 2, (i + 1) * rows // 2, 8):
            for t in range(cols // LANES):
                total = None
                for c in range(channels):
                    value = STEP_SPARSE * jnp.maximum(own[c, r : r + 8, t * LANES : (t + 1) * LANES], 0.0)
                    total = value * value if total is None else total + value * value
                packed[i].append(total)
    store_halves(packed, keep_more, send_more)


def border_kernel(sides, own, above, keep_more, send_more, *refs):
    around = refs[:sides]
    table, u_ref, keep, send, ext, coef = refs[sides:]
    channels, rows, cols = own.shape
    x, y = lax.axis_index("frow"), lax.axis_index("chan") % 2
    places = Places(rows, cols)
    fill_rows(ext, HALO * x, HALO, pl.multiple_of((1 - x) * (rows - HALO), HALO), own, around)
    for c in range(channels):
        at = pl.ds(HALO * (1 - x) * channels + c, HALO, stride=channels)
        for t in range(cols // LANES):
            start = (c * (cols // LANES) + t) * HALO
            ext[t, at, :] = jnp.maximum(above[start : start + HALO, :], 0.0)
        for t in range(sides):
            start = (channels * (cols // LANES) + t) * HALO
            corner = jnp.maximum(above[start : start + HALO, :], 0.0)
            ext[cols // LANES + t, at, :] = corner if c == 0 else pltpu.roll(corner, LANES - NEAR * c, 1)
    filter_columns(ext, table, cols, coef)
    squares = coefficients(coef, 0, range(2 * NDB + 1), u_ref, 4)
    strips = pack_strip(squares[8 * NDB :], 2)
    needed = []
    for tile in range(2 * NDB):
        rows_here = squares[4 * tile : 4 * tile + 4]
        count = BORDER_ROWS[tile % NDB]
        needed += [jnp.where(x == 0, a, b) for a, b in zip(rows_here[:count], rows_here[4 - count :])]
    middle = len(needed) // 2
    store_halves([pack_half(needed[:middle]), pack_half(needed[middle:])], keep, send, places.border - places.strip)
    keep[: places.border - places.strip, :] = keep_more[...]
    send[: places.border - places.strip, :] = send_more[...]
    keep[:8, :] = keep_more[:8, :] + jnp.where(y == 0, *strips)
    send[:8, :] = send_more[:8, :] + jnp.where(y == 0, *strips[::-1])


def pairing_rounds(order):
    players = list(range(order))
    rounds = []
    for _ in range(order - 1):
        rounds.append([(min(a, b), max(a, b)) for a, b in zip(players[: order // 2], players[: order // 2 - 1 : -1])])
        players = [players[0]] + [players[-1]] + players[1:-1]
    return rounds


def down(values):
    for step in (4, 2, 1):
        values = values + pltpu.roll(values, step, 0)
    return values


def nuclear_kernel(limit, own, other, out, group, mix):
    channels, rows, cols = own.shape
    order = 2 * channels
    y = lax.axis_index("chan") % 2
    for c in range(channels):
        group[y * channels + c] = jnp.maximum(own[c], 0.0)
        group[(1 - y) * channels + c] = jnp.maximum(other[c], 0.0)
    blocks = [(slice(r, r + 8), slice(t, t + LANES)) for r in range(0, rows, 8) for t in range(0, cols, LANES)]
    partial = {}
    for at in blocks:
        held = [group[(c, *at)] for c in range(order)]
        for i in range(order):
            for j in range(i + 1):
                term = held[i] * held[j]
                partial[i, j] = partial[i, j] + term if (i, j) in partial else term
    row_sum = {key: jnp.sum(value, axis=0, keepdims=True) for key, value in partial.items()}
    sub = lax.broadcasted_iota(jnp.int32, (order, LANES), 0)
    turned, vectors, diag = [], [], []
    for j in range(order):
        stacked = jnp.concatenate([row_sum[max(i, j), min(i, j)] for i in range(order)], 0)
        column = jnp.broadcast_to(jnp.sum(stacked, axis=1, keepdims=True), (order, LANES))
        turned.append(column)
        unit = jnp.where(sub == j, F32(1.0), F32(0.0))
        vectors.append(unit)
        diag.append(down(column * unit))

    rounds = pairing_rounds(order)

    def sweep(_, state):
        turned, vectors, diag = (list(part) for part in state)
        for pairs in rounds:
            for p, q in pairs:
                coupling = down(vectors[p] * turned[q])
                spread = diag[q] - diag[p]
                square = spread * spread + 4.0 * coupling * coupling
                positive = square > 0.0
                inverse = jnp.where(positive, lax.rsqrt(jnp.where(positive, square, 1.0)), 0.0)
                cosine2 = jnp.where(positive, 0.5 + 0.5 * jnp.abs(spread) * inverse, 1.0)
                other = lax.rsqrt(cosine2)
                c = cosine2 * other
                s = jnp.where(spread >= 0.0, coupling, -coupling) * inverse * other
                shift = s * other * coupling
                diag[p], diag[q] = diag[p] - shift, diag[q] + shift
                turned[p], turned[q] = c * turned[p] - s * turned[q], s * turned[p] + c * turned[q]
                vectors[p], vectors[q] = c * vectors[p] - s * vectors[q], s * vectors[p] + c * vectors[q]
        return tuple(turned), tuple(vectors), tuple(diag)

    turned, vectors, _ = lax.fori_loop(0, JACOBI_SWEEPS, sweep, (tuple(turned), tuple(vectors), tuple(diag)))
    weighted = []
    for j in range(order):
        value = down(vectors[j] * turned[j])
        weighted.append(vectors[j] * (limit / jnp.maximum(jnp.sqrt(jnp.maximum(value, 0.0)), limit)))
    for k in range(order):
        total = None
        for j in range(order):
            term = weighted[j] * jnp.broadcast_to(vectors[j][k : k + 1, :], (order, LANES))
            total = term if total is None else total + term
        mix[k] = total
    for i in range(channels):
        row = [jnp.broadcast_to(mix[k, pl.ds(y * channels + i, 1), :], (order, LANES)) for k in range(order)]
        for at in blocks:
            total = None
            for k in range(order):
                term = row[k] * group[(k, *at)]
                total = term if total is None else total + term
            out[(i, *at)] = total


def scales(limit, norms):
    return limit * lax.rsqrt(jnp.maximum(norms, limit * limit))


def widen(scale, at, item):
    sub = lax.broadcasted_iota(jnp.int32, (8, LANES), 0)
    first = jnp.broadcast_to(scale[at + item : at + item + 1, :], (8, LANES))
    second = jnp.broadcast_to(scale[at + 4 + item : at + 5 + item, :], (8, LANES))
    return jnp.where(sub < 4, first, second)


def spread_rows(inner, border, taps, spread, lanes):
    x = lax.axis_index("frow")
    empty = jnp.zeros((8, LANES), F32)
    count = len(inner)
    upper = [empty, empty, *inner, *border]
    lower = [*border, *inner, empty, empty]
    padded = [jnp.where(x == 0, a, b) for a, b in zip(upper, lower)]
    for i in range(count + 2):
        spread[8 * i : 8 * i + 8, lanes] = filter_rows(taps, padded, lambda s: i + 2 - s)


class Places:
    def __init__(self, rows, cols):
        self.inner = rows // 2 - 2
        self.strip = 2 * NDB * self.inner
        self.dirac = self.strip + 8
        self.border = self.dirac + rows * cols // LANES // 2
        self.all = self.border + 2 * sum(BORDER_ROWS)


def half_duals(places, half, scale, u_inner, u_border, spread):
    x = lax.axis_index("frow")
    for family in range(NDB):
        if isinstance(half, int):
            lanes = slice((half * NDB + family) * LANES, (half * NDB + family + 1) * LANES)
        else:
            lanes = pl.ds(pl.multiple_of((half * NDB + family) * LANES, LANES), LANES)
        count = places.inner
        factors = [widen(scale, 8 * ((family * count + j) // 4), (family * count + j) % 4) for j in range(count)]
        inner = [u_inner[8 * j : 8 * j + 8, lanes] * factors[j] for j in range(count)]
        first, count = sum(BORDER_ROWS[:family]), BORDER_ROWS[family]
        factors = [widen(scale, places.border + 8 * (k // 4), k % 4) for k in range(first, first + count)]
        spare = [jnp.zeros((8, LANES), F32)] * (4 - count)
        factors = [jnp.where(x == 0, a, b) for a, b in zip(factors + spare, spare + factors)] if spare else factors
        duals = inner, [u_border[8 * j : 8 * j + 8, lanes] * factors[j] for j in range(4)]
        spread_rows(*duals, row_taps(family, (1, 2), 1.0), spread, slice(family * LANES, (family + 1) * LANES))


def first_kernel(limit, raw, density, nuclear, u_inner, u_border, mine, table, step, spread, scale):
    channels, rows, cols = raw.shape
    y = lax.axis_index("chan") % 2
    scale[...] = scales(limit, mine[...])
    half_duals(Places(rows, cols), y, scale, u_inner, u_border, spread)
    lanes = pl.ds(pl.multiple_of(y * NDB * LANES, NDB * LANES), NDB * LANES)
    result = dot3(halves(spread[...]), [table[i, :cols, lanes] for i in range(2)], ((1,), (1,)))
    for t in range(cols // LANES):
        step[cols // LANES + t] = result[:, t * LANES : (t + 1) * LANES]
    for c in range(channels):
        for t in range(cols // LANES):
            lanes = slice(t * LANES, (t + 1) * LANES)
            estimate = jnp.maximum(raw[c, :, lanes], 0.0)
            step[t, c * rows : (c + 1) * rows, :] = density[c, :, lanes] * estimate - raw[c, :, lanes] + nuclear[c, :, lanes]


def second_kernel(limit, raw, step, u_inner, u_border, mine, theirs, table, out, spread, image, scale):
    channels, rows, cols = raw.shape
    y = lax.axis_index("chan") % 2
    places = Places(rows, cols)
    scale[y] = scales(limit, mine[...])
    scale[1 - y] = scales(limit, theirs[...])
    half_duals(places, 1 - y, scale.at[1 - y], u_inner, u_border, spread)
    main = 2 * NDB * LANES
    duals = []
    for ref, item, count in ((u_inner, 0, places.inner), (u_border, 2, 4)):
        rolled = []
        for j in range(count):
            half, k = divmod(j, count // 2)
            factor = widen(scale.at[half], places.strip, item + k // 4)
            factor = factor if k % 4 == 0 else pltpu.roll(factor, LANES - STRIP * (k % 4), 1)
            rolled.append(ref[8 * j : 8 * j + 8, main:] * factor)
        duals.append(rolled)
    spread_rows(*duals, strip_row_taps((1, 2), 1.0), spread, slice(NDB * LANES, (NDB + 1) * LANES))
    lanes = pl.ds(pl.multiple_of((1 - y) * NDB * LANES, NDB * LANES), NDB * LANES)
    left = halves(spread[...])
    right = [jnp.concatenate([table[i, :cols, lanes], table[i, :cols, main:]], 1) for i in range(2)]
    result = dot3(left, right, ((1,), (1,)))
    for t in range(cols // LANES):
        image[t] = result[:, t * LANES : (t + 1) * LANES] + step[cols // LANES + t]
    for c in range(channels):
        for r in range(0, rows, 8):
            for t in range(cols // LANES):
                lanes = slice(t * LANES, (t + 1) * LANES)
                half, inside = divmod(r, rows // 2)
                at = places.dirac + 8 * (inside // 8 * (cols // LANES) + t)
                estimate = jnp.maximum(raw[c, r : r + 8, lanes], 0.0)
                dual = STEP_SPARSE * estimate * scale[half, at : at + 8, :]
                synthesis = dual + image[t, pl.ds(r * channels + c, 8, stride=channels), :]
                total = step[t, c * rows + r : c * rows + r + 8, :] + synthesis
                out[c, r : r + 8, lanes] = jnp.maximum(estimate - STEP_PRIMAL * total, 0.0)


def fixed_taps(family, band, index):
    total = jnp.zeros(index.shape, F32)
    for k, tap in enumerate(band_taps(family)[band]):
        total = jnp.where(index == k, F32(tap), total)
    return total


def hold_kernel(dirty, own, table):
    own[...] = dirty[...]
    cols = dirty.shape[2]
    blocks = cols // NEAR
    rows = {block: block * NEAR for block in range(blocks)} | {-1: cols, blocks: cols + NEAR}
    row = lax.broadcasted_iota(jnp.int32, (NEAR, LANES), 0)
    lane = lax.broadcasted_iota(jnp.int32, (NEAR, LANES), 1)

    def put(block, tile, value):
        at, lanes = slice(rows[block], rows[block] + NEAR), slice(tile * LANES, (tile + 1) * LANES)
        top = value.astype(BF16)
        table[0, at, lanes] = top
        table[1, at, lanes] = (value - top.astype(F32)).astype(BF16)

    pairs = [(f, b) for b in range(2) for f in range(NDB)]
    for tile, (f, b) in enumerate(pairs):
        base = fixed_taps(f, b, row - 2 * (lane - 2) + len(DAUBECHIES[f]) // 2 - 1)
        for block in range(blocks):
            value = pltpu.roll(base, (block * NEAR // 2 - 2) % LANES, 1)
            if block == 0:
                value = jnp.where(lane < LANES // 2, value, 0.0)
            if block == blocks - 1:
                value = jnp.where(lane < LANES // 2, 0.0, value)
            put(block, tile, value)

    def chosen(block, position, tile_of):
        value = jnp.zeros((NEAR, LANES), F32)
        for tile, (f, b) in enumerate(pairs):
            part = fixed_taps(f, b, row + block * NEAR - 2 * position + len(DAUBECHIES[f]) // 2 - 1)
            value = jnp.where(tile_of == tile, part, value)
        return value

    column = lane % 4
    position = jnp.where(column < 2, column - 2, column + cols // 2 - 2)
    for block in rows:
        inside = block in (-1, 0, blocks - 1, blocks)
        put(block, len(pairs), chosen(block, position, lane // 4) if inside else jnp.zeros((NEAR, LANES), F32))
    column = lane % NEAR
    position = jnp.where(column < NEAR // 2, column, column + cols // 2 - NEAR)
    for block in (-1, blocks):
        put(block, 0, chosen(block, position, lane // NEAR))


def rows_kernel(own, *refs):
    *around, edge = refs
    channels, rows, cols = own.shape
    start = pl.ds(pl.multiple_of((1 - lax.axis_index("frow")) * (rows - HALO), HALO), HALO)
    at = 0
    for c in range(channels):
        for t in range(cols // LANES):
            edge[at : at + HALO, :] = own[c, start, t * LANES : (t + 1) * LANES]
            at += HALO
    lane = lax.broadcasted_iota(jnp.int32, (HALO, LANES), 1) // NEAR
    totals = near_columns(around, 0, start)
    for c in range(1, channels):
        parts = near_columns(around, c, start)
        totals = [jnp.where(lane == c, pltpu.roll(part, NEAR * c, 1), total) for part, total in zip(parts, totals)]
    for total in totals:
        edge[at : at + HALO, :] = total
        at += HALO


def add_kernel(one, two, *refs):
    refs[-1][...] = one[...] + two[...]


def add_parts_kernel(one, two, three, four, out):
    count = one.shape[0]
    out[:count, :] = one[...] + two[...]
    out[count:, :] = three[...] + four[...]


def exchange(values, axis, bit):
    count = lax.axis_size(axis)
    return lax.ppermute(values, axis, [(i, i ^ bit) for i in range(count)])


def vmem(count):
    return [pl.BlockSpec(memory_space=pltpu.VMEM)] * count


def call(kernel, name, shapes, operands, scratch=(), limit=16, later=()):
    many = [jax.ShapeDtypeStruct(shape, F32) if isinstance(shape, tuple) else shape for shape in shapes]
    results = pl.pallas_call(
        kernel,
        name=name,
        out_shape=many,
        in_specs=vmem(len(operands)) + [pl.BlockSpec(memory_space=pl.ANY)] * len(later),
        out_specs=vmem(len(many)),
        scratch_shapes=[pltpu.VMEM(shape, F32) for shape in scratch],
        compiler_params=pltpu.CompilerParams(vmem_limit_bytes=limit * MIB),
    )(*operands, *later)
    return results if len(results) > 1 else results[0]


def from_neighbours(values):
    facets = lax.axis_size("fcol")
    if facets == 2:
        return [exchange(values, "fcol", 1)]
    return [
        lax.ppermute(values, "fcol", [(i, i + 1) for i in range(facets - 1)]),
        lax.ppermute(values, "fcol", [(i + 1, i) for i in range(facets - 1)]),
    ]


def on_device(dirty_image, density):
    channels, rows, cols = dirty_image.shape
    facets, chans = lax.axis_size("fcol"), lax.axis_size("chan")
    nuclear_limit = math.sqrt(rows * cols)
    sparse_limit = SPARSE_SCALE * math.sqrt(channels * chans)
    sides = 1 if facets == 2 else 2
    places, tiles = Places(rows, cols), 2 * NDB + 1
    lane_tiles = cols // LANES + sides

    around = from_neighbours(dirty_image)
    near = jax.ShapeDtypeStruct((2, cols + 2 * NEAR, tiles * LANES), BF16)
    own, near = call(hold_kernel, "hold", [dirty_image.shape, near], [dirty_image])
    edge = call(rows_kernel, "rows", [((channels * (cols // LANES) + sides) * HALO, LANES)], [own, *around])
    above = exchange(edge, "frow", 1)
    main, more = (places.strip, LANES), (places.border - places.strip, LANES)
    u_inner, keep, send, keep_more, send_more = call(
        inner_kernel,
        "inner",
        [(8 * places.inner, tiles * LANES), main, main, more, more],
        [own, *around, near],
        [(lane_tiles, 8 * (places.inner + 4), LANES), (8 * (places.inner + 4), tiles * LANES)],
        24,
    )
    received = exchange(send, "chan", 1)
    u_border, keep_more, send_more = call(
        lambda *refs: border_kernel(sides, *refs),
        "border",
        [(8 * 4, tiles * LANES)] + [(places.all - places.strip, LANES)] * 2,
        [own, above, keep_more, send_more, *around, near],
        [(lane_tiles, 8 * 8, LANES), (8 * 8, tiles * LANES)],
        24,
    )
    received_more = exchange(send_more, "chan", 1)
    total = call(add_parts_kernel, "add", [(places.all, LANES)], [keep, received, keep_more, received_more])
    other = exchange(own, "chan", 1)
    nuclear = call(
        lambda *refs: nuclear_kernel(nuclear_limit, *refs),
        "nuclear",
        [dirty_image.shape],
        [own, other],
        [(2 * channels, rows, cols), (2 * channels, 2 * channels, LANES)],
    )
    bit = 2
    while bit < chans:
        received = exchange(total, "chan", bit)
        total = call(add_kernel, "add", [(places.all, LANES)], [total, received], later=[] if 2 * bit < chans else [nuclear])
        bit *= 2
    theirs = exchange(total, "chan", 1)
    step = call(
        lambda *refs: first_kernel(sparse_limit, *refs),
        "first",
        [(2 * cols // LANES, channels * rows, LANES)],
        [own, density, nuclear, u_inner, u_border, total, near],
        [(4 * rows, NDB * LANES), (places.all, LANES)],
        24,
    )
    return call(
        lambda *refs: second_kernel(sparse_limit, *refs),
        "second",
        [dirty_image.shape],
        [own, step, u_inner, u_border, total, theirs, near],
        [(4 * rows, (NDB + 1) * LANES), (cols // LANES, 4 * rows, LANES), (2, places.all, LANES)],
        24,
    )


def solution(mesh):
    return jax.shard_map(
        on_device,
        mesh=mesh,
        in_specs=(P("chan", "frow", "fcol"), P("chan", "frow", "fcol")),
        out_specs=P("chan", "frow", "fcol"),
        check_vma=False,
    )
```

```python
import math

import jax
import jax.numpy as jnp
from jax import lax
from jax.experimental import pallas as pl
from jax.experimental.pallas import tpu as pltpu
from jax.sharding import PartitionSpec as P

DAUBECHIES = (
    (0.7071067811865476, 0.7071067811865476),
    (0.48296291314469025, 0.836516303737469, 0.22414386804185735, -0.12940952255092145),
    (
        0.3326705529509569,
        0.8068915093133388,
        0.4598775021193313,
        -0.13501102001039084,
        -0.08544127388224149,
        0.035226291882100656,
    ),
    (
        0.23037781330885523,
        0.7148465705525415,
        0.6308807679295904,
        -0.02798376941698385,
        -0.18703481171888114,
        0.030841381835986965,
        0.032883011666982945,
        -0.010597401784997278,
    ),
)
NDB = len(DAUBECHIES)
JACOBI_SWEEPS = 6
STEP_PRIMAL = 0.2
STEP_SPARSE = 0.5
SPARSE_SCALE = 0.5
LANES = 128
BORDER_ROWS = [2 + len(taps) // 4 for taps in DAUBECHIES]
STRIP = 32
NEAR = 16
HALO = 8
MIB = 1 << 20
F32 = jnp.float32
BF16 = jnp.bfloat16


def band_taps(family):
    low = DAUBECHIES[family]
    high = [(-1.0) ** k * low[len(low) - 1 - k] for k in range(len(low))]
    return low, high


def phase_taps(family):
    low, high = band_taps(family)
    offset = len(low) // 2 - 1
    table = {}
    for k in range(len(low)):
        s, odd = divmod(k - offset, 2)
        entry = table.setdefault(s, [0.0, 0.0, 0.0, 0.0])
        entry[odd] = low[k]
        entry[2 + odd] = high[k]
    return table


def halves(values):
    top = values.astype(BF16)
    return top, (values - top.astype(F32)).astype(BF16)


def dot3(left, right, dims=((1,), (0,))):
    def dot(one, two):
        return lax.dot_general(one, two, (dims, ((), ())), preferred_element_type=F32)

    count = left[0].shape[0]
    both = dot(jnp.concatenate(left, 0), right[0])
    return both[:count] + (both[count:] + dot(left[0], right[1]))


def side_by_side(ref, tiles):
    return jnp.concatenate([ref[t] for t in tiles], 1)


def swap_halves(values):
    return pltpu.roll(values, 4, 0)


def sublane_taps(first, second):
    rows = lax.broadcasted_iota(jnp.int32, (8, LANES), 0)
    return jnp.where(rows < 4, F32(first), F32(second))


def strip_taps(pick_first, pick_second, s):
    family = lax.broadcasted_iota(jnp.int32, (8, LANES), 1) // 4 % 4
    total = jnp.zeros((8, LANES), F32)
    for f in range(NDB):
        entry = phase_taps(f).get(s)
        if entry is not None:
            total = jnp.where(family == f, sublane_taps(entry[pick_first], entry[pick_second]), total)
    return total


def row_taps(family, cross, scale):
    table = phase_taps(family)
    return {s: (sublane_taps(e[0] * scale, e[3] * scale), sublane_taps(e[cross[0]] * scale, e[cross[1]] * scale)) for s, e in table.items()}


def strip_row_taps(cross, scale):
    column = lax.broadcasted_iota(jnp.int32, (8, LANES), 1) % 4
    place, facets = lax.axis_index("fcol"), lax.axis_size("fcol")
    kept = jnp.where(column < 2, jnp.where(place > 0, F32(scale), F32(0.0)), jnp.where(place < facets - 1, F32(scale), F32(0.0)))
    return {s: (strip_taps(0, 3, s) * kept, strip_taps(*cross, s) * kept) for s in range(-2, 3)}


def filter_rows(taps, pairs, at):
    direct = crossed = None
    for s, (d, e) in taps.items():
        source = pairs[at(s)]
        direct = d * source if direct is None else direct + d * source
        crossed = e * source if crossed is None else crossed + e * source
    return direct + swap_halves(crossed)


def pack4(items):
    rows = lax.broadcasted_iota(jnp.int32, (8, LANES), 0)

    def merge(a, b, step):
        keep = rows % (2 * step) < step
        return jnp.where(keep, a, pltpu.roll(b, step, 0)) + jnp.where(keep, pltpu.roll(a, 8 - step, 0), b)

    return merge(merge(items[0], items[1], 1), merge(items[2], items[3], 1), 2)


def near_columns(sources, c, at, lane=0):
    def last(ref):
        return pltpu.roll(ref[c, at, ref.shape[2] - LANES :], lane + NEAR, 1)

    def first(ref):
        return pltpu.roll(ref[c, at, :LANES], lane, 1) if lane else ref[c, at, :LANES]

    if len(sources) > 1:
        return [last(sources[0]), first(sources[1])]
    place = lax.axis_index("fcol")
    start = pl.multiple_of(place * (sources[0].shape[2] - LANES), LANES)
    return [pltpu.roll(sources[0][c, at, pl.ds(start, LANES)], lane + NEAR * place, 1)]


def fill_rows(ext, row, count, start, own, around):
    channels, _, cols = own.shape
    rows = pl.ds(start, count)
    for c in range(channels):
        at = pl.ds(row * channels + c, count, stride=channels)
        for t in range(cols // LANES):
            ext[t, at, :] = jnp.maximum(own[c, rows, t * LANES : (t + 1) * LANES], 0.0)
        for t, value in enumerate(near_columns(around, c, rows)):
            ext[cols // LANES + t, at, :] = jnp.maximum(value, 0.0)


def filter_columns(ext, table, cols, coef):
    tiles, main = cols // LANES, 2 * NDB * LANES
    coef[...] = dot3(halves(side_by_side(ext, range(tiles))), [table[i, :cols, :] for i in range(2)])
    place = lax.axis_index("fcol")
    lane = lax.broadcasted_iota(jnp.int32, (ext.shape[1], LANES), 1)
    right = [place == 0] if ext.shape[0] - tiles == 1 else [False, True]
    for t, last in enumerate(right):
        start = cols + NEAR * t if len(right) > 1 else pl.multiple_of(cols + NEAR * (1 - place), NEAR)
        rows = pl.ds(start, NEAR)
        weights = [jnp.concatenate([table[i, rows, :LANES], table[i, rows, main:]], 1) for i in range(2)]
        part = dot3(halves(ext[tiles + t][:, :NEAR]), weights)
        coef[:, main:] += part[:, LANES:]
        first = jnp.where(last, LANES - 2, 0)
        for tile in range(2 * NDB):
            turn = lax.rem(jnp.where(last, LANES - NEAR, 0) + LANES - NEAR * tile, LANES)
            moved = pltpu.roll(part[:, :LANES], turn, 1)
            coef[:, tile * LANES : (tile + 1) * LANES] += jnp.where((lane >= first) & (lane < first + 2), moved, 0.0)


def coefficients(coef, first, tiles, u_ref, count):
    squares = []
    for tile in tiles:
        lanes = slice((tile - first) * LANES, (tile - first + 1) * LANES)
        taps = strip_row_taps((2, 1), STEP_SPARSE) if tile == 2 * NDB else row_taps(tile % NDB, (2, 1), STEP_SPARSE)
        pairs = [coef[8 * i : 8 * i + 8, lanes] for i in range(count + 4)]
        for j in range(count):
            value = filter_rows(taps, pairs, lambda s: j + 2 + s)
            u_ref[8 * j : 8 * j + 8, tile * LANES : (tile + 1) * LANES] = value
            squares.append(value * value)
    return squares


def pack_half(squares):
    return [pack4(squares[g : g + 4]) for g in range(0, len(squares), 4)]


def pack_strip(squares, item):
    packed = []
    count = len(squares) // 2
    for half in range(2):
        strip = squares[half * count : (half + 1) * count]
        items = [jnp.zeros((8, LANES), F32)] * item
        for g in range(0, count, 4):
            total = strip[g]
            for k in range(1, len(strip[g : g + 4])):
                total = total + pltpu.roll(strip[g + k], STRIP * k, 1)
            items.append(total)
        items += [jnp.zeros((8, LANES), F32)] * (4 - len(items))
        packed.append(pack4(items))
    return packed


def store_halves(packed, keep, send, base=0):
    y = lax.axis_index("chan") % 2
    for i, (a, b) in enumerate(zip(*packed)):
        keep[base + 8 * i : base + 8 * i + 8, :] = jnp.where(y == 0, a, b)
        send[base + 8 * i : base + 8 * i + 8, :] = jnp.where(y == 0, b, a)


def inner_kernel(own, *refs):
    *around, table, u_ref, keep, send, keep_more, send_more, ext, coef = refs
    channels, rows, cols = own.shape
    x = lax.axis_index("frow")
    edge = jnp.zeros((ext.shape[0], 4 * channels, LANES), F32)
    ext[:, pl.ds(pl.multiple_of(x * rows * channels, 16), 4 * channels), :] = edge
    fill_rows(ext, 4 * (1 - x), rows, 0, own, around)
    filter_columns(ext, table, cols, coef)
    count = rows // 2 - 2
    squares = coefficients(coef, 0, range(2 * NDB + 1), u_ref, count)
    store_halves([pack_half(squares[i * NDB * count : (i + 1) * NDB * count]) for i in range(2)], keep, send)
    packed = [[strip] for strip in pack_strip(squares[2 * NDB * count :], 0)]
    for i in range(2):
        for r in range(i * rows // 2, (i + 1) * rows // 2, 8):
            for t in range(cols // LANES):
                total = None
                for c in range(channels):
                    value = STEP_SPARSE * jnp.maximum(own[c, r : r + 8, t * LANES : (t + 1) * LANES], 0.0)
                    total = value * value if total is None else total + value * value
                packed[i].append(total)
    store_halves(packed, keep_more, send_more)


def border_kernel(sides, own, above, keep_more, send_more, *refs):
    around = refs[:sides]
    table, u_ref, keep, send, ext, coef = refs[sides:]
    channels, rows, cols = own.shape
    x, y = lax.axis_index("frow"), lax.axis_index("chan") % 2
    places = Places(rows, cols)
    fill_rows(ext, HALO * x, HALO, pl.multiple_of((1 - x) * (rows - HALO), HALO), own, around)
    for c in range(channels):
        at = pl.ds(HALO * (1 - x) * channels + c, HALO, stride=channels)
        for t in range(cols // LANES):
            start = (c * (cols // LANES) + t) * HALO
            ext[t, at, :] = jnp.maximum(above[start : start + HALO, :], 0.0)
        for t in range(sides):
            start = (channels * (cols // LANES) + t) * HALO
            corner = jnp.maximum(above[start : start + HALO, :], 0.0)
            ext[cols // LANES + t, at, :] = corner if c == 0 else pltpu.roll(corner, LANES - NEAR * c, 1)
    filter_columns(ext, table, cols, coef)
    squares = coefficients(coef, 0, range(2 * NDB + 1), u_ref, 4)
    strips = pack_strip(squares[8 * NDB :], 2)
    needed = []
    for tile in range(2 * NDB):
        rows_here = squares[4 * tile : 4 * tile + 4]
        count = BORDER_ROWS[tile % NDB]
        needed += [jnp.where(x == 0, a, b) for a, b in zip(rows_here[:count], rows_here[4 - count :])]
    middle = len(needed) // 2
    store_halves([pack_half(needed[:middle]), pack_half(needed[middle:])], keep, send, places.border - places.strip)
    keep[: places.border - places.strip, :] = keep_more[...]
    send[: places.border - places.strip, :] = send_more[...]
    keep[:8, :] = keep_more[:8, :] + jnp.where(y == 0, *strips)
    send[:8, :] = send_more[:8, :] + jnp.where(y == 0, *strips[::-1])


def pairing_rounds(order):
    players = list(range(order))
    rounds = []
    for _ in range(order - 1):
        rounds.append([(min(a, b), max(a, b)) for a, b in zip(players[: order // 2], players[: order // 2 - 1 : -1])])
        players = [players[0]] + [players[-1]] + players[1:-1]
    return rounds


def down(values):
    for step in (4, 2, 1):
        values = values + pltpu.roll(values, step, 0)
    return values


def nuclear_kernel(limit, own, other, out, group, mix):
    channels, rows, cols = own.shape
    order = 2 * channels
    y = lax.axis_index("chan") % 2
    for c in range(channels):
        group[y * channels + c] = jnp.maximum(own[c], 0.0)
        group[(1 - y) * channels + c] = jnp.maximum(other[c], 0.0)
    blocks = [(slice(r, r + 8), slice(t, t + LANES)) for r in range(0, rows, 8) for t in range(0, cols, LANES)]
    partial = {}
    for at in blocks:
        held = [group[(c, *at)] for c in range(order)]
        for i in range(order):
            for j in range(i + 1):
                term = held[i] * held[j]
                partial[i, j] = partial[i, j] + term if (i, j) in partial else term
    row_sum = {key: jnp.sum(value, axis=0, keepdims=True) for key, value in partial.items()}
    sub = lax.broadcasted_iota(jnp.int32, (order, LANES), 0)
    turned, vectors, diag = [], [], []
    for j in range(order):
        stacked = jnp.concatenate([row_sum[max(i, j), min(i, j)] for i in range(order)], 0)
        column = jnp.broadcast_to(jnp.sum(stacked, axis=1, keepdims=True), (order, LANES))
        turned.append(column)
        unit = jnp.where(sub == j, F32(1.0), F32(0.0))
        vectors.append(unit)
        diag.append(down(column * unit))

    rounds = pairing_rounds(order)

    def sweep(_, state):
        turned, vectors, diag = (list(part) for part in state)
        for pairs in rounds:
            for p, q in pairs:
                coupling = down(vectors[p] * turned[q])
                spread = diag[q] - diag[p]
                square = spread * spread + 4.0 * coupling * coupling
                positive = square > 0.0
                inverse = jnp.where(positive, lax.rsqrt(jnp.where(positive, square, 1.0)), 0.0)
                cosine2 = jnp.where(positive, 0.5 + 0.5 * jnp.abs(spread) * inverse, 1.0)
                other = lax.rsqrt(cosine2)
                c = cosine2 * other
                s = jnp.where(spread >= 0.0, coupling, -coupling) * inverse * other
                shift = s * other * coupling
                diag[p], diag[q] = diag[p] - shift, diag[q] + shift
                turned[p], turned[q] = c * turned[p] - s * turned[q], s * turned[p] + c * turned[q]
                vectors[p], vectors[q] = c * vectors[p] - s * vectors[q], s * vectors[p] + c * vectors[q]
        return tuple(turned), tuple(vectors), tuple(diag)

    turned, vectors, _ = lax.fori_loop(0, JACOBI_SWEEPS, sweep, (tuple(turned), tuple(vectors), tuple(diag)))
    weighted = []
    for j in range(order):
        value = down(vectors[j] * turned[j])
        weighted.append(vectors[j] * (limit / jnp.maximum(jnp.sqrt(jnp.maximum(value, 0.0)), limit)))
    for k in range(order):
        total = None
        for j in range(order):
            term = weighted[j] * jnp.broadcast_to(vectors[j][k : k + 1, :], (order, LANES))
            total = term if total is None else total + term
        mix[k] = total
    for i in range(channels):
        row = [jnp.broadcast_to(mix[k, pl.ds(y * channels + i, 1), :], (order, LANES)) for k in range(order)]
        for at in blocks:
            total = None
            for k in range(order):
                term = row[k] * group[(k, *at)]
                total = term if total is None else total + term
            out[(i, *at)] = total


def scales(limit, norms):
    return limit * lax.rsqrt(jnp.maximum(norms, limit * limit))


def widen(scale, at, item):
    sub = lax.broadcasted_iota(jnp.int32, (8, LANES), 0)
    first = jnp.broadcast_to(scale[at + item : at + item + 1, :], (8, LANES))
    second = jnp.broadcast_to(scale[at + 4 + item : at + 5 + item, :], (8, LANES))
    return jnp.where(sub < 4, first, second)


def spread_rows(inner, border, taps, spread, lanes):
    x = lax.axis_index("frow")
    empty = jnp.zeros((8, LANES), F32)
    count = len(inner)
    upper = [empty, empty, *inner, *border]
    lower = [*border, *inner, empty, empty]
    padded = [jnp.where(x == 0, a, b) for a, b in zip(upper, lower)]
    for i in range(count + 2):
        spread[8 * i : 8 * i + 8, lanes] = filter_rows(taps, padded, lambda s: i + 2 - s)


class Places:
    def __init__(self, rows, cols):
        self.inner = rows // 2 - 2
        self.strip = 2 * NDB * self.inner
        self.dirac = self.strip + 8
        self.border = self.dirac + rows * cols // LANES // 2
        self.all = self.border + 2 * sum(BORDER_ROWS)


def half_duals(places, half, scale, u_inner, u_border, spread):
    x = lax.axis_index("frow")
    for family in range(NDB):
        if isinstance(half, int):
            lanes = slice((half * NDB + family) * LANES, (half * NDB + family + 1) * LANES)
        else:
            lanes = pl.ds(pl.multiple_of((half * NDB + family) * LANES, LANES), LANES)
        count = places.inner
        factors = [widen(scale, 8 * ((family * count + j) // 4), (family * count + j) % 4) for j in range(count)]
        inner = [u_inner[8 * j : 8 * j + 8, lanes] * factors[j] for j in range(count)]
        first, count = sum(BORDER_ROWS[:family]), BORDER_ROWS[family]
        factors = [widen(scale, places.border + 8 * (k // 4), k % 4) for k in range(first, first + count)]
        spare = [jnp.zeros((8, LANES), F32)] * (4 - count)
        factors = [jnp.where(x == 0, a, b) for a, b in zip(factors + spare, spare + factors)] if spare else factors
        duals = inner, [u_border[8 * j : 8 * j + 8, lanes] * factors[j] for j in range(4)]
        spread_rows(*duals, row_taps(family, (1, 2), 1.0), spread, slice(family * LANES, (family + 1) * LANES))


def first_kernel(limit, raw, density, nuclear, u_inner, u_border, mine, table, step, spread, scale):
    channels, rows, cols = raw.shape
    y = lax.axis_index("chan") % 2
    scale[...] = scales(limit, mine[...])
    half_duals(Places(rows, cols), y, scale, u_inner, u_border, spread)
    lanes = pl.ds(pl.multiple_of(y * NDB * LANES, NDB * LANES), NDB * LANES)
    result = dot3(halves(spread[...]), [table[i, :cols, lanes] for i in range(2)], ((1,), (1,)))
    for t in range(cols // LANES):
        step[cols // LANES + t] = result[:, t * LANES : (t + 1) * LANES]
    for c in range(channels):
        for t in range(cols // LANES):
            lanes = slice(t * LANES, (t + 1) * LANES)
            estimate = jnp.maximum(raw[c, :, lanes], 0.0)
            step[t, c * rows : (c + 1) * rows, :] = density[c, :, lanes] * estimate - raw[c, :, lanes] + nuclear[c, :, lanes]


def second_kernel(limit, raw, step, u_inner, u_border, mine, theirs, table, out, spread, image, scale):
    channels, rows, cols = raw.shape
    y = lax.axis_index("chan") % 2
    places = Places(rows, cols)
    both = slice(places.strip, places.border)
    scale[y, both, :] = scales(limit, mine[both, :])
    scale[1 - y] = scales(limit, theirs[...])
    half_duals(places, 1 - y, scale.at[1 - y], u_inner, u_border, spread)
    main = 2 * NDB * LANES
    duals = []
    for ref, item, count in ((u_inner, 0, places.inner), (u_border, 2, 4)):
        rolled = []
        for j in range(count):
            half, k = divmod(j, count // 2)
            factor = widen(scale.at[half], places.strip, item + k // 4)
            factor = factor if k % 4 == 0 else pltpu.roll(factor, LANES - STRIP * (k % 4), 1)
            rolled.append(ref[8 * j : 8 * j + 8, main:] * factor)
        duals.append(rolled)
    spread_rows(*duals, strip_row_taps((1, 2), 1.0), spread, slice(NDB * LANES, (NDB + 1) * LANES))
    lanes = pl.ds(pl.multiple_of((1 - y) * NDB * LANES, NDB * LANES), NDB * LANES)
    left = halves(spread[...])
    right = [jnp.concatenate([table[i, :cols, lanes], table[i, :cols, main:]], 1) for i in range(2)]
    result = dot3(left, right, ((1,), (1,)))
    for t in range(cols // LANES):
        image[t] = result[:, t * LANES : (t + 1) * LANES] + step[cols // LANES + t]
    for c in range(channels):
        for r in range(0, rows, 8):
            for t in range(cols // LANES):
                lanes = slice(t * LANES, (t + 1) * LANES)
                half, inside = divmod(r, rows // 2)
                at = places.dirac + 8 * (inside // 8 * (cols // LANES) + t)
                estimate = jnp.maximum(raw[c, r : r + 8, lanes], 0.0)
                dual = STEP_SPARSE * estimate * scale[half, at : at + 8, :]
                synthesis = dual + image[t, pl.ds(r * channels + c, 8, stride=channels), :]
                total = step[t, c * rows + r : c * rows + r + 8, :] + synthesis
                out[c, r : r + 8, lanes] = jnp.maximum(estimate - STEP_PRIMAL * total, 0.0)


def fixed_taps(family, band, index):
    total = jnp.zeros(index.shape, F32)
    for k, tap in enumerate(band_taps(family)[band]):
        total = jnp.where(index == k, F32(tap), total)
    return total


def hold_kernel(dirty, own, table):
    own[...] = dirty[...]
    cols = dirty.shape[2]
    blocks = cols // NEAR
    rows = {block: block * NEAR for block in range(blocks)} | {-1: cols, blocks: cols + NEAR}
    row = lax.broadcasted_iota(jnp.int32, (NEAR, LANES), 0)
    lane = lax.broadcasted_iota(jnp.int32, (NEAR, LANES), 1)

    def put(block, tile, value):
        at, lanes = slice(rows[block], rows[block] + NEAR), slice(tile * LANES, (tile + 1) * LANES)
        top = value.astype(BF16)
        table[0, at, lanes] = top
        table[1, at, lanes] = (value - top.astype(F32)).astype(BF16)

    pairs = [(f, b) for b in range(2) for f in range(NDB)]
    for tile, (f, b) in enumerate(pairs):
        base = fixed_taps(f, b, row - 2 * (lane - 2) + len(DAUBECHIES[f]) // 2 - 1)
        for block in range(blocks):
            value = pltpu.roll(base, (block * NEAR // 2 - 2) % LANES, 1)
            if block == 0:
                value = jnp.where(lane < LANES // 2, value, 0.0)
            if block == blocks - 1:
                value = jnp.where(lane < LANES // 2, 0.0, value)
            put(block, tile, value)

    def chosen(block, position, tile_of):
        value = jnp.zeros((NEAR, LANES), F32)
        for tile, (f, b) in enumerate(pairs):
            part = fixed_taps(f, b, row + block * NEAR - 2 * position + len(DAUBECHIES[f]) // 2 - 1)
            value = jnp.where(tile_of == tile, part, value)
        return value

    column = lane % 4
    position = jnp.where(column < 2, column - 2, column + cols // 2 - 2)
    for block in rows:
        inside = block in (-1, 0, blocks - 1, blocks)
        put(block, len(pairs), chosen(block, position, lane // 4) if inside else jnp.zeros((NEAR, LANES), F32))
    column = lane % NEAR
    position = jnp.where(column < NEAR // 2, column, column + cols // 2 - NEAR)
    for block in (-1, blocks):
        put(block, 0, chosen(block, position, lane // NEAR))


def rows_kernel(own, *refs):
    *around, edge = refs
    channels, rows, cols = own.shape
    start = pl.ds(pl.multiple_of((1 - lax.axis_index("frow")) * (rows - HALO), HALO), HALO)
    at = 0
    for c in range(channels):
        for t in range(cols // LANES):
            edge[at : at + HALO, :] = own[c, start, t * LANES : (t + 1) * LANES]
            at += HALO
    lane = lax.broadcasted_iota(jnp.int32, (HALO, LANES), 1) // NEAR
    totals = near_columns(around, 0, start)
    for c in range(1, channels):
        parts = near_columns(around, c, start, NEAR * c)
        totals = [jnp.where(lane == c, part, total) for part, total in zip(parts, totals)]
    for total in totals:
        edge[at : at + HALO, :] = total
        at += HALO


def add_kernel(one, two, *refs):
    refs[-1][...] = one[...] + two[...]


def add_parts_kernel(one, two, three, four, out):
    count = one.shape[0]
    out[:count, :] = one[...] + two[...]
    out[count:, :] = three[...] + four[...]


def exchange(values, axis, bit):
    count = lax.axis_size(axis)
    return lax.ppermute(values, axis, [(i, i ^ bit) for i in range(count)])


def vmem(count):
    return [pl.BlockSpec(memory_space=pltpu.VMEM)] * count


def call(kernel, name, shapes, operands, scratch=(), limit=16, later=()):
    many = [jax.ShapeDtypeStruct(shape, F32) if isinstance(shape, tuple) else shape for shape in shapes]
    results = pl.pallas_call(
        kernel,
        name=name,
        out_shape=many,
        in_specs=vmem(len(operands)) + [pl.BlockSpec(memory_space=pl.ANY)] * len(later),
        out_specs=vmem(len(many)),
        scratch_shapes=[pltpu.VMEM(shape, F32) for shape in scratch],
        compiler_params=pltpu.CompilerParams(vmem_limit_bytes=limit * MIB),
    )(*operands, *later)
    return results if len(results) > 1 else results[0]


def from_neighbours(values):
    facets = lax.axis_size("fcol")
    if facets == 2:
        return [exchange(values, "fcol", 1)]
    return [
        lax.ppermute(values, "fcol", [(i, i + 1) for i in range(facets - 1)]),
        lax.ppermute(values, "fcol", [(i + 1, i) for i in range(facets - 1)]),
    ]


def on_device(dirty_image, density):
    channels, rows, cols = dirty_image.shape
    facets, chans = lax.axis_size("fcol"), lax.axis_size("chan")
    nuclear_limit = math.sqrt(rows * cols)
    sparse_limit = SPARSE_SCALE * math.sqrt(channels * chans)
    sides = 1 if facets == 2 else 2
    places, tiles = Places(rows, cols), 2 * NDB + 1
    lane_tiles = cols // LANES + sides

    around = from_neighbours(dirty_image)
    near = jax.ShapeDtypeStruct((2, cols + 2 * NEAR, tiles * LANES), BF16)
    own, near = call(hold_kernel, "hold", [dirty_image.shape, near], [dirty_image])
    edge = call(rows_kernel, "rows", [((channels * (cols // LANES) + sides) * HALO, LANES)], [own, *around])
    above = exchange(edge, "frow", 1)
    main, more = (places.strip, LANES), (places.border - places.strip, LANES)
    u_inner, keep, send, keep_more, send_more = call(
        inner_kernel,
        "inner",
        [(8 * places.inner, tiles * LANES), main, main, more, more],
        [own, *around, near],
        [(lane_tiles, 8 * (places.inner + 4), LANES), (8 * (places.inner + 4), tiles * LANES)],
        24,
    )
    received = exchange(send, "chan", 1)
    u_border, keep_more, send_more = call(
        lambda *refs: border_kernel(sides, *refs),
        "border",
        [(8 * 4, tiles * LANES)] + [(places.all - places.strip, LANES)] * 2,
        [own, above, keep_more, send_more, *around, near],
        [(lane_tiles, 8 * 8, LANES), (8 * 8, tiles * LANES)],
        24,
    )
    received_more = exchange(send_more, "chan", 1)
    total = call(add_parts_kernel, "add", [(places.all, LANES)], [keep, received, keep_more, received_more])
    other = exchange(own, "chan", 1)
    nuclear = call(
        lambda *refs: nuclear_kernel(nuclear_limit, *refs),
        "nuclear",
        [dirty_image.shape],
        [own, other],
        [(2 * channels, rows, cols), (2 * channels, 2 * channels, LANES)],
    )
    bit = 2
    while bit < chans:
        received = exchange(total, "chan", bit)
        total = call(add_kernel, "add", [(places.all, LANES)], [total, received], later=[] if 2 * bit < chans else [nuclear])
        bit *= 2
    theirs = exchange(total, "chan", 1)
    step = call(
        lambda *refs: first_kernel(sparse_limit, *refs),
        "first",
        [(2 * cols // LANES, channels * rows, LANES)],
        [own, density, nuclear, u_inner, u_border, total, near],
        [(4 * rows, NDB * LANES), (places.all, LANES)],
        24,
    )
    return call(
        lambda *refs: second_kernel(sparse_limit, *refs),
        "second",
        [dirty_image.shape],
        [own, step, u_inner, u_border, total, theirs, near],
        [(4 * rows, (NDB + 1) * LANES), (cols // LANES, 4 * rows, LANES), (2, places.all, LANES)],
        24,
    )


def solution(mesh):
    return jax.shard_map(
        on_device,
        mesh=mesh,
        in_specs=(P("chan", "frow", "fcol"), P("chan", "frow", "fcol")),
        out_specs=P("chan", "frow", "fcol"),
        check_vma=False,
    )
```

```python
import math

import jax
import jax.numpy as jnp
from jax import lax
from jax.experimental import pallas as pl
from jax.experimental.pallas import tpu as pltpu
from jax.sharding import PartitionSpec as P

DAUBECHIES = (
    (0.7071067811865476, 0.7071067811865476),
    (0.48296291314469025, 0.836516303737469, 0.22414386804185735, -0.12940952255092145),
    (
        0.3326705529509569,
        0.8068915093133388,
        0.4598775021193313,
        -0.13501102001039084,
        -0.08544127388224149,
        0.035226291882100656,
    ),
    (
        0.23037781330885523,
        0.7148465705525415,
        0.6308807679295904,
        -0.02798376941698385,
        -0.18703481171888114,
        0.030841381835986965,
        0.032883011666982945,
        -0.010597401784997278,
    ),
)
NDB = len(DAUBECHIES)
JACOBI_SWEEPS = 6
STEP_PRIMAL = 0.2
STEP_SPARSE = 0.5
SPARSE_SCALE = 0.5
LANES = 128
BORDER_ROWS = [2 + len(taps) // 4 for taps in DAUBECHIES]
STRIP = 32
NEAR = 16
HALO = 8
MIB = 1 << 20
F32 = jnp.float32
BF16 = jnp.bfloat16


def band_taps(family):
    low = DAUBECHIES[family]
    high = [(-1.0) ** k * low[len(low) - 1 - k] for k in range(len(low))]
    return low, high


def phase_taps(family):
    low, high = band_taps(family)
    offset = len(low) // 2 - 1
    table = {}
    for k in range(len(low)):
        s, odd = divmod(k - offset, 2)
        entry = table.setdefault(s, [0.0, 0.0, 0.0, 0.0])
        entry[odd] = low[k]
        entry[2 + odd] = high[k]
    return table


def halves(values):
    top = values.astype(BF16)
    return top, (values - top.astype(F32)).astype(BF16)


def dot3(left, right, dims=((1,), (0,))):
    def dot(one, two):
        return lax.dot_general(one, two, (dims, ((), ())), preferred_element_type=F32)

    count = left[0].shape[0]
    both = dot(jnp.concatenate(left, 0), right[0])
    return both[:count] + (both[count:] + dot(left[0], right[1]))


def side_by_side(ref, tiles):
    return jnp.concatenate([ref[t] for t in tiles], 1)


def swap_halves(values):
    return pltpu.roll(values, 4, 0)


def sublane_taps(first, second):
    rows = lax.broadcasted_iota(jnp.int32, (8, LANES), 0)
    return jnp.where(rows < 4, F32(first), F32(second))


def strip_taps(pick_first, pick_second, s):
    family = lax.broadcasted_iota(jnp.int32, (8, LANES), 1) // 4 % 4
    total = jnp.zeros((8, LANES), F32)
    for f in range(NDB):
        entry = phase_taps(f).get(s)
        if entry is not None:
            total = jnp.where(family == f, sublane_taps(entry[pick_first], entry[pick_second]), total)
    return total


def row_taps(family, cross, scale):
    table = phase_taps(family)
    return {s: (sublane_taps(e[0] * scale, e[3] * scale), sublane_taps(e[cross[0]] * scale, e[cross[1]] * scale)) for s, e in table.items()}


def strip_row_taps(cross, scale):
    column = lax.broadcasted_iota(jnp.int32, (8, LANES), 1) % 4
    place, facets = lax.axis_index("fcol"), lax.axis_size("fcol")
    kept = jnp.where(column < 2, jnp.where(place > 0, F32(scale), F32(0.0)), jnp.where(place < facets - 1, F32(scale), F32(0.0)))
    return {s: (strip_taps(0, 3, s) * kept, strip_taps(*cross, s) * kept) for s in range(-2, 3)}


def filter_rows(taps, pairs, at):
    direct = crossed = None
    for s, (d, e) in taps.items():
        source = pairs[at(s)]
        direct = d * source if direct is None else direct + d * source
        crossed = e * source if crossed is None else crossed + e * source
    return direct + swap_halves(crossed)


def pack4(items):
    rows = lax.broadcasted_iota(jnp.int32, (8, LANES), 0)

    def merge(a, b, step):
        keep = rows % (2 * step) < step
        return jnp.where(keep, a, pltpu.roll(b, step, 0)) + jnp.where(keep, pltpu.roll(a, 8 - step, 0), b)

    return merge(merge(items[0], items[1], 1), merge(items[2], items[3], 1), 2)


def near_columns(sources, c, at, lane=0):
    def last(ref):
        return pltpu.roll(ref[c, at, ref.shape[2] - LANES :], lane + NEAR, 1)

    def first(ref):
        return pltpu.roll(ref[c, at, :LANES], lane, 1) if lane else ref[c, at, :LANES]

    if len(sources) > 1:
        return [last(sources[0]), first(sources[1])]
    place = lax.axis_index("fcol")
    start = pl.multiple_of(place * (sources[0].shape[2] - LANES), LANES)
    return [pltpu.roll(sources[0][c, at, pl.ds(start, LANES)], lane + NEAR * place, 1)]


def fill_rows(ext, row, count, start, own, around):
    channels, _, cols = own.shape
    rows = pl.ds(start, count)
    for c in range(channels):
        at = pl.ds(row * channels + c, count, stride=channels)
        for t in range(cols // LANES):
            ext[t, at, :] = jnp.maximum(own[c, rows, t * LANES : (t + 1) * LANES], 0.0)
        for t, value in enumerate(near_columns(around, c, rows)):
            ext[cols // LANES + t, at, :] = jnp.maximum(value, 0.0)


def filter_columns(ext, table, cols, coef):
    tiles, main = cols // LANES, 2 * NDB * LANES
    coef[...] = dot3(halves(side_by_side(ext, range(tiles))), [table[i, :cols, :] for i in range(2)])
    place = lax.axis_index("fcol")
    lane = lax.broadcasted_iota(jnp.int32, (ext.shape[1], LANES), 1)
    right = [place == 0] if ext.shape[0] - tiles == 1 else [False, True]
    for t, last in enumerate(right):
        start = cols + NEAR * t if len(right) > 1 else pl.multiple_of(cols + NEAR * (1 - place), NEAR)
        rows = pl.ds(start, NEAR)
        weights = [jnp.concatenate([table[i, rows, :LANES], table[i, rows, main:]], 1) for i in range(2)]
        part = dot3(halves(ext[tiles + t][:, :NEAR]), weights)
        coef[:, main:] += part[:, LANES:]
        first = jnp.where(last, LANES - 2, 0)
        for tile in range(2 * NDB):
            turn = lax.rem(jnp.where(last, LANES - NEAR, 0) + LANES - NEAR * tile, LANES)
            moved = pltpu.roll(part[:, :LANES], turn, 1)
            coef[:, tile * LANES : (tile + 1) * LANES] += jnp.where((lane >= first) & (lane < first + 2), moved, 0.0)


def coefficients(coef, first, tiles, u_ref, count):
    squares = []
    for tile in tiles:
        lanes = slice((tile - first) * LANES, (tile - first + 1) * LANES)
        taps = strip_row_taps((2, 1), STEP_SPARSE) if tile == 2 * NDB else row_taps(tile % NDB, (2, 1), STEP_SPARSE)
        pairs = [coef[8 * i : 8 * i + 8, lanes] for i in range(count + 4)]
        for j in range(count):
            value = filter_rows(taps, pairs, lambda s: j + 2 + s)
            u_ref[8 * j : 8 * j + 8, tile * LANES : (tile + 1) * LANES] = value
            squares.append(value * value)
    return squares


def pack_half(squares):
    return [pack4(squares[g : g + 4]) for g in range(0, len(squares), 4)]


def pack_strip(squares, item):
    packed = []
    count = len(squares) // 2
    for half in range(2):
        strip = squares[half * count : (half + 1) * count]
        items = [jnp.zeros((8, LANES), F32)] * item
        for g in range(0, count, 4):
            total = strip[g]
            for k in range(1, len(strip[g : g + 4])):
                total = total + pltpu.roll(strip[g + k], STRIP * k, 1)
            items.append(total)
        items += [jnp.zeros((8, LANES), F32)] * (4 - len(items))
        packed.append(pack4(items))
    return packed


def store_halves(packed, keep, send, base=0):
    y = lax.axis_index("chan") % 2
    for i, (a, b) in enumerate(zip(*packed)):
        keep[base + 8 * i : base + 8 * i + 8, :] = jnp.where(y == 0, a, b)
        send[base + 8 * i : base + 8 * i + 8, :] = jnp.where(y == 0, b, a)


def inner_kernel(own, *refs):
    *around, table, u_ref, keep, send, keep_more, send_more, ext, coef = refs
    channels, rows, cols = own.shape
    x = lax.axis_index("frow")
    edge = jnp.zeros((ext.shape[0], 4 * channels, LANES), F32)
    ext[:, pl.ds(pl.multiple_of(x * rows * channels, 16), 4 * channels), :] = edge
    fill_rows(ext, 4 * (1 - x), rows, 0, own, around)
    filter_columns(ext, table, cols, coef)
    count = rows // 2 - 2
    squares = coefficients(coef, 0, range(2 * NDB + 1), u_ref, count)
    store_halves([pack_half(squares[i * NDB * count : (i + 1) * NDB * count]) for i in range(2)], keep, send)
    packed = [[strip] for strip in pack_strip(squares[2 * NDB * count :], 0)]
    for i in range(2):
        for r in range(i * rows // 2, (i + 1) * rows // 2, 8):
            for t in range(cols // LANES):
                total = None
                for c in range(channels):
                    value = STEP_SPARSE * jnp.maximum(own[c, r : r + 8, t * LANES : (t + 1) * LANES], 0.0)
                    total = value * value if total is None else total + value * value
                packed[i].append(total)
    store_halves(packed, keep_more, send_more)


def border_kernel(sides, own, above, keep_more, send_more, *refs):
    around = refs[:sides]
    table, u_ref, keep, send, ext, coef = refs[sides:]
    channels, rows, cols = own.shape
    x, y = lax.axis_index("frow"), lax.axis_index("chan") % 2
    places = Places(rows, cols)
    fill_rows(ext, HALO * x, HALO, pl.multiple_of((1 - x) * (rows - HALO), HALO), own, around)
    for c in range(channels):
        at = pl.ds(HALO * (1 - x) * channels + c, HALO, stride=channels)
        for t in range(cols // LANES):
            start = (c * (cols // LANES) + t) * HALO
            ext[t, at, :] = jnp.maximum(above[start : start + HALO, :], 0.0)
        for t in range(sides):
            start = (channels * (cols // LANES) + t) * HALO
            corner = jnp.maximum(above[start : start + HALO, :], 0.0)
            ext[cols // LANES + t, at, :] = corner if c == 0 else pltpu.roll(corner, LANES - NEAR * c, 1)
    filter_columns(ext, table, cols, coef)
    squares = coefficients(coef, 0, range(2 * NDB + 1), u_ref, 4)
    strips = pack_strip(squares[8 * NDB :], 2)
    needed = []
    for tile in range(2 * NDB):
        rows_here = squares[4 * tile : 4 * tile + 4]
        count = BORDER_ROWS[tile % NDB]
        needed += [jnp.where(x == 0, a, b) for a, b in zip(rows_here[:count], rows_here[4 - count :])]
    middle = len(needed) // 2
    store_halves([pack_half(needed[:middle]), pack_half(needed[middle:])], keep, send, places.border - places.strip)
    keep[: places.border - places.strip, :] = keep_more[...]
    send[: places.border - places.strip, :] = send_more[...]
    keep[:8, :] = keep_more[:8, :] + jnp.where(y == 0, *strips)
    send[:8, :] = send_more[:8, :] + jnp.where(y == 0, *strips[::-1])


def pairing_rounds(order):
    players = list(range(order))
    rounds = []
    for _ in range(order - 1):
        rounds.append([(min(a, b), max(a, b)) for a, b in zip(players[: order // 2], players[: order // 2 - 1 : -1])])
        players = [players[0]] + [players[-1]] + players[1:-1]
    return rounds


def down(values):
    for step in (4, 2, 1):
        values = values + pltpu.roll(values, step, 0)
    return values


def nuclear_kernel(limit, own, other, out, group, mix):
    channels, rows, cols = own.shape
    order = 2 * channels
    y = lax.axis_index("chan") % 2
    for c in range(channels):
        group[y * channels + c] = jnp.maximum(own[c], 0.0)
        group[(1 - y) * channels + c] = jnp.maximum(other[c], 0.0)
    blocks = [(slice(r, r + 8), slice(t, t + LANES)) for r in range(0, rows, 8) for t in range(0, cols, LANES)]
    partial = {}
    for at in blocks:
        held = [group[(c, *at)] for c in range(order)]
        for i in range(order):
            for j in range(i + 1):
                term = held[i] * held[j]
                partial[i, j] = partial[i, j] + term if (i, j) in partial else term
    row_sum = {key: jnp.sum(value, axis=0, keepdims=True) for key, value in partial.items()}
    sub = lax.broadcasted_iota(jnp.int32, (order, LANES), 0)
    turned, vectors, diag = [], [], []
    for j in range(order):
        stacked = jnp.concatenate([row_sum[max(i, j), min(i, j)] for i in range(order)], 0)
        column = jnp.broadcast_to(jnp.sum(stacked, axis=1, keepdims=True), (order, LANES))
        turned.append(column)
        unit = jnp.where(sub == j, F32(1.0), F32(0.0))
        vectors.append(unit)
        diag.append(down(column * unit))

    rounds = pairing_rounds(order)

    def sweep(_, state):
        turned, vectors, diag = (list(part) for part in state)
        for pairs in rounds:
            for p, q in pairs:
                coupling = down(vectors[p] * turned[q])
                spread = diag[q] - diag[p]
                square = spread * spread + 4.0 * coupling * coupling
                positive = square > 0.0
                inverse = jnp.where(positive, lax.rsqrt(jnp.where(positive, square, 1.0)), 0.0)
                cosine2 = jnp.where(positive, 0.5 + 0.5 * jnp.abs(spread) * inverse, 1.0)
                other = lax.rsqrt(cosine2)
                c = cosine2 * other
                s = jnp.where(spread >= 0.0, coupling, -coupling) * inverse * other
                shift = s * other * coupling
                diag[p], diag[q] = diag[p] - shift, diag[q] + shift
                turned[p], turned[q] = c * turned[p] - s * turned[q], s * turned[p] + c * turned[q]
                vectors[p], vectors[q] = c * vectors[p] - s * vectors[q], s * vectors[p] + c * vectors[q]
        return tuple(turned), tuple(vectors), tuple(diag)

    turned, vectors, _ = lax.fori_loop(0, JACOBI_SWEEPS, sweep, (tuple(turned), tuple(vectors), tuple(diag)))
    weighted = []
    for j in range(order):
        value = down(vectors[j] * turned[j])
        weighted.append(vectors[j] * (limit / jnp.maximum(jnp.sqrt(jnp.maximum(value, 0.0)), limit)))
    for k in range(order):
        total = None
        for j in range(order):
            term = weighted[j] * jnp.broadcast_to(vectors[j][k : k + 1, :], (order, LANES))
            total = term if total is None else total + term
        mix[k] = total
    for i in range(channels):
        row = [jnp.broadcast_to(mix[k, pl.ds(y * channels + i, 1), :], (order, LANES)) for k in range(order)]
        for at in blocks:
            total = None
            for k in range(order):
                term = row[k] * group[(k, *at)]
                total = term if total is None else total + term
            out[(i, *at)] = total


def scales(limit, norms):
    return limit * lax.rsqrt(jnp.maximum(norms, limit * limit))


def widen(scale, at, item):
    sub = lax.broadcasted_iota(jnp.int32, (8, LANES), 0)
    first = jnp.broadcast_to(scale[at + item : at + item + 1, :], (8, LANES))
    second = jnp.broadcast_to(scale[at + 4 + item : at + 5 + item, :], (8, LANES))
    return jnp.where(sub < 4, first, second)


def spread_rows(inner, border, taps, spread, lanes):
    x = lax.axis_index("frow")
    empty = jnp.zeros((8, LANES), F32)
    count = len(inner)
    upper = [empty, empty, *inner, *border]
    lower = [*border, *inner, empty, empty]
    padded = [jnp.where(x == 0, a, b) for a, b in zip(upper, lower)]
    for i in range(count + 2):
        spread[8 * i : 8 * i + 8, lanes] = filter_rows(taps, padded, lambda s: i + 2 - s)


class Places:
    def __init__(self, rows, cols):
        self.inner = rows // 2 - 2
        self.strip = 2 * NDB * self.inner
        self.dirac = self.strip + 8
        self.border = self.dirac + rows * cols // LANES // 2
        self.all = self.border + 2 * sum(BORDER_ROWS)


def half_duals(places, half, scale, u_inner, u_border, spread):
    x = lax.axis_index("frow")
    for family in range(NDB):
        if isinstance(half, int):
            lanes = slice((half * NDB + family) * LANES, (half * NDB + family + 1) * LANES)
        else:
            lanes = pl.ds(pl.multiple_of((half * NDB + family) * LANES, LANES), LANES)
        count = places.inner
        factors = [widen(scale, 8 * ((family * count + j) // 4), (family * count + j) % 4) for j in range(count)]
        inner = [u_inner[8 * j : 8 * j + 8, lanes] * factors[j] for j in range(count)]
        first, count = sum(BORDER_ROWS[:family]), BORDER_ROWS[family]
        factors = [widen(scale, places.border + 8 * (k // 4), k % 4) for k in range(first, first + count)]
        spare = [jnp.zeros((8, LANES), F32)] * (4 - count)
        factors = [jnp.where(x == 0, a, b) for a, b in zip(factors + spare, spare + factors)] if spare else factors
        duals = inner, [u_border[8 * j : 8 * j + 8, lanes] * factors[j] for j in range(4)]
        spread_rows(*duals, row_taps(family, (1, 2), 1.0), spread, slice(family * LANES, (family + 1) * LANES))


def first_kernel(limit, raw, density, nuclear, u_inner, u_border, mine, table, step, spread, scale):
    channels, rows, cols = raw.shape
    y = lax.axis_index("chan") % 2
    scale[...] = scales(limit, mine[...])
    half_duals(Places(rows, cols), y, scale, u_inner, u_border, spread)
    lanes = pl.ds(pl.multiple_of(y * NDB * LANES, NDB * LANES), NDB * LANES)
    result = dot3(halves(spread[...]), [table[i, :cols, lanes] for i in range(2)], ((1,), (1,)))
    for t in range(cols // LANES):
        step[cols // LANES + t] = result[:, t * LANES : (t + 1) * LANES]
    for c in range(channels):
        for t in range(cols // LANES):
            lanes = slice(t * LANES, (t + 1) * LANES)
            estimate = jnp.maximum(raw[c, :, lanes], 0.0)
            step[t, c * rows : (c + 1) * rows, :] = density[c, :, lanes] * estimate - raw[c, :, lanes] + nuclear[c, :, lanes]


def second_kernel(limit, raw, step, u_inner, u_border, mine, theirs, table, out, spread, image, scale):
    channels, rows, cols = raw.shape
    y = lax.axis_index("chan") % 2
    places = Places(rows, cols)
    both = slice(places.strip, places.border)
    scale[y, both, :] = scales(limit, mine[both, :])
    scale[1 - y] = scales(limit, theirs[...])
    half_duals(places, 1 - y, scale.at[1 - y], u_inner, u_border, spread)
    main = 2 * NDB * LANES
    duals = []
    for ref, item, count in ((u_inner, 0, places.inner), (u_border, 2, 4)):
        rolled = []
        for j in range(count):
            half, k = divmod(j, count // 2)
            factor = widen(scale.at[half], places.strip, item + k // 4)
            factor = factor if k % 4 == 0 else pltpu.roll(factor, LANES - STRIP * (k % 4), 1)
            rolled.append(ref[8 * j : 8 * j + 8, main:] * factor)
        duals.append(rolled)
    spread_rows(*duals, strip_row_taps((1, 2), 1.0), spread, slice(NDB * LANES, (NDB + 1) * LANES))
    lanes = pl.ds(pl.multiple_of((1 - y) * NDB * LANES, NDB * LANES), NDB * LANES)
    left = halves(spread[...])
    right = [jnp.concatenate([table[i, :cols, lanes], table[i, :cols, main:]], 1) for i in range(2)]
    result = dot3(left, right, ((1,), (1,)))
    for t in range(cols // LANES):
        image[t] = result[:, t * LANES : (t + 1) * LANES] + step[cols // LANES + t]
    for c in range(channels):
        for r in range(0, rows, 8):
            for t in range(cols // LANES):
                lanes = slice(t * LANES, (t + 1) * LANES)
                half, inside = divmod(r, rows // 2)
                at = places.dirac + 8 * (inside // 8 * (cols // LANES) + t)
                estimate = jnp.maximum(raw[c, r : r + 8, lanes], 0.0)
                dual = STEP_SPARSE * estimate * scale[half, at : at + 8, :]
                synthesis = dual + image[t, pl.ds(r * channels + c, 8, stride=channels), :]
                total = step[t, c * rows + r : c * rows + r + 8, :] + synthesis
                out[c, r : r + 8, lanes] = jnp.maximum(estimate - STEP_PRIMAL * total, 0.0)


def fixed_taps(family, band, index):
    total = jnp.zeros(index.shape, F32)
    for k, tap in enumerate(band_taps(family)[band]):
        total = jnp.where(index == k, F32(tap), total)
    return total


def hold_kernel(dirty, own, table):
    own[...] = dirty[...]
    cols = dirty.shape[2]
    blocks = cols // NEAR
    rows = {block: block * NEAR for block in range(blocks)} | {-1: cols, blocks: cols + NEAR}
    row = lax.broadcasted_iota(jnp.int32, (NEAR, LANES), 0)
    lane = lax.broadcasted_iota(jnp.int32, (NEAR, LANES), 1)

    def put(block, tile, value):
        at, lanes = slice(rows[block], rows[block] + NEAR), slice(tile * LANES, (tile + 1) * LANES)
        top = value.astype(BF16)
        table[0, at, lanes] = top
        table[1, at, lanes] = (value - top.astype(F32)).astype(BF16)

    pairs = [(f, b) for b in range(2) for f in range(NDB)]
    for tile, (f, b) in enumerate(pairs):
        base = fixed_taps(f, b, row - 2 * (lane - 2) + len(DAUBECHIES[f]) // 2 - 1)
        for block in range(blocks):
            value = pltpu.roll(base, (block * NEAR // 2 - 2) % LANES, 1)
            if block == 0:
                value = jnp.where(lane < LANES // 2, value, 0.0)
            if block == blocks - 1:
                value = jnp.where(lane < LANES // 2, 0.0, value)
            put(block, tile, value)

    def chosen(block, position, tile_of):
        value = jnp.zeros((NEAR, LANES), F32)
        for tile, (f, b) in enumerate(pairs):
            part = fixed_taps(f, b, row + block * NEAR - 2 * position + len(DAUBECHIES[f]) // 2 - 1)
            value = jnp.where(tile_of == tile, part, value)
        return value

    column = lane % 4
    position = jnp.where(column < 2, column - 2, column + cols // 2 - 2)
    for block in rows:
        inside = block in (-1, 0, blocks - 1, blocks)
        put(block, len(pairs), chosen(block, position, lane // 4) if inside else jnp.zeros((NEAR, LANES), F32))
    column = lane % NEAR
    position = jnp.where(column < NEAR // 2, column, column + cols // 2 - NEAR)
    for block in (-1, blocks):
        put(block, 0, chosen(block, position, lane // NEAR))


def rows_kernel(own, *refs):
    *around, edge = refs
    channels, rows, cols = own.shape
    start = pl.ds(pl.multiple_of((1 - lax.axis_index("frow")) * (rows - HALO), HALO), HALO)
    at = 0
    for c in range(channels):
        for t in range(cols // LANES):
            edge[at : at + HALO, :] = own[c, start, t * LANES : (t + 1) * LANES]
            at += HALO
    lane = lax.broadcasted_iota(jnp.int32, (HALO, LANES), 1) // NEAR
    totals = near_columns(around, 0, start)
    for c in range(1, channels):
        parts = near_columns(around, c, start, NEAR * c)
        totals = [jnp.where(lane == c, part, total) for part, total in zip(parts, totals)]
    for total in totals:
        edge[at : at + HALO, :] = total
        at += HALO


def add_kernel(one, two, *refs):
    refs[-1][...] = one[...] + two[...]


def add_parts_kernel(one, two, three, four, out):
    count = one.shape[0]
    out[:count, :] = one[...] + two[...]
    out[count:, :] = three[...] + four[...]


def exchange(values, axis, bit):
    count = lax.axis_size(axis)
    return lax.ppermute(values, axis, [(i, i ^ bit) for i in range(count)])


def vmem(count):
    return [pl.BlockSpec(memory_space=pltpu.VMEM)] * count


def call(kernel, name, shapes, operands, scratch=(), limit=16, later=()):
    many = [jax.ShapeDtypeStruct(shape, F32) if isinstance(shape, tuple) else shape for shape in shapes]
    results = pl.pallas_call(
        kernel,
        name=name,
        out_shape=many,
        in_specs=vmem(len(operands)) + [pl.BlockSpec(memory_space=pl.ANY)] * len(later),
        out_specs=vmem(len(many)),
        scratch_shapes=[pltpu.VMEM(shape, F32) for shape in scratch],
        compiler_params=pltpu.CompilerParams(vmem_limit_bytes=limit * MIB),
    )(*operands, *later)
    return results if len(results) > 1 else results[0]


def from_neighbours(values):
    facets = lax.axis_size("fcol")
    if facets == 2:
        return [exchange(values, "fcol", 1)]
    return [
        lax.ppermute(values, "fcol", [(i, i + 1) for i in range(facets - 1)]),
        lax.ppermute(values, "fcol", [(i + 1, i) for i in range(facets - 1)]),
    ]


def on_device(dirty_image, density):
    channels, rows, cols = dirty_image.shape
    facets, chans = lax.axis_size("fcol"), lax.axis_size("chan")
    nuclear_limit = math.sqrt(rows * cols)
    sparse_limit = SPARSE_SCALE * math.sqrt(channels * chans)
    sides = 1 if facets == 2 else 2
    places, tiles = Places(rows, cols), 2 * NDB + 1
    lane_tiles = cols // LANES + sides

    around = from_neighbours(dirty_image)
    near = jax.ShapeDtypeStruct((2, cols + 2 * NEAR, tiles * LANES), BF16)
    own, near = call(hold_kernel, "hold", [dirty_image.shape, near], [dirty_image])
    edge = call(rows_kernel, "rows", [((channels * (cols // LANES) + sides) * HALO, LANES)], [own, *around])
    above = exchange(edge, "frow", 1)
    main, more = (places.strip, LANES), (places.border - places.strip, LANES)
    u_inner, keep, send, keep_more, send_more = call(
        inner_kernel,
        "inner",
        [(8 * places.inner, tiles * LANES), main, main, more, more],
        [own, *around, near],
        [(lane_tiles, 8 * (places.inner + 4), LANES), (8 * (places.inner + 4), tiles * LANES)],
        24,
    )
    received = exchange(send, "chan", 1)
    u_border, keep_more, send_more = call(
        lambda *refs: border_kernel(sides, *refs),
        "border",
        [(8 * 4, tiles * LANES)] + [(places.all - places.strip, LANES)] * 2,
        [own, above, keep_more, send_more, *around, near],
        [(lane_tiles, 8 * 8, LANES), (8 * 8, tiles * LANES)],
        24,
    )
    received_more = exchange(send_more, "chan", 1)
    total = call(add_parts_kernel, "add", [(places.all, LANES)], [keep, received, keep_more, received_more])
    other = exchange(own, "chan", 1)
    nuclear = call(
        lambda *refs: nuclear_kernel(nuclear_limit, *refs),
        "nuclear",
        [dirty_image.shape],
        [own, other],
        [(2 * channels, rows, cols), (2 * channels, 2 * channels, LANES)],
    )
    bit = 2
    while bit < chans:
        received = exchange(total, "chan", bit)
        total = call(add_kernel, "add", [(places.all, LANES)], [total, received])
        bit *= 2
    theirs = exchange(total, "chan", 1)
    step = call(
        lambda *refs: first_kernel(sparse_limit, *refs),
        "first",
        [(2 * cols // LANES, channels * rows, LANES)],
        [own, density, nuclear, u_inner, u_border, total, near],
        [(4 * rows, NDB * LANES), (places.all, LANES)],
        24,
    )
    return call(
        lambda *refs: second_kernel(sparse_limit, *refs),
        "second",
        [dirty_image.shape],
        [own, step, u_inner, u_border, total, theirs, near],
        [(4 * rows, (NDB + 1) * LANES), (cols // LANES, 4 * rows, LANES), (2, places.all, LANES)],
        24,
    )


def solution(mesh):
    return jax.shard_map(
        on_device,
        mesh=mesh,
        in_specs=(P("chan", "frow", "fcol"), P("chan", "frow", "fcol")),
        out_specs=P("chan", "frow", "fcol"),
        check_vma=False,
    )
```

```python
import math

import jax
import jax.numpy as jnp
from jax import lax
from jax.experimental import pallas as pl
from jax.experimental.pallas import tpu as pltpu
from jax.sharding import PartitionSpec as P

DAUBECHIES = (
    (0.7071067811865476, 0.7071067811865476),
    (0.48296291314469025, 0.836516303737469, 0.22414386804185735, -0.12940952255092145),
    (
        0.3326705529509569,
        0.8068915093133388,
        0.4598775021193313,
        -0.13501102001039084,
        -0.08544127388224149,
        0.035226291882100656,
    ),
    (
        0.23037781330885523,
        0.7148465705525415,
        0.6308807679295904,
        -0.02798376941698385,
        -0.18703481171888114,
        0.030841381835986965,
        0.032883011666982945,
        -0.010597401784997278,
    ),
)
NDB = len(DAUBECHIES)
JACOBI_SWEEPS = 6
STEP_PRIMAL = 0.2
STEP_SPARSE = 0.5
SPARSE_SCALE = 0.5
LANES = 128
BORDER_ROWS = [2 + len(taps) // 4 for taps in DAUBECHIES]
STRIP = 32
NEAR = 16
HALO = 8
MIB = 1 << 20
F32 = jnp.float32
BF16 = jnp.bfloat16


def band_taps(family):
    low = DAUBECHIES[family]
    high = [(-1.0) ** k * low[len(low) - 1 - k] for k in range(len(low))]
    return low, high


def phase_taps(family):
    low, high = band_taps(family)
    offset = len(low) // 2 - 1
    table = {}
    for k in range(len(low)):
        s, odd = divmod(k - offset, 2)
        entry = table.setdefault(s, [0.0, 0.0, 0.0, 0.0])
        entry[odd] = low[k]
        entry[2 + odd] = high[k]
    return table


def halves(values):
    top = values.astype(BF16)
    return top, (values - top.astype(F32)).astype(BF16)


def dot3(left, right):
    def dot(one, two):
        return jnp.dot(one, two, preferred_element_type=F32)

    count = left[0].shape[0]
    both = dot(jnp.concatenate(left, 0), right[0])
    return both[:count] + (both[count:] + dot(left[0], right[1]))


def side_by_side(ref, tiles):
    return jnp.concatenate([ref[t] for t in tiles], 1)


def swap_halves(values):
    return pltpu.roll(values, 4, 0)


def sublane_taps(first, second):
    rows = lax.broadcasted_iota(jnp.int32, (8, LANES), 0)
    return jnp.where(rows < 4, F32(first), F32(second))


def strip_taps(pick_first, pick_second, s):
    family = lax.broadcasted_iota(jnp.int32, (8, LANES), 1) // 4 % 4
    total = jnp.zeros((8, LANES), F32)
    for f in range(NDB):
        entry = phase_taps(f).get(s)
        if entry is not None:
            total = jnp.where(family == f, sublane_taps(entry[pick_first], entry[pick_second]), total)
    return total


def row_taps(family, cross, scale):
    table = phase_taps(family)
    return {s: (sublane_taps(e[0] * scale, e[3] * scale), sublane_taps(e[cross[0]] * scale, e[cross[1]] * scale)) for s, e in table.items()}


def strip_row_taps(cross, scale):
    column = lax.broadcasted_iota(jnp.int32, (8, LANES), 1) % 4
    place, facets = lax.axis_index("fcol"), lax.axis_size("fcol")
    kept = jnp.where(column < 2, jnp.where(place > 0, F32(scale), F32(0.0)), jnp.where(place < facets - 1, F32(scale), F32(0.0)))
    return {s: (strip_taps(0, 3, s) * kept, strip_taps(*cross, s) * kept) for s in range(-2, 3)}


def filter_rows(taps, pairs, at):
    direct = crossed = None
    for s, (d, e) in taps.items():
        source = pairs[at(s)]
        direct = d * source if direct is None else direct + d * source
        crossed = e * source if crossed is None else crossed + e * source
    return direct + swap_halves(crossed)


def pack4(items):
    rows = lax.broadcasted_iota(jnp.int32, (8, LANES), 0)

    def merge(a, b, step):
        keep = rows % (2 * step) < step
        return jnp.where(keep, a, pltpu.roll(b, step, 0)) + jnp.where(keep, pltpu.roll(a, 8 - step, 0), b)

    return merge(merge(items[0], items[1], 1), merge(items[2], items[3], 1), 2)


def near_columns(sources, c, at, lane=0):
    def last(ref):
        return pltpu.roll(ref[c, at, ref.shape[2] - LANES :], lane + NEAR, 1)

    def first(ref):
        return pltpu.roll(ref[c, at, :LANES], lane, 1) if lane else ref[c, at, :LANES]

    if len(sources) > 1:
        return [last(sources[0]), first(sources[1])]
    place = lax.axis_index("fcol")
    start = pl.multiple_of(place * (sources[0].shape[2] - LANES), LANES)
    return [pltpu.roll(sources[0][c, at, pl.ds(start, LANES)], lane + NEAR * place, 1)]


def fill_rows(ext, row, count, start, own, around):
    channels, _, cols = own.shape
    rows = pl.ds(start, count)
    for c in range(channels):
        at = pl.ds(row * channels + c, count, stride=channels)
        for t in range(cols // LANES):
            ext[t, at, :] = jnp.maximum(own[c, rows, t * LANES : (t + 1) * LANES], 0.0)
        for t, value in enumerate(near_columns(around, c, rows)):
            ext[cols // LANES + t, at, :] = jnp.maximum(value, 0.0)


def filter_columns(ext, table, cols, coef):
    tiles, main = cols // LANES, 2 * NDB * LANES
    coef[...] = dot3(halves(side_by_side(ext, range(tiles))), [table[i, :cols, :] for i in range(2)])
    place = lax.axis_index("fcol")
    lane = lax.broadcasted_iota(jnp.int32, (ext.shape[1], LANES), 1)
    right = [place == 0] if ext.shape[0] - tiles == 1 else [False, True]
    for t, last in enumerate(right):
        start = cols + NEAR * t if len(right) > 1 else pl.multiple_of(cols + NEAR * (1 - place), NEAR)
        rows = pl.ds(start, NEAR)
        weights = [jnp.concatenate([table[i, rows, :LANES], table[i, rows, main:]], 1) for i in range(2)]
        part = dot3(halves(ext[tiles + t][:, :NEAR]), weights)
        coef[:, main:] += part[:, LANES:]
        first = jnp.where(last, LANES - 2, 0)
        for tile in range(2 * NDB):
            turn = lax.rem(jnp.where(last, LANES - NEAR, 0) + LANES - NEAR * tile, LANES)
            moved = pltpu.roll(part[:, :LANES], turn, 1)
            coef[:, tile * LANES : (tile + 1) * LANES] += jnp.where((lane >= first) & (lane < first + 2), moved, 0.0)


def coefficients(coef, first, tiles, u_ref, count):
    squares = []
    for tile in tiles:
        lanes = slice((tile - first) * LANES, (tile - first + 1) * LANES)
        taps = strip_row_taps((2, 1), STEP_SPARSE) if tile == 2 * NDB else row_taps(tile % NDB, (2, 1), STEP_SPARSE)
        pairs = [coef[8 * i : 8 * i + 8, lanes] for i in range(count + 4)]
        for j in range(count):
            value = filter_rows(taps, pairs, lambda s: j + 2 + s)
            u_ref[8 * j : 8 * j + 8, tile * LANES : (tile + 1) * LANES] = value
            squares.append(value * value)
    return squares


def pack_half(squares):
    return [pack4(squares[g : g + 4]) for g in range(0, len(squares), 4)]


def pack_strip(squares, item):
    packed = []
    count = len(squares) // 2
    for half in range(2):
        strip = squares[half * count : (half + 1) * count]
        items = [jnp.zeros((8, LANES), F32)] * item
        for g in range(0, count, 4):
            total = strip[g]
            for k in range(1, len(strip[g : g + 4])):
                total = total + pltpu.roll(strip[g + k], STRIP * k, 1)
            items.append(total)
        items += [jnp.zeros((8, LANES), F32)] * (4 - len(items))
        packed.append(pack4(items))
    return packed


def store_halves(packed, keep, send, base=0):
    y = lax.axis_index("chan") % 2
    for i, (a, b) in enumerate(zip(*packed)):
        keep[base + 8 * i : base + 8 * i + 8, :] = jnp.where(y == 0, a, b)
        send[base + 8 * i : base + 8 * i + 8, :] = jnp.where(y == 0, b, a)


def inner_kernel(own, *refs):
    *around, table, u_ref, keep, send, keep_more, send_more, ext, coef = refs
    channels, rows, cols = own.shape
    x = lax.axis_index("frow")
    edge = jnp.zeros((ext.shape[0], 4 * channels, LANES), F32)
    ext[:, pl.ds(pl.multiple_of(x * rows * channels, 16), 4 * channels), :] = edge
    fill_rows(ext, 4 * (1 - x), rows, 0, own, around)
    filter_columns(ext, table, cols, coef)
    count = rows // 2 - 2
    squares = coefficients(coef, 0, range(2 * NDB + 1), u_ref, count)
    store_halves([pack_half(squares[i * NDB * count : (i + 1) * NDB * count]) for i in range(2)], keep, send)
    packed = [[strip] for strip in pack_strip(squares[2 * NDB * count :], 0)]
    for i in range(2):
        for r in range(i * rows // 2, (i + 1) * rows // 2, 8):
            for t in range(cols // LANES):
                total = None
                for c in range(channels):
                    value = STEP_SPARSE * jnp.maximum(own[c, r : r + 8, t * LANES : (t + 1) * LANES], 0.0)
                    total = value * value if total is None else total + value * value
                packed[i].append(total)
    store_halves(packed, keep_more, send_more)


def border_kernel(sides, own, above, keep_more, send_more, *refs):
    around = refs[:sides]
    table, u_ref, keep, send, ext, coef = refs[sides:]
    channels, rows, cols = own.shape
    x, y = lax.axis_index("frow"), lax.axis_index("chan") % 2
    places = Places(rows, cols)
    fill_rows(ext, HALO * x, HALO, pl.multiple_of((1 - x) * (rows - HALO), HALO), own, around)
    for c in range(channels):
        at = pl.ds(HALO * (1 - x) * channels + c, HALO, stride=channels)
        for t in range(cols // LANES):
            start = (c * (cols // LANES) + t) * HALO
            ext[t, at, :] = jnp.maximum(above[start : start + HALO, :], 0.0)
        for t in range(sides):
            start = (channels * (cols // LANES) + t) * HALO
            corner = jnp.maximum(above[start : start + HALO, :], 0.0)
            ext[cols // LANES + t, at, :] = corner if c == 0 else pltpu.roll(corner, LANES - NEAR * c, 1)
    filter_columns(ext, table, cols, coef)
    squares = coefficients(coef, 0, range(2 * NDB + 1), u_ref, 4)
    strips = pack_strip(squares[8 * NDB :], 2)
    needed = []
    for tile in range(2 * NDB):
        rows_here = squares[4 * tile : 4 * tile + 4]
        count = BORDER_ROWS[tile % NDB]
        needed += [jnp.where(x == 0, a, b) for a, b in zip(rows_here[:count], rows_here[4 - count :])]
    middle = len(needed) // 2
    store_halves([pack_half(needed[:middle]), pack_half(needed[middle:])], keep, send, places.border - places.strip)
    keep[: places.border - places.strip, :] = keep_more[...]
    send[: places.border - places.strip, :] = send_more[...]
    keep[:8, :] = keep_more[:8, :] + jnp.where(y == 0, *strips)
    send[:8, :] = send_more[:8, :] + jnp.where(y == 0, *strips[::-1])


def pairing_rounds(order):
    players = list(range(order))
    rounds = []
    for _ in range(order - 1):
        rounds.append([(min(a, b), max(a, b)) for a, b in zip(players[: order // 2], players[: order // 2 - 1 : -1])])
        players = [players[0]] + [players[-1]] + players[1:-1]
    return rounds


def down(values):
    for step in (4, 2, 1):
        values = values + pltpu.roll(values, step, 0)
    return values


def nuclear_kernel(limit, own, other, out, group, mix):
    channels, rows, cols = own.shape
    order = 2 * channels
    y = lax.axis_index("chan") % 2
    for c in range(channels):
        group[y * channels + c] = jnp.maximum(own[c], 0.0)
        group[(1 - y) * channels + c] = jnp.maximum(other[c], 0.0)
    blocks = [(slice(r, r + 8), slice(t, t + LANES)) for r in range(0, rows, 8) for t in range(0, cols, LANES)]
    partial = {}
    for at in blocks:
        held = [group[(c, *at)] for c in range(order)]
        for i in range(order):
            for j in range(i + 1):
                term = held[i] * held[j]
                partial[i, j] = partial[i, j] + term if (i, j) in partial else term
    row_sum = {key: jnp.sum(value, axis=0, keepdims=True) for key, value in partial.items()}
    sub = lax.broadcasted_iota(jnp.int32, (order, LANES), 0)
    turned, vectors, diag = [], [], []
    for j in range(order):
        stacked = jnp.concatenate([row_sum[max(i, j), min(i, j)] for i in range(order)], 0)
        column = jnp.broadcast_to(jnp.sum(stacked, axis=1, keepdims=True), (order, LANES))
        turned.append(column)
        unit = jnp.where(sub == j, F32(1.0), F32(0.0))
        vectors.append(unit)
        diag.append(down(column * unit))

    rounds = pairing_rounds(order)

    def sweep(_, state):
        turned, vectors, diag = (list(part) for part in state)
        for pairs in rounds:
            for p, q in pairs:
                coupling = down(vectors[p] * turned[q])
                spread = diag[q] - diag[p]
                square = spread * spread + 4.0 * coupling * coupling
                positive = square > 0.0
                inverse = jnp.where(positive, lax.rsqrt(jnp.where(positive, square, 1.0)), 0.0)
                cosine2 = jnp.where(positive, 0.5 + 0.5 * jnp.abs(spread) * inverse, 1.0)
                other = lax.rsqrt(cosine2)
                c = cosine2 * other
                s = jnp.where(spread >= 0.0, coupling, -coupling) * inverse * other
                shift = s * other * coupling
                diag[p], diag[q] = diag[p] - shift, diag[q] + shift
                turned[p], turned[q] = c * turned[p] - s * turned[q], s * turned[p] + c * turned[q]
                vectors[p], vectors[q] = c * vectors[p] - s * vectors[q], s * vectors[p] + c * vectors[q]
        return tuple(turned), tuple(vectors), tuple(diag)

    turned, vectors, _ = lax.fori_loop(0, JACOBI_SWEEPS, sweep, (tuple(turned), tuple(vectors), tuple(diag)))
    weighted = []
    for j in range(order):
        value = down(vectors[j] * turned[j])
        weighted.append(vectors[j] * (limit / jnp.maximum(jnp.sqrt(jnp.maximum(value, 0.0)), limit)))
    for k in range(order):
        total = None
        for j in range(order):
            term = weighted[j] * jnp.broadcast_to(vectors[j][k : k + 1, :], (order, LANES))
            total = term if total is None else total + term
        mix[k] = total
    for i in range(channels):
        row = [jnp.broadcast_to(mix[k, pl.ds(y * channels + i, 1), :], (order, LANES)) for k in range(order)]
        for at in blocks:
            total = None
            for k in range(order):
                term = row[k] * group[(k, *at)]
                total = term if total is None else total + term
            out[(i, *at)] = total


def scales(limit, norms):
    return limit * lax.rsqrt(jnp.maximum(norms, limit * limit))


def widen(scale, at, item):
    sub = lax.broadcasted_iota(jnp.int32, (8, LANES), 0)
    first = jnp.broadcast_to(scale[at + item : at + item + 1, :], (8, LANES))
    second = jnp.broadcast_to(scale[at + 4 + item : at + 5 + item, :], (8, LANES))
    return jnp.where(sub < 4, first, second)


def spread_rows(inner, border, taps, spread, lanes):
    x = lax.axis_index("frow")
    empty = jnp.zeros((8, LANES), F32)
    count = len(inner)
    upper = [empty, empty, *inner, *border]
    lower = [*border, *inner, empty, empty]
    padded = [jnp.where(x == 0, a, b) for a, b in zip(upper, lower)]
    for i in range(count + 2):
        spread[8 * i : 8 * i + 8, lanes] = filter_rows(taps, padded, lambda s: i + 2 - s)


class Places:
    def __init__(self, rows, cols):
        self.inner = rows // 2 - 2
        self.strip = 2 * NDB * self.inner
        self.dirac = self.strip + 8
        self.border = self.dirac + rows * cols // LANES // 2
        self.all = self.border + 2 * sum(BORDER_ROWS)


def half_duals(places, half, scale, u_inner, u_border, spread):
    x = lax.axis_index("frow")
    for family in range(NDB):
        if isinstance(half, int):
            lanes = slice((half * NDB + family) * LANES, (half * NDB + family + 1) * LANES)
        else:
            lanes = pl.ds(pl.multiple_of((half * NDB + family) * LANES, LANES), LANES)
        count = places.inner
        factors = [widen(scale, 8 * ((family * count + j) // 4), (family * count + j) % 4) for j in range(count)]
        inner = [u_inner[8 * j : 8 * j + 8, lanes] * factors[j] for j in range(count)]
        first, count = sum(BORDER_ROWS[:family]), BORDER_ROWS[family]
        factors = [widen(scale, places.border + 8 * (k // 4), k % 4) for k in range(first, first + count)]
        spare = [jnp.zeros((8, LANES), F32)] * (4 - count)
        factors = [jnp.where(x == 0, a, b) for a, b in zip(factors + spare, spare + factors)] if spare else factors
        duals = inner, [u_border[8 * j : 8 * j + 8, lanes] * factors[j] for j in range(4)]
        spread_rows(*duals, row_taps(family, (1, 2), 1.0), spread, slice(family * LANES, (family + 1) * LANES))


def first_kernel(limit, raw, density, nuclear, u_inner, u_border, mine, table, step, spread, scale):
    channels, rows, cols = raw.shape
    y = lax.axis_index("chan") % 2
    scale[...] = scales(limit, mine[...])
    half_duals(Places(rows, cols), y, scale, u_inner, u_border, spread)
    lanes = pl.ds(pl.multiple_of(y * NDB * LANES, NDB * LANES), NDB * LANES)
    result = dot3(halves(spread[...]), [table[i, lanes, :] for i in range(2)])
    for t in range(cols // LANES):
        step[cols // LANES + t] = result[:, t * LANES : (t + 1) * LANES]
    for c in range(channels):
        for t in range(cols // LANES):
            lanes = slice(t * LANES, (t + 1) * LANES)
            estimate = jnp.maximum(raw[c, :, lanes], 0.0)
            step[t, c * rows : (c + 1) * rows, :] = density[c, :, lanes] * estimate - raw[c, :, lanes] + nuclear[c, :, lanes]


def second_kernel(limit, raw, step, u_inner, u_border, mine, theirs, table, out, spread, image, scale):
    channels, rows, cols = raw.shape
    y = lax.axis_index("chan") % 2
    places = Places(rows, cols)
    both = slice(places.strip, places.border)
    scale[y, both, :] = scales(limit, mine[both, :])
    scale[1 - y] = scales(limit, theirs[...])
    half_duals(places, 1 - y, scale.at[1 - y], u_inner, u_border, spread)
    main = 2 * NDB * LANES
    duals = []
    for ref, item, count in ((u_inner, 0, places.inner), (u_border, 2, 4)):
        rolled = []
        for j in range(count):
            half, k = divmod(j, count // 2)
            factor = widen(scale.at[half], places.strip, item + k // 4)
            factor = factor if k % 4 == 0 else pltpu.roll(factor, LANES - STRIP * (k % 4), 1)
            rolled.append(ref[8 * j : 8 * j + 8, main:] * factor)
        duals.append(rolled)
    spread_rows(*duals, strip_row_taps((1, 2), 1.0), spread, slice(NDB * LANES, (NDB + 1) * LANES))
    lanes = pl.ds(pl.multiple_of((1 - y) * NDB * LANES, NDB * LANES), NDB * LANES)
    left = halves(spread[...])
    right = [jnp.concatenate([table[i, lanes, :], table[i, main:, :]], 0) for i in range(2)]
    result = dot3(left, right)
    for t in range(cols // LANES):
        image[t] = result[:, t * LANES : (t + 1) * LANES] + step[cols // LANES + t]
    for c in range(channels):
        for r in range(0, rows, 8):
            for t in range(cols // LANES):
                lanes = slice(t * LANES, (t + 1) * LANES)
                half, inside = divmod(r, rows // 2)
                at = places.dirac + 8 * (inside // 8 * (cols // LANES) + t)
                estimate = jnp.maximum(raw[c, r : r + 8, lanes], 0.0)
                dual = STEP_SPARSE * estimate * scale[half, at : at + 8, :]
                synthesis = dual + image[t, pl.ds(r * channels + c, 8, stride=channels), :]
                total = step[t, c * rows + r : c * rows + r + 8, :] + synthesis
                out[c, r : r + 8, lanes] = jnp.maximum(estimate - STEP_PRIMAL * total, 0.0)


def fixed_taps(family, band, index):
    total = jnp.zeros(index.shape, F32)
    for k, tap in enumerate(band_taps(family)[band]):
        total = jnp.where(index == k, F32(tap), total)
    return total


def hold_kernel(dirty, own, table):
    own[...] = dirty[...]
    cols = dirty.shape[2]
    blocks = cols // NEAR
    rows = {block: block * NEAR for block in range(blocks)} | {-1: cols, blocks: cols + NEAR}
    row = lax.broadcasted_iota(jnp.int32, (NEAR, LANES), 0)
    lane = lax.broadcasted_iota(jnp.int32, (NEAR, LANES), 1)

    def put(block, tile, value):
        at, lanes = slice(rows[block], rows[block] + NEAR), slice(tile * LANES, (tile + 1) * LANES)
        top = value.astype(BF16)
        table[0, at, lanes] = top
        table[1, at, lanes] = (value - top.astype(F32)).astype(BF16)

    pairs = [(f, b) for b in range(2) for f in range(NDB)]
    for tile, (f, b) in enumerate(pairs):
        base = fixed_taps(f, b, row - 2 * (lane - 2) + len(DAUBECHIES[f]) // 2 - 1)
        for block in range(blocks):
            value = pltpu.roll(base, (block * NEAR // 2 - 2) % LANES, 1)
            if block == 0:
                value = jnp.where(lane < LANES // 2, value, 0.0)
            if block == blocks - 1:
                value = jnp.where(lane < LANES // 2, 0.0, value)
            put(block, tile, value)

    def chosen(block, position, tile_of):
        value = jnp.zeros((NEAR, LANES), F32)
        for tile, (f, b) in enumerate(pairs):
            part = fixed_taps(f, b, row + block * NEAR - 2 * position + len(DAUBECHIES[f]) // 2 - 1)
            value = jnp.where(tile_of == tile, part, value)
        return value

    column = lane % 4
    position = jnp.where(column < 2, column - 2, column + cols // 2 - 2)
    for block in rows:
        inside = block in (-1, 0, blocks - 1, blocks)
        put(block, len(pairs), chosen(block, position, lane // 4) if inside else jnp.zeros((NEAR, LANES), F32))
    column = lane % NEAR
    position = jnp.where(column < NEAR // 2, column, column + cols // 2 - NEAR)
    for block in (-1, blocks):
        put(block, 0, chosen(block, position, lane // NEAR))


def rows_kernel(own, *refs):
    *around, edge = refs
    channels, rows, cols = own.shape
    start = pl.ds(pl.multiple_of((1 - lax.axis_index("frow")) * (rows - HALO), HALO), HALO)
    at = 0
    for c in range(channels):
        for t in range(cols // LANES):
            edge[at : at + HALO, :] = own[c, start, t * LANES : (t + 1) * LANES]
            at += HALO
    lane = lax.broadcasted_iota(jnp.int32, (HALO, LANES), 1) // NEAR
    totals = near_columns(around, 0, start)
    for c in range(1, channels):
        parts = near_columns(around, c, start, NEAR * c)
        totals = [jnp.where(lane == c, part, total) for part, total in zip(parts, totals)]
    for total in totals:
        edge[at : at + HALO, :] = total
        at += HALO


def add_kernel(one, two, *refs):
    refs[-1][...] = one[...] + two[...]


def add_parts_kernel(one, two, three, four, out):
    count = one.shape[0]
    out[:count, :] = one[...] + two[...]
    out[count:, :] = three[...] + four[...]


def turn_kernel(table, out):
    cols = out.shape[2]
    for i in range(2):
        for t in range(0, table.shape[2], LANES):
            out[i, t : t + LANES, :] = table[i, :cols, t : t + LANES].astype(F32).T.astype(BF16)


def exchange(values, axis, bit):
    count = lax.axis_size(axis)
    return lax.ppermute(values, axis, [(i, i ^ bit) for i in range(count)])


def vmem(count):
    return [pl.BlockSpec(memory_space=pltpu.VMEM)] * count


def call(kernel, name, shapes, operands, scratch=(), limit=16, later=()):
    many = [jax.ShapeDtypeStruct(shape, F32) if isinstance(shape, tuple) else shape for shape in shapes]
    results = pl.pallas_call(
        kernel,
        name=name,
        out_shape=many,
        in_specs=vmem(len(operands)) + [pl.BlockSpec(memory_space=pl.ANY)] * len(later),
        out_specs=vmem(len(many)),
        scratch_shapes=[pltpu.VMEM(shape, F32) for shape in scratch],
        compiler_params=pltpu.CompilerParams(vmem_limit_bytes=limit * MIB),
    )(*operands, *later)
    return results if len(results) > 1 else results[0]


def from_neighbours(values):
    facets = lax.axis_size("fcol")
    if facets == 2:
        return [exchange(values, "fcol", 1)]
    return [
        lax.ppermute(values, "fcol", [(i, i + 1) for i in range(facets - 1)]),
        lax.ppermute(values, "fcol", [(i + 1, i) for i in range(facets - 1)]),
    ]


def on_device(dirty_image, density):
    channels, rows, cols = dirty_image.shape
    facets, chans = lax.axis_size("fcol"), lax.axis_size("chan")
    nuclear_limit = math.sqrt(rows * cols)
    sparse_limit = SPARSE_SCALE * math.sqrt(channels * chans)
    sides = 1 if facets == 2 else 2
    places, tiles = Places(rows, cols), 2 * NDB + 1
    lane_tiles = cols // LANES + sides

    around = from_neighbours(dirty_image)
    near = jax.ShapeDtypeStruct((2, cols + 2 * NEAR, tiles * LANES), BF16)
    own, near = call(hold_kernel, "hold", [dirty_image.shape, near], [dirty_image])
    edge = call(rows_kernel, "rows", [((channels * (cols // LANES) + sides) * HALO, LANES)], [own, *around])
    above = exchange(edge, "frow", 1)
    main, more = (places.strip, LANES), (places.border - places.strip, LANES)
    u_inner, keep, send, keep_more, send_more = call(
        inner_kernel,
        "inner",
        [(8 * places.inner, tiles * LANES), main, main, more, more],
        [own, *around, near],
        [(lane_tiles, 8 * (places.inner + 4), LANES), (8 * (places.inner + 4), tiles * LANES)],
        24,
    )
    received = exchange(send, "chan", 1)
    u_border, keep_more, send_more = call(
        lambda *refs: border_kernel(sides, *refs),
        "border",
        [(8 * 4, tiles * LANES)] + [(places.all - places.strip, LANES)] * 2,
        [own, above, keep_more, send_more, *around, near],
        [(lane_tiles, 8 * 8, LANES), (8 * 8, tiles * LANES)],
        24,
    )
    received_more = exchange(send_more, "chan", 1)
    total = call(add_parts_kernel, "add", [(places.all, LANES)], [keep, received, keep_more, received_more])
    other = exchange(own, "chan", 1)
    turned = call(turn_kernel, "turn", [jax.ShapeDtypeStruct((2, tiles * LANES, cols), BF16)], [near])
    nuclear = call(
        lambda *refs: nuclear_kernel(nuclear_limit, *refs),
        "nuclear",
        [dirty_image.shape],
        [own, other],
        [(2 * channels, rows, cols), (2 * channels, 2 * channels, LANES)],
    )
    bit = 2
    while bit < chans:
        received = exchange(total, "chan", bit)
        total = call(add_kernel, "add", [(places.all, LANES)], [total, received])
        bit *= 2
    theirs = exchange(total, "chan", 1)
    step = call(
        lambda *refs: first_kernel(sparse_limit, *refs),
        "first",
        [(2 * cols // LANES, channels * rows, LANES)],
        [own, density, nuclear, u_inner, u_border, total, turned],
        [(4 * rows, NDB * LANES), (places.all, LANES)],
        24,
    )
    return call(
        lambda *refs: second_kernel(sparse_limit, *refs),
        "second",
        [dirty_image.shape],
        [own, step, u_inner, u_border, total, theirs, turned],
        [(4 * rows, (NDB + 1) * LANES), (cols // LANES, 4 * rows, LANES), (2, places.all, LANES)],
        24,
    )


def solution(mesh):
    return jax.shard_map(
        on_device,
        mesh=mesh,
        in_specs=(P("chan", "frow", "fcol"), P("chan", "frow", "fcol")),
        out_specs=P("chan", "frow", "fcol"),
        check_vma=False,
    )
```

```python
import math

import jax
import jax.numpy as jnp
from jax import lax
from jax.experimental import pallas as pl
from jax.experimental.pallas import tpu as pltpu
from jax.sharding import PartitionSpec as P

DAUBECHIES = (
    (0.7071067811865476, 0.7071067811865476),
    (0.48296291314469025, 0.836516303737469, 0.22414386804185735, -0.12940952255092145),
    (
        0.3326705529509569,
        0.8068915093133388,
        0.4598775021193313,
        -0.13501102001039084,
        -0.08544127388224149,
        0.035226291882100656,
    ),
    (
        0.23037781330885523,
        0.7148465705525415,
        0.6308807679295904,
        -0.02798376941698385,
        -0.18703481171888114,
        0.030841381835986965,
        0.032883011666982945,
        -0.010597401784997278,
    ),
)
NDB = len(DAUBECHIES)
JACOBI_SWEEPS = 6
STEP_PRIMAL = 0.2
STEP_SPARSE = 0.5
SPARSE_SCALE = 0.5
LANES = 128
BORDER_ROWS = [2 + len(taps) // 4 for taps in DAUBECHIES]
STRIP = 32
NEAR = 16
HALO = 8
MIB = 1 << 20
F32 = jnp.float32
BF16 = jnp.bfloat16


def band_taps(family):
    low = DAUBECHIES[family]
    high = [(-1.0) ** k * low[len(low) - 1 - k] for k in range(len(low))]
    return low, high


def phase_taps(family):
    low, high = band_taps(family)
    offset = len(low) // 2 - 1
    table = {}
    for k in range(len(low)):
        s, odd = divmod(k - offset, 2)
        entry = table.setdefault(s, [0.0, 0.0, 0.0, 0.0])
        entry[odd] = low[k]
        entry[2 + odd] = high[k]
    return table


def halves(values):
    top = values.astype(BF16)
    return top, (values - top.astype(F32)).astype(BF16)


def dot3(left, right, dims=((1,), (0,))):
    def dot(one, two):
        return lax.dot_general(one, two, (dims, ((), ())), preferred_element_type=F32)

    count = left[0].shape[0]
    both = dot(jnp.concatenate(left, 0), right[0])
    return both[:count] + (both[count:] + dot(left[0], right[1]))


def side_by_side(ref, tiles):
    return jnp.concatenate([ref[t] for t in tiles], 1)


def swap_halves(values):
    return pltpu.roll(values, 4, 0)


def sublane_taps(first, second):
    rows = lax.broadcasted_iota(jnp.int32, (8, LANES), 0)
    return jnp.where(rows < 4, F32(first), F32(second))


def strip_taps(pick_first, pick_second, s):
    family = lax.broadcasted_iota(jnp.int32, (8, LANES), 1) // 4 % 4
    total = jnp.zeros((8, LANES), F32)
    for f in range(NDB):
        entry = phase_taps(f).get(s)
        if entry is not None:
            total = jnp.where(family == f, sublane_taps(entry[pick_first], entry[pick_second]), total)
    return total


def row_taps(family, cross, scale):
    table = phase_taps(family)
    return {s: (sublane_taps(e[0] * scale, e[3] * scale), sublane_taps(e[cross[0]] * scale, e[cross[1]] * scale)) for s, e in table.items()}


def strip_row_taps(cross, scale):
    column = lax.broadcasted_iota(jnp.int32, (8, LANES), 1) % 4
    place, facets = lax.axis_index("fcol"), lax.axis_size("fcol")
    kept = jnp.where(column < 2, jnp.where(place > 0, F32(scale), F32(0.0)), jnp.where(place < facets - 1, F32(scale), F32(0.0)))
    return {s: (strip_taps(0, 3, s) * kept, strip_taps(*cross, s) * kept) for s in range(-2, 3)}


def filter_rows(taps, pairs, at):
    direct = crossed = None
    for s, (d, e) in taps.items():
        source = pairs[at(s)]
        direct = d * source if direct is None else direct + d * source
        crossed = e * source if crossed is None else crossed + e * source
    return direct + swap_halves(crossed)


def pack4(items):
    rows = lax.broadcasted_iota(jnp.int32, (8, LANES), 0)

    def merge(a, b, step):
        keep = rows % (2 * step) < step
        return jnp.where(keep, a, pltpu.roll(b, step, 0)) + jnp.where(keep, pltpu.roll(a, 8 - step, 0), b)

    return merge(merge(items[0], items[1], 1), merge(items[2], items[3], 1), 2)


def near_columns(sources, c, at, lane=0):
    def last(ref):
        return pltpu.roll(ref[c, at, ref.shape[2] - LANES :], lane + NEAR, 1)

    def first(ref):
        return pltpu.roll(ref[c, at, :LANES], lane, 1) if lane else ref[c, at, :LANES]

    if len(sources) > 1:
        return [last(sources[0]), first(sources[1])]
    place = lax.axis_index("fcol")
    start = pl.multiple_of(place * (sources[0].shape[2] - LANES), LANES)
    return [pltpu.roll(sources[0][c, at, pl.ds(start, LANES)], lane + NEAR * place, 1)]


def fill_rows(ext, row, count, start, own, around):
    channels, _, cols = own.shape
    rows = pl.ds(start, count)
    for c in range(channels):
        at = pl.ds(row * channels + c, count, stride=channels)
        for t in range(cols // LANES):
            ext[t, at, :] = jnp.maximum(own[c, rows, t * LANES : (t + 1) * LANES], 0.0)
        for t, value in enumerate(near_columns(around, c, rows)):
            ext[cols // LANES + t, at, :] = jnp.maximum(value, 0.0)


def filter_columns(ext, table, cols, coef):
    tiles, main = cols // LANES, 2 * NDB * LANES
    coef[...] = dot3(halves(side_by_side(ext, range(tiles))), [table[i, :cols, :] for i in range(2)])
    place = lax.axis_index("fcol")
    lane = lax.broadcasted_iota(jnp.int32, (ext.shape[1], LANES), 1)
    right = [place == 0] if ext.shape[0] - tiles == 1 else [False, True]
    for t, last in enumerate(right):
        start = cols + NEAR * t if len(right) > 1 else pl.multiple_of(cols + NEAR * (1 - place), NEAR)
        rows = pl.ds(start, NEAR)
        weights = [jnp.concatenate([table[i, rows, :LANES], table[i, rows, main:]], 1) for i in range(2)]
        part = dot3(halves(ext[tiles + t][:, :NEAR]), weights)
        coef[:, main:] += part[:, LANES:]
        first = jnp.where(last, LANES - 2, 0)
        for tile in range(2 * NDB):
            turn = lax.rem(jnp.where(last, LANES - NEAR, 0) + LANES - NEAR * tile, LANES)
            moved = pltpu.roll(part[:, :LANES], turn, 1)
            coef[:, tile * LANES : (tile + 1) * LANES] += jnp.where((lane >= first) & (lane < first + 2), moved, 0.0)


def coefficients(coef, first, tiles, u_ref, count):
    squares = []
    for tile in tiles:
        lanes = slice((tile - first) * LANES, (tile - first + 1) * LANES)
        taps = strip_row_taps((2, 1), STEP_SPARSE) if tile == 2 * NDB else row_taps(tile % NDB, (2, 1), STEP_SPARSE)
        pairs = [coef[8 * i : 8 * i + 8, lanes] for i in range(count + 4)]
        for j in range(count):
            value = filter_rows(taps, pairs, lambda s: j + 2 + s)
            u_ref[8 * j : 8 * j + 8, tile * LANES : (tile + 1) * LANES] = value
            squares.append(value * value)
    return squares


def pack_half(squares):
    return [pack4(squares[g : g + 4]) for g in range(0, len(squares), 4)]


def pack_strip(squares, item):
    packed = []
    count = len(squares) // 2
    for half in range(2):
        strip = squares[half * count : (half + 1) * count]
        items = [jnp.zeros((8, LANES), F32)] * item
        for g in range(0, count, 4):
            total = strip[g]
            for k in range(1, len(strip[g : g + 4])):
                total = total + pltpu.roll(strip[g + k], STRIP * k, 1)
            items.append(total)
        items += [jnp.zeros((8, LANES), F32)] * (4 - len(items))
        packed.append(pack4(items))
    return packed


def store_halves(packed, keep, send, base=0):
    y = lax.axis_index("chan") % 2
    for i, (a, b) in enumerate(zip(*packed)):
        keep[base + 8 * i : base + 8 * i + 8, :] = jnp.where(y == 0, a, b)
        send[base + 8 * i : base + 8 * i + 8, :] = jnp.where(y == 0, b, a)


def inner_kernel(own, *refs):
    *around, table, u_ref, keep, send, keep_more, send_more, ext, coef = refs
    channels, rows, cols = own.shape
    x = lax.axis_index("frow")
    edge = jnp.zeros((ext.shape[0], 4 * channels, LANES), F32)
    ext[:, pl.ds(pl.multiple_of(x * rows * channels, 16), 4 * channels), :] = edge
    fill_rows(ext, 4 * (1 - x), rows, 0, own, around)
    filter_columns(ext, table, cols, coef)
    count = rows // 2 - 2
    squares = coefficients(coef, 0, range(2 * NDB + 1), u_ref, count)
    store_halves([pack_half(squares[i * NDB * count : (i + 1) * NDB * count]) for i in range(2)], keep, send)
    packed = [[strip] for strip in pack_strip(squares[2 * NDB * count :], 0)]
    for i in range(2):
        for r in range(i * rows // 2, (i + 1) * rows // 2, 8):
            for t in range(cols // LANES):
                total = None
                for c in range(channels):
                    value = STEP_SPARSE * jnp.maximum(own[c, r : r + 8, t * LANES : (t + 1) * LANES], 0.0)
                    total = value * value if total is None else total + value * value
                packed[i].append(total)
    store_halves(packed, keep_more, send_more)


def border_kernel(sides, own, above, keep_more, send_more, *refs):
    around = refs[:sides]
    table, u_ref, keep, send, ext, coef = refs[sides:]
    channels, rows, cols = own.shape
    x, y = lax.axis_index("frow"), lax.axis_index("chan") % 2
    places = Places(rows, cols)
    fill_rows(ext, HALO * x, HALO, pl.multiple_of((1 - x) * (rows - HALO), HALO), own, around)
    for c in range(channels):
        at = pl.ds(HALO * (1 - x) * channels + c, HALO, stride=channels)
        for t in range(cols // LANES):
            start = (c * (cols // LANES) + t) * HALO
            ext[t, at, :] = jnp.maximum(above[start : start + HALO, :], 0.0)
        for t in range(sides):
            start = (channels * (cols // LANES) + t) * HALO
            corner = jnp.maximum(above[start : start + HALO, :], 0.0)
            ext[cols // LANES + t, at, :] = corner if c == 0 else pltpu.roll(corner, LANES - NEAR * c, 1)
    filter_columns(ext, table, cols, coef)
    squares = coefficients(coef, 0, range(2 * NDB + 1), u_ref, 4)
    strips = pack_strip(squares[8 * NDB :], 2)
    needed = []
    for tile in range(2 * NDB):
        rows_here = squares[4 * tile : 4 * tile + 4]
        count = BORDER_ROWS[tile % NDB]
        needed += [jnp.where(x == 0, a, b) for a, b in zip(rows_here[:count], rows_here[4 - count :])]
    middle = len(needed) // 2
    store_halves([pack_half(needed[:middle]), pack_half(needed[middle:])], keep, send, places.border - places.strip)
    keep[: places.border - places.strip, :] = keep_more[...]
    send[: places.border - places.strip, :] = send_more[...]
    keep[:8, :] = keep_more[:8, :] + jnp.where(y == 0, *strips)
    send[:8, :] = send_more[:8, :] + jnp.where(y == 0, *strips[::-1])


def pairing_rounds(order):
    players = list(range(order))
    rounds = []
    for _ in range(order - 1):
        rounds.append([(min(a, b), max(a, b)) for a, b in zip(players[: order // 2], players[: order // 2 - 1 : -1])])
        players = [players[0]] + [players[-1]] + players[1:-1]
    return rounds


def down(values):
    for step in (4, 2, 1):
        values = values + pltpu.roll(values, step, 0)
    return values


def nuclear_kernel(limit, own, other, out, group, mix):
    channels, rows, cols = own.shape
    order = 2 * channels
    y = lax.axis_index("chan") % 2
    for c in range(channels):
        group[y * channels + c] = jnp.maximum(own[c], 0.0)
        group[(1 - y) * channels + c] = jnp.maximum(other[c], 0.0)
    blocks = [(slice(r, r + 8), slice(t, t + LANES)) for r in range(0, rows, 8) for t in range(0, cols, LANES)]
    partial = {}
    for at in blocks:
        held = [group[(c, *at)] for c in range(order)]
        for i in range(order):
            for j in range(i + 1):
                term = held[i] * held[j]
                partial[i, j] = partial[i, j] + term if (i, j) in partial else term
    row_sum = {key: jnp.sum(value, axis=0, keepdims=True) for key, value in partial.items()}
    sub = lax.broadcasted_iota(jnp.int32, (order, LANES), 0)
    turned, vectors, diag = [], [], []
    for j in range(order):
        stacked = jnp.concatenate([row_sum[max(i, j), min(i, j)] for i in range(order)], 0)
        column = jnp.broadcast_to(jnp.sum(stacked, axis=1, keepdims=True), (order, LANES))
        turned.append(column)
        unit = jnp.where(sub == j, F32(1.0), F32(0.0))
        vectors.append(unit)
        diag.append(down(column * unit))

    rounds = pairing_rounds(order)

    def sweep(_, state):
        turned, vectors, diag = (list(part) for part in state)
        for pairs in rounds:
            for p, q in pairs:
                coupling = down(vectors[p] * turned[q])
                spread = diag[q] - diag[p]
                square = spread * spread + 4.0 * coupling * coupling
                positive = square > 0.0
                inverse = jnp.where(positive, lax.rsqrt(jnp.where(positive, square, 1.0)), 0.0)
                cosine2 = jnp.where(positive, 0.5 + 0.5 * jnp.abs(spread) * inverse, 1.0)
                other = lax.rsqrt(cosine2)
                c = cosine2 * other
                s = jnp.where(spread >= 0.0, coupling, -coupling) * inverse * other
                shift = s * other * coupling
                diag[p], diag[q] = diag[p] - shift, diag[q] + shift
                turned[p], turned[q] = c * turned[p] - s * turned[q], s * turned[p] + c * turned[q]
                vectors[p], vectors[q] = c * vectors[p] - s * vectors[q], s * vectors[p] + c * vectors[q]
        return tuple(turned), tuple(vectors), tuple(diag)

    turned, vectors, _ = lax.fori_loop(0, JACOBI_SWEEPS, sweep, (tuple(turned), tuple(vectors), tuple(diag)))
    weighted = []
    for j in range(order):
        value = down(vectors[j] * turned[j])
        weighted.append(vectors[j] * (limit / jnp.maximum(jnp.sqrt(jnp.maximum(value, 0.0)), limit)))
    for k in range(order):
        total = None
        for j in range(order):
            term = weighted[j] * jnp.broadcast_to(vectors[j][k : k + 1, :], (order, LANES))
            total = term if total is None else total + term
        mix[k] = total
    for i in range(channels):
        row = [jnp.broadcast_to(mix[k, pl.ds(y * channels + i, 1), :], (order, LANES)) for k in range(order)]
        for at in blocks:
            total = None
            for k in range(order):
                term = row[k] * group[(k, *at)]
                total = term if total is None else total + term
            out[(i, *at)] = total


def scales(limit, norms):
    return limit * lax.rsqrt(jnp.maximum(norms, limit * limit))


def widen(scale, at, item):
    sub = lax.broadcasted_iota(jnp.int32, (8, LANES), 0)
    first = jnp.broadcast_to(scale[at + item : at + item + 1, :], (8, LANES))
    second = jnp.broadcast_to(scale[at + 4 + item : at + 5 + item, :], (8, LANES))
    return jnp.where(sub < 4, first, second)


def spread_rows(inner, border, taps, spread, lanes):
    x = lax.axis_index("frow")
    empty = jnp.zeros((8, LANES), F32)
    count = len(inner)
    upper = [empty, empty, *inner, *border]
    lower = [*border, *inner, empty, empty]
    padded = [jnp.where(x == 0, a, b) for a, b in zip(upper, lower)]
    for i in range(count + 2):
        spread[8 * i : 8 * i + 8, lanes] = filter_rows(taps, padded, lambda s: i + 2 - s)


class Places:
    def __init__(self, rows, cols):
        self.inner = rows // 2 - 2
        self.strip = 2 * NDB * self.inner
        self.dirac = self.strip + 8
        self.border = self.dirac + rows * cols // LANES // 2
        self.all = self.border + 2 * sum(BORDER_ROWS)


def half_duals(places, half, scale, u_inner, u_border, spread):
    x = lax.axis_index("frow")
    for family in range(NDB):
        if isinstance(half, int):
            lanes = slice((half * NDB + family) * LANES, (half * NDB + family + 1) * LANES)
        else:
            lanes = pl.ds(pl.multiple_of((half * NDB + family) * LANES, LANES), LANES)
        count = places.inner
        factors = [widen(scale, 8 * ((family * count + j) // 4), (family * count + j) % 4) for j in range(count)]
        inner = [u_inner[8 * j : 8 * j + 8, lanes] * factors[j] for j in range(count)]
        first, count = sum(BORDER_ROWS[:family]), BORDER_ROWS[family]
        factors = [widen(scale, places.border + 8 * (k // 4), k % 4) for k in range(first, first + count)]
        spare = [jnp.zeros((8, LANES), F32)] * (4 - count)
        factors = [jnp.where(x == 0, a, b) for a, b in zip(factors + spare, spare + factors)] if spare else factors
        duals = inner, [u_border[8 * j : 8 * j + 8, lanes] * factors[j] for j in range(4)]
        spread_rows(*duals, row_taps(family, (1, 2), 1.0), spread, slice(family * LANES, (family + 1) * LANES))


def first_kernel(limit, raw, density, nuclear, u_inner, u_border, mine, table, step, spread, scale):
    channels, rows, cols = raw.shape
    y = lax.axis_index("chan") % 2
    scale[...] = scales(limit, mine[...])
    half_duals(Places(rows, cols), y, scale, u_inner, u_border, spread)
    lanes = pl.ds(pl.multiple_of(y * NDB * LANES, NDB * LANES), NDB * LANES)
    result = dot3(halves(spread[...]), [table[i, :cols, lanes] for i in range(2)], ((1,), (1,)))
    for t in range(cols // LANES):
        step[cols // LANES + t] = result[:, t * LANES : (t + 1) * LANES]
    for c in range(channels):
        for t in range(cols // LANES):
            lanes = slice(t * LANES, (t + 1) * LANES)
            estimate = jnp.maximum(raw[c, :, lanes], 0.0)
            step[t, c * rows : (c + 1) * rows, :] = density[c, :, lanes] * estimate - raw[c, :, lanes] + nuclear[c, :, lanes]


def second_kernel(limit, raw, step, u_inner, u_border, mine, theirs, table, out, spread, image, scale):
    channels, rows, cols = raw.shape
    y = lax.axis_index("chan") % 2
    places = Places(rows, cols)
    scale[y] = scales(limit, mine[...])
    scale[1 - y] = scales(limit, theirs[...])
    half_duals(places, 1 - y, scale.at[1 - y], u_inner, u_border, spread)
    main = 2 * NDB * LANES
    duals = []
    for ref, item, count in ((u_inner, 0, places.inner), (u_border, 2, 4)):
        rolled = []
        for j in range(count):
            half, k = divmod(j, count // 2)
            factor = widen(scale.at[half], places.strip, item + k // 4)
            factor = factor if k % 4 == 0 else pltpu.roll(factor, LANES - STRIP * (k % 4), 1)
            rolled.append(ref[8 * j : 8 * j + 8, main:] * factor)
        duals.append(rolled)
    spread_rows(*duals, strip_row_taps((1, 2), 1.0), spread, slice(NDB * LANES, (NDB + 1) * LANES))
    lanes = pl.ds(pl.multiple_of((1 - y) * NDB * LANES, NDB * LANES), NDB * LANES)
    left = halves(spread[...])
    right = [jnp.concatenate([table[i, :cols, lanes], table[i, :cols, main:]], 1) for i in range(2)]
    result = dot3(left, right, ((1,), (1,)))
    for t in range(cols // LANES):
        image[t] = result[:, t * LANES : (t + 1) * LANES] + step[cols // LANES + t]
    for c in range(channels):
        for r in range(0, rows, 8):
            for t in range(cols // LANES):
                lanes = slice(t * LANES, (t + 1) * LANES)
                half, inside = divmod(r, rows // 2)
                at = places.dirac + 8 * (inside // 8 * (cols // LANES) + t)
                estimate = jnp.maximum(raw[c, r : r + 8, lanes], 0.0)
                dual = STEP_SPARSE * estimate * scale[half, at : at + 8, :]
                synthesis = dual + image[t, pl.ds(r * channels + c, 8, stride=channels), :]
                total = step[t, c * rows + r : c * rows + r + 8, :] + synthesis
                out[c, r : r + 8, lanes] = jnp.maximum(estimate - STEP_PRIMAL * total, 0.0)


def fixed_taps(family, band, index):
    total = jnp.zeros(index.shape, F32)
    for k, tap in enumerate(band_taps(family)[band]):
        total = jnp.where(index == k, F32(tap), total)
    return total


def hold_kernel(dirty, own, table):
    own[...] = dirty[...]
    cols = dirty.shape[2]
    blocks = cols // NEAR
    rows = {block: block * NEAR for block in range(blocks)} | {-1: cols, blocks: cols + NEAR}
    row = lax.broadcasted_iota(jnp.int32, (NEAR, LANES), 0)
    lane = lax.broadcasted_iota(jnp.int32, (NEAR, LANES), 1)

    def put(block, tile, value):
        at, lanes = slice(rows[block], rows[block] + NEAR), slice(tile * LANES, (tile + 1) * LANES)
        top = value.astype(BF16)
        table[0, at, lanes] = top
        table[1, at, lanes] = (value - top.astype(F32)).astype(BF16)

    pairs = [(f, b) for b in range(2) for f in range(NDB)]
    for tile, (f, b) in enumerate(pairs):
        base = fixed_taps(f, b, row - 2 * (lane - 2) + len(DAUBECHIES[f]) // 2 - 1)
        for block in range(blocks):
            value = pltpu.roll(base, (block * NEAR // 2 - 2) % LANES, 1)
            if block == 0:
                value = jnp.where(lane < LANES // 2, value, 0.0)
            if block == blocks - 1:
                value = jnp.where(lane < LANES // 2, 0.0, value)
            put(block, tile, value)

    def chosen(block, position, tile_of):
        value = jnp.zeros((NEAR, LANES), F32)
        for tile, (f, b) in enumerate(pairs):
            part = fixed_taps(f, b, row + block * NEAR - 2 * position + len(DAUBECHIES[f]) // 2 - 1)
            value = jnp.where(tile_of == tile, part, value)
        return value

    column = lane % 4
    position = jnp.where(column < 2, column - 2, column + cols // 2 - 2)
    for block in rows:
        inside = block in (-1, 0, blocks - 1, blocks)
        put(block, len(pairs), chosen(block, position, lane // 4) if inside else jnp.zeros((NEAR, LANES), F32))
    column = lane % NEAR
    position = jnp.where(column < NEAR // 2, column, column + cols // 2 - NEAR)
    for block in (-1, blocks):
        put(block, 0, chosen(block, position, lane // NEAR))


def rows_kernel(own, *refs):
    *around, edge = refs
    channels, rows, cols = own.shape
    start = pl.ds(pl.multiple_of((1 - lax.axis_index("frow")) * (rows - HALO), HALO), HALO)
    at = 0
    for c in range(channels):
        for t in range(cols // LANES):
            edge[at : at + HALO, :] = own[c, start, t * LANES : (t + 1) * LANES]
            at += HALO
    lane = lax.broadcasted_iota(jnp.int32, (HALO, LANES), 1) // NEAR
    totals = near_columns(around, 0, start)
    for c in range(1, channels):
        parts = near_columns(around, c, start, NEAR * c)
        totals = [jnp.where(lane == c, part, total) for part, total in zip(parts, totals)]
    for total in totals:
        edge[at : at + HALO, :] = total
        at += HALO


def add_kernel(one, two, *refs):
    refs[-1][...] = one[...] + two[...]


def add_parts_kernel(one, two, three, four, out):
    count = one.shape[0]
    out[:count, :] = one[...] + two[...]
    out[count:, :] = three[...] + four[...]


def exchange(values, axis, bit):
    count = lax.axis_size(axis)
    return lax.ppermute(values, axis, [(i, i ^ bit) for i in range(count)])


def vmem(count):
    return [pl.BlockSpec(memory_space=pltpu.VMEM)] * count


def call(kernel, name, shapes, operands, scratch=(), limit=16, later=()):
    many = [jax.ShapeDtypeStruct(shape, F32) if isinstance(shape, tuple) else shape for shape in shapes]
    results = pl.pallas_call(
        kernel,
        name=name,
        out_shape=many,
        in_specs=vmem(len(operands)) + [pl.BlockSpec(memory_space=pl.ANY)] * len(later),
        out_specs=vmem(len(many)),
        scratch_shapes=[pltpu.VMEM(shape, F32) for shape in scratch],
        compiler_params=pltpu.CompilerParams(vmem_limit_bytes=limit * MIB),
    )(*operands, *later)
    return results if len(results) > 1 else results[0]


def from_neighbours(values):
    facets = lax.axis_size("fcol")
    if facets == 2:
        return [exchange(values, "fcol", 1)]
    return [
        lax.ppermute(values, "fcol", [(i, i + 1) for i in range(facets - 1)]),
        lax.ppermute(values, "fcol", [(i + 1, i) for i in range(facets - 1)]),
    ]


def on_device(dirty_image, density):
    channels, rows, cols = dirty_image.shape
    facets, chans = lax.axis_size("fcol"), lax.axis_size("chan")
    nuclear_limit = math.sqrt(rows * cols)
    sparse_limit = SPARSE_SCALE * math.sqrt(channels * chans)
    sides = 1 if facets == 2 else 2
    places, tiles = Places(rows, cols), 2 * NDB + 1
    lane_tiles = cols // LANES + sides

    around = from_neighbours(dirty_image)
    near = jax.ShapeDtypeStruct((2, cols + 2 * NEAR, tiles * LANES), BF16)
    own, near = call(hold_kernel, "hold", [dirty_image.shape, near], [dirty_image])
    edge = call(rows_kernel, "rows", [((channels * (cols // LANES) + sides) * HALO, LANES)], [own, *around])
    above = exchange(edge, "frow", 1)
    main, more = (places.strip, LANES), (places.border - places.strip, LANES)
    u_inner, keep, send, keep_more, send_more = call(
        inner_kernel,
        "inner",
        [(8 * places.inner, tiles * LANES), main, main, more, more],
        [own, *around, near],
        [(lane_tiles, 8 * (places.inner + 4), LANES), (8 * (places.inner + 4), tiles * LANES)],
        24,
    )
    received = exchange(send, "chan", 1)
    u_border, keep_more, send_more = call(
        lambda *refs: border_kernel(sides, *refs),
        "border",
        [(8 * 4, tiles * LANES)] + [(places.all - places.strip, LANES)] * 2,
        [own, above, keep_more, send_more, *around, near],
        [(lane_tiles, 8 * 8, LANES), (8 * 8, tiles * LANES)],
        24,
    )
    received_more = exchange(send_more, "chan", 1)
    total = call(add_parts_kernel, "add", [(places.all, LANES)], [keep, received, keep_more, received_more])
    other = exchange(own, "chan", 1)
    nuclear = call(
        lambda *refs: nuclear_kernel(nuclear_limit, *refs),
        "nuclear",
        [dirty_image.shape],
        [own, other],
        [(2 * channels, rows, cols), (2 * channels, 2 * channels, LANES)],
    )
    bit = 2
    while bit < chans:
        received = exchange(total, "chan", bit)
        total = call(add_kernel, "add", [(places.all, LANES)], [total, received])
        bit *= 2
    theirs = exchange(total, "chan", 1)
    step = call(
        lambda *refs: first_kernel(sparse_limit, *refs),
        "first",
        [(2 * cols // LANES, channels * rows, LANES)],
        [own, density, nuclear, u_inner, u_border, total, near],
        [(4 * rows, NDB * LANES), (places.all, LANES)],
        24,
    )
    return call(
        lambda *refs: second_kernel(sparse_limit, *refs),
        "second",
        [dirty_image.shape],
        [own, step, u_inner, u_border, total, theirs, near],
        [(4 * rows, (NDB + 1) * LANES), (cols // LANES, 4 * rows, LANES), (2, places.all, LANES)],
        24,
    )


def solution(mesh):
    return jax.shard_map(
        on_device,
        mesh=mesh,
        in_specs=(P("chan", "frow", "fcol"), P("chan", "frow", "fcol")),
        out_specs=P("chan", "frow", "fcol"),
        check_vma=False,
    )
```
